32 devices in a mesh: groups: 2 (over x), sky: 16 (over z, y, core).
Axes of the slice: x: 2, y: 2, z: 4, core: 2. Of those that a mesh axis runs over, the one named last changes fastest.
Arguments:
- potential: float32 [8, 128, 1024], P('groups', 'sky'), parts along dimension 0, may hold values from -6 to 6
- lens_weight: float32 [4], replicated, may hold values from 0.08 to 0.25
- ray_start: float32 [4096, 2, 256], P(('groups', 'sky')), parts along dimension 0, may hold values from 0 to 32
- patch_index: int32 [8, 2048], P('groups', 'sky'), parts along dimension 0, may hold values from 0 to 127
- destination: int32 [4096, 1], P(('groups', 'sky')), parts along dimension 0, may hold values from 0 to 15; in each aligned block of 128 rows (0 to 127, 128 to 255, ...) at most 16 rows name the same one
Outputs:
- ray_shift: float32 [8192, 2, 256], P(('groups', 'sky')), parts along dimension 0
- distortion: float32 [8192, 4, 256], P(('groups', 'sky')), parts along dimension 0
The draws below stay inside these ranges and needn't reach their ends.
There are 2 independent parts, one for each index of `groups`. The reference program is written for one: setup_inputs(seed, part) draws one part's arguments, and reference() takes and returns one part's arrays. A program takes and returns all parts, laid end to end along the dimension named above; an argument that names none is the same for every part. Nothing has to cross between parts.
Inputs may be any that keep to these rules, and one draw needn't show every extreme that they name: Among the 128 bundles of one owner at most 16 name one destination, and in every draw some owner sends exactly 16 to one destination.
All inputs are finite; a program needn't handle non-finite values.
Results may differ from the reference program's by a relative error of at most 0.0003.
Values sent between devices are 32-bit elements; how exact they have to be, the bound alone decides.
No kernel may reach another device: no remote copies, remote signals or barrier semaphores. Data moves between devices by JAX's collectives and lax.ppermute only.
A program may use at most 64 MiB of HBM per device.

```python
import math
import jax
import jax.numpy as jnp
import numpy as np
from jax import lax

G = 32
B = 256
PLANES = 4
NB = 128
CAP = 16
RECV = 256
BUNDLES = 2048
PATCHES = 128
N_SKY = 16


def place_ends(result, key, least, high):
    spot = [jax.random.randint(jax.random.fold_in(key, axis), (), 0, length) for axis, length in enumerate(result.shape)]
    widest = result.shape.index(max(result.shape))
    beside = spot[:widest] + [(spot[widest] + 1) % result.shape[widest]] + spot[widest + 1:]
    return result.at[tuple(spot)].set(least).at[tuple(beside)].set(high)


def block_levels(rng, shape, split, smallest, largest):
    def one(axis_at, shards_of):
        draws = jax.random.uniform(jax.random.fold_in(jax.random.fold_in(rng, 6), axis_at), (shards_of,), jnp.float32, smallest / len(split), largest / len(split))
        return jnp.repeat(jnp.exp(draws), shape[axis_at] // shards_of).reshape((-1,) + (1,) * (len(shape) - axis_at - 1))

    level = one(*split[0])
    for cut in split[1:]:
        level = level * one(*cut)
    return level


def routed_block(rng, own, number, rows, count, top, limit, skew):
    ranking = jax.random.permutation(rng, count)
    crowded, ordinary = load_shares(count, rows * top, limit, skew, True), load_shares(count, rows * top, limit, skew, False)
    places = jnp.arange(count)

    def named(tallies, offset_by):
        used = int((tallies > 0).sum())
        fixed = max(1, used // 4)
        moved = fixed + (places - fixed + offset_by * (used - fixed)) % max(1, count - fixed)
        return jnp.zeros((count,), jnp.int32).at[ranking[jnp.where(places < fixed, places, moved)]].set(jnp.asarray(tallies, jnp.int32))

    tallies = jnp.where(number % 4 == 0, named(crowded, number // 4), named(ordinary, number - number // 4 - 1))
    mixed = jax.random.permutation(jax.random.fold_in(own, 3), count)
    donor, receiver = mixed[0:count // 2 * 2:2], mixed[1:count // 2 * 2:2]
    room = jnp.minimum(tallies[donor] - 1, limit - tallies[receiver]) // 2
    room = jnp.where((donor == ranking[0]) | (receiver == ranking[0]) | (tallies[receiver] == 0), 0, jnp.maximum(room, 0))
    moved = jax.random.randint(jax.random.fold_in(own, 4), (count // 2,), 0, 1 << 20) % (room + 1)
    tallies = tallies.at[donor].add(-moved).at[receiver].add(moved)
    labels = jnp.searchsorted(jnp.cumsum(tallies), jnp.arange(rows * top), side="right").astype(jnp.int32)
    table = labels.reshape(top, rows).T
    table = table[jax.random.permutation(jax.random.fold_in(own, 1), rows)]
    offset_by = jax.random.randint(jax.random.fold_in(own, 2), (rows, 1), 0, top)
    return jnp.take_along_axis(table, (jnp.arange(top)[None, :] + offset_by) % top, axis=1)


def load_shares(amount, total, most, skew, full):
    weights = [(1 << 20) // math.isqrt(grade ** skew) + 1 for grade in range(1, amount + 1)]
    largest = most if full else min(most, max(-(-total // amount), total * weights[0] // sum(weights)))
    least = 1 if total - largest >= amount - 1 else 0
    given, spare = [largest] + [least] * (amount - 1), total - largest - least * (amount - 1)
    while spare > 0:
        movable = [i for i in range(1, amount) if given[i] < largest] or [i for i in range(1, amount) if given[i] < most]
        pool, remaining = sum([weights[i] for i in movable]), spare
        for i in movable:
            extra = min(most - given[i], max(1, remaining * weights[i] // pool), spare)
            given[i] = given[i] + extra
            spare = spare - extra
    return np.array(given)


def normal_values(key, dims, scale, reach, cuts=(), kind=jnp.bfloat16):
    drawn = jax.random.normal(key, dims, jnp.float32) * scale
    if len(cuts) > 0:
        drawn = block_levels(key, dims, cuts, -0.22, 0.18) * drawn
    return jnp.clip(drawn, min=-reach, max=reach).astype(kind)


def setup_inputs(seed: int = 0, part: int = 0) -> dict:
    key_list = jax.random.split(jax.random.key(seed), 6)
    part_splits = jax.random.split(jax.random.fold_in(key_list[5], part), 6)
    potential = normal_values(part_splits[0], (PLANES, PATCHES, G * G), 1.0, 6.0, ((1, 16),), jnp.float32)
    lens_weight = jnp.clip(jnp.exp(jax.random.uniform(key_list[1], (PLANES,), jnp.float32, math.log(0.08), math.log(0.25))), 0.08, 0.25)
    ray_start = jnp.clip(32.0 * jax.random.uniform(part_splits[2], (BUNDLES, 2, B), jnp.float32) ** block_levels(part_splits[2], (BUNDLES, 2, B), ((0, 16),), -0.2, 0.2), 0.0, 32.0)
    patch_index = place_ends(jax.random.randint(part_splits[3], (PLANES, BUNDLES), 0, PATCHES), jax.random.fold_in(part_splits[3], 1), 0, PATCHES - 1).astype(jnp.int32)
    destination_keys = jax.random.split(jax.random.fold_in(part_splits[4], 1), BUNDLES // NB)
    destination_turns = jax.random.permutation(jax.random.fold_in(part_splits[4], 3), BUNDLES // NB)
    destination = jax.vmap(lambda own, number: routed_block(jax.random.fold_in(part_splits[4], 2), own, number, NB, N_SKY, 1, CAP, 2))(destination_keys, destination_turns).reshape((BUNDLES, 1))
    return dict(potential=potential, lens_weight=lens_weight, ray_start=ray_start, patch_index=patch_index, destination=destination)


def hat_weights(pos, side):
    grid = jnp.arange(side).astype(pos.dtype)
    dist = jnp.mod(pos[..., None] - grid + side / 2.0, side) - side / 2.0
    return jnp.maximum(0.0, 1.0 - jnp.abs(dist))


def derive_fields(patch):
    east = jnp.roll(patch, -1, axis=2)
    west = jnp.roll(patch, 1, axis=2)
    north = jnp.roll(patch, -1, axis=1)
    south = jnp.roll(patch, 1, axis=1)
    grad_x = (east - west) * 0.5
    grad_y = (north - south) * 0.5
    curv_xx = east - 2.0 * patch + west
    curv_yy = north - 2.0 * patch + south
    cross = (jnp.roll(east, -1, axis=1) - jnp.roll(west, -1, axis=1) - jnp.roll(east, 1, axis=1) + jnp.roll(west, 1, axis=1)) * 0.25
    return jnp.concatenate([grad_x, grad_y, curv_xx, cross, curv_yy], axis=2)


def sample_fields(fields, pos_x, pos_y):
    side = fields.shape[1]
    weight_x = hat_weights(pos_x, side)
    weight_y = hat_weights(pos_y, side)
    rows = jnp.einsum("nrg,ngk->nrk", weight_y, fields, precision=lax.Precision.HIGHEST)
    rows = rows.reshape(rows.shape[0], rows.shape[1], 5, side)
    return jnp.sum(rows * weight_x[:, :, None, :], axis=-1)


def trace_rays(start, lens_weight, select):
    pos_x = start[:, 0]
    pos_y = start[:, 1]
    a_one = jnp.ones_like(pos_x)
    a_zero = jnp.zeros_like(pos_x)
    m11, m12, m21, m22 = a_one, a_zero, a_zero, a_one
    for plane in range(PLANES):
        patch = select(plane)
        fields = derive_fields(patch.reshape(patch.shape[0], G, G))
        vals = sample_fields(fields, pos_x, pos_y)
        strength = lens_weight[plane]
        hxx, hxy, hyy = vals[:, :, 2], vals[:, :, 3], vals[:, :, 4]
        n11 = m11 - strength * (hxx * m11 + hxy * m21)
        n12 = m12 - strength * (hxx * m12 + hxy * m22)
        n21 = m21 - strength * (hxy * m11 + hyy * m21)
        n22 = m22 - strength * (hxy * m12 + hyy * m22)
        m11, m12, m21, m22 = n11, n12, n21, n22
        pos_x = pos_x - strength * vals[:, :, 0]
        pos_y = pos_y - strength * vals[:, :, 1]
    shift = jnp.stack([pos_x - start[:, 0], pos_y - start[:, 1]], axis=1)
    matrix = jnp.stack([m11, m12, m21, m22], axis=1)
    return shift, matrix


def reference(potential, lens_weight, ray_start, patch_index, destination):
    starts = ray_start.reshape(N_SKY, NB, 2, B)
    indices = jnp.transpose(patch_index.reshape(PLANES, N_SKY, NB), (1, 0, 2))

    def one_owner(item):
        start, ids = item

        def select(plane):
            return jnp.take(potential[plane], ids[plane], axis=0)

        return trace_rays(start, lens_weight, select)

    shifts, matrices = lax.map(one_owner, (starts, indices))
    dest = destination.reshape(N_SKY, NB)
    same = dest[:, :, None] == dest[:, None, :]
    earlier = jnp.arange(NB)[None, :] < jnp.arange(NB)[:, None]
    rank = jnp.sum((same & earlier[None]).astype(jnp.int32), axis=2)
    owner = jnp.arange(N_SKY).astype(jnp.int32)[:, None]
    slot = (dest * RECV + owner * CAP + rank).reshape(-1).astype(jnp.int32)
    ray_shift = jnp.zeros((N_SKY * RECV, 2, B), jnp.float32).astype(shifts.dtype)
    ray_shift = ray_shift.at[slot].set(shifts.reshape(-1, 2, B))
    distortion = jnp.zeros((N_SKY * RECV, 4, B), jnp.float32).astype(matrices.dtype)
    distortion = distortion.at[slot].set(matrices.reshape(-1, 4, B))
    return ray_shift, distortion
```

```python
import functools

import jax
import jax.numpy as jnp
from jax import lax
from jax.experimental import pallas as pl
from jax.experimental.pallas import tpu as pltpu
from jax.sharding import PartitionSpec as P

LANES = 128
SUB = 8
SIDE = 32
CHUNKS = 8


def lane_gather(table, idx):
    dims = lax.GatherDimensionNumbers(
        offset_dims=(),
        collapsed_slice_dims=(1,),
        start_index_map=(1,),
        operand_batching_dims=(0,),
        start_indices_batching_dims=(0,),
    )
    return lax.gather(
        table,
        idx[..., None],
        dims,
        slice_sizes=(1, 1),
        mode=lax.GatherScatterMode.PROMISE_IN_BOUNDS,
    )


def split3(value):
    high = value.astype(jnp.bfloat16)
    rest = value - high.astype(jnp.float32)
    middle = rest.astype(jnp.bfloat16)
    low = (rest - middle.astype(jnp.float32)).astype(jnp.bfloat16)
    return high, middle, low


def regroup_kernel(src_ref, dst_ref):
    planes, tiles, _ = src_ref.shape
    lane = lax.broadcasted_iota(jnp.int32, (SUB, LANES), 1)
    source = (lane & 96) + ((lane & 15) << 1) + ((lane >> 4) & 1)
    for plane in range(planes):
        for base in range(0, tiles, SUB):
            rows = pl.ds(base, SUB)
            parts = [
                lane_gather(src_ref[plane, rows, pl.ds(c * LANES, LANES)], source)
                for c in range(CHUNKS)
            ]
            for step in (1, 2, 4):
                keep = ((lane >> 4) & step) == 0
                for c in range(CHUNKS):
                    if c & step:
                        continue
                    one, two = parts[c], parts[c + step]
                    parts[c] = jnp.where(keep, one, pltpu.roll(two, step * 16, 1))
                    parts[c + step] = jnp.where(keep, pltpu.roll(one, LANES - step * 16, 1), two)
            for c in range(CHUNKS):
                dst_ref[plane, rows, pl.ds(c * LANES, LANES)] = parts[c]


def regroup(potential):
    return pl.pallas_call(
        regroup_kernel,
        out_shape=jax.ShapeDtypeStruct(potential.shape, potential.dtype),
        in_specs=[pl.BlockSpec(memory_space=pltpu.VMEM)],
        out_specs=pl.BlockSpec(memory_space=pltpu.VMEM),
        name="regroup",
    )(potential)


def pack_kernel(n_sky, each, dest_ref, ids_ref, rays_ref, out_ref):
    bundles = dest_ref.shape[1]
    slots = n_sky * each
    dest_row = jnp.broadcast_to(dest_ref[...], (bundles, bundles))
    dest_col = jnp.transpose(dest_row)
    row = lax.broadcasted_iota(jnp.int32, (bundles, bundles), 0)
    col = lax.broadcasted_iota(jnp.int32, (bundles, bundles), 1)
    hits = jnp.where((dest_row == dest_col) & (row < col), 1.0, 0.0)
    rank = jnp.sum(hits, axis=0, keepdims=True).astype(jnp.int32)
    slot = dest_ref[...] * each + rank
    place = lax.broadcasted_iota(jnp.int32, (slots, bundles), 0) == slot
    place = jnp.where(place, 1.0, 0.0)
    place3 = jnp.concatenate([place] * 3, axis=1).astype(jnp.bfloat16)
    for part in range(4):
        rays = rays_ref[pl.ds(part, bundles, stride=4), :]
        terms = jnp.concatenate(split3(rays), axis=0)
        sent = jnp.dot(place3, terms, preferred_element_type=jnp.float32)
        for o in range(n_sky):
            out_ref[o, pl.ds(part, each, stride=4), :] = sent[o * each:(o + 1) * each]
    ids = ids_ref[...] + 1
    pad = jnp.zeros((SUB - ids.shape[0], bundles), jnp.float32)
    fine = jnp.concatenate([(ids & 15).astype(jnp.float32), pad], axis=0)
    coarse = jnp.concatenate([(ids >> 4).astype(jnp.float32), pad], axis=0)
    place = place.astype(jnp.bfloat16)
    contract = (((1,), (1,)), ((), ()))
    fine = lax.dot_general(fine.astype(jnp.bfloat16), place, contract, preferred_element_type=jnp.float32)
    coarse = lax.dot_general(coarse.astype(jnp.bfloat16), place, contract, preferred_element_type=jnp.float32)
    numbers = coarse * 16.0 + fine
    lane = lax.broadcasted_iota(jnp.int32, (SUB, LANES), 1)
    for o in range(n_sky):
        first = o * each
        block = numbers[:, first // LANES * LANES:first // LANES * LANES + LANES]
        turn = (LANES - first % LANES) % LANES
        if turn:
            block = pltpu.roll(block, turn, 1)
        out_ref[o, pl.ds(4 * each, SUB), :] = jnp.where(lane < each, block, 0.0)


def pack(n_sky, each, dest, ids, rays):
    return pl.pallas_call(
        functools.partial(pack_kernel, n_sky, each),
        out_shape=jax.ShapeDtypeStruct((n_sky, 4 * each + SUB, LANES), jnp.float32),
        in_specs=[pl.BlockSpec(memory_space=pltpu.VMEM)] * 3,
        out_specs=pl.BlockSpec(memory_space=pltpu.VMEM),
        name="pack",
    )(dest, ids, rays)


def bilinear(f00, f01, f10, f11, u, v):
    one = f00 + u * (f01 - f00)
    two = f10 + u * (f11 - f10)
    return one + v * (two - one)


def lerp(one, two, t):
    return one + t * (two - one)


def window(tables, pos_x, pos_y):
    ix = (pos_x + float(SIDE)).astype(jnp.int32)
    iy = (pos_y + float(SIDE)).astype(jnp.int32)
    u = pos_x - (ix.astype(jnp.float32) - float(SIDE))
    v = pos_y - (iy.astype(jnp.float32) - float(SIDE))
    odd = (ix - 1) >> 1
    even = ix >> 1
    columns = (((even & 15), ((even + 1) & 15)), ((odd & 15), ((odd + 1) & 15)))
    odd_first = (ix & 1) == 0
    by_two = ((iy - 1) & 2) != 0
    by_one = (iy & 1) == 0
    sorted_columns = []
    for a in range(4):
        line = ((iy + (2 - a)) & 28) << 2
        e0, e1 = [lane_gather(tables[2 * a], line + c) for c in columns[0]]
        o0, o1 = [lane_gather(tables[2 * a + 1], line + c) for c in columns[1]]
        sorted_columns.append((
            jnp.where(odd_first, o0, e0),
            jnp.where(odd_first, e0, o0),
            jnp.where(odd_first, o1, e1),
            jnp.where(odd_first, e1, o1),
        ))
    w = [[None] * 4 for _ in range(4)]
    for k in range(4):
        half = [jnp.where(by_two, sorted_columns[(r + 2) & 3][k], sorted_columns[r][k]) for r in range(4)]
        for r in range(4):
            w[r][k] = jnp.where(by_one, half[(r + 1) & 3], half[r])
    return w, u, v


def trace_step(tables, strength, pos_x, pos_y, matrix):
    w, u, v = window(tables, pos_x, pos_y)
    gx = [lerp(w[1][k + 1] - w[1][k], w[2][k + 1] - w[2][k], v) for k in range(3)]
    gy = [lerp(w[r + 1][1] - w[r][1], w[r + 1][2] - w[r][2], u) for r in range(3)]
    fx2 = lerp(gx[0] + gx[1], gx[1] + gx[2], u)
    fxx = lerp(gx[1] - gx[0], gx[2] - gx[1], u)
    fy2 = lerp(gy[0] + gy[1], gy[1] + gy[2], v)
    fyy = lerp(gy[1] - gy[0], gy[2] - gy[1], v)
    wide = [[w[r][k + 2] - w[r][k] for k in range(2)] for r in range(4)]
    fxy4 = bilinear(
        wide[2][0] - wide[0][0], wide[2][1] - wide[0][1],
        wide[3][0] - wide[1][0], wide[3][1] - wide[1][1], u, v)
    half = 0.5 * strength
    hxx, hxy, hyy = strength * fxx, (0.25 * strength) * fxy4, strength * fyy
    m11, m12, m21, m22 = matrix
    matrix = (
        m11 - (hxx * m11 + hxy * m21),
        m12 - (hxx * m12 + hxy * m22),
        m21 - (hxy * m11 + hyy * m21),
        m22 - (hxy * m12 + hyy * m22),
    )
    return pos_x - half * fx2, pos_y - half * fy2, matrix


def trace_kernel(each, lens_ref, tiles_ref, got_ref, shift_ref, matrix_ref, chosen, rays, taken):
    planes, patches, pixels = tiles_ref.shape
    n_sky = got_ref.shape[0]
    slots = n_sky * each
    groups = LANES // each
    for d in range(n_sky):
        rays[pl.ds(d * 4 * each, 4 * each), :] = got_ref[d, pl.ds(0, 4 * each), :]
    numbers = []
    for first in range(0, n_sky, groups):
        total = None
        for d in range(first, min(first + groups, n_sky)):
            block = got_ref[d, pl.ds(4 * each, SUB), :]
            turn = (d - first) * each
            if turn:
                block = pltpu.roll(block, turn, 1)
            total = block if total is None else total + block
        numbers.append(total)
    tile_row = lax.broadcasted_iota(jnp.int32, (patches, LANES), 0).astype(jnp.float32) + 1.0
    for plane in range(planes):
        terms = split3(tiles_ref[plane])
        for part, number in enumerate(numbers):
            match = jnp.where(tile_row == number[plane:plane + 1, :], 1.0, 0.0)
            match = jnp.transpose(match)
            if plane == 0:
                found = jnp.sum(match, axis=1, keepdims=True)
                taken[pl.ds(part * LANES, LANES), :] = jnp.broadcast_to(found, (LANES, LANES))
            match = match.astype(jnp.bfloat16)
            total = None
            for term in terms:
                piece = jnp.dot(match, term, preferred_element_type=jnp.float32)
                total = piece if total is None else total + piece
            chosen[plane, pl.ds(part * LANES, LANES), :] = total

    def body(group, carry):
        base = pl.multiple_of(group * SUB, SUB)
        used = taken[pl.ds(base, SUB), :]
        start, state = [], []
        for h in range(2):
            x0 = rays[pl.ds(base * 4 + 2 * h, SUB, stride=4), :]
            y0 = rays[pl.ds(base * 4 + 2 * h + 1, SUB, stride=4), :]
            start.append((x0, y0))
            state.append((x0, y0, (used, jnp.zeros_like(used), jnp.zeros_like(used), used)))
        for plane in range(planes):
            tables = [chosen[plane, pl.ds(base, SUB), pl.ds(c * LANES, LANES)] for c in range(CHUNKS)]
            strength = lens_ref[plane]
            state = [trace_step(tables, strength, *one) for one in state]
        for h in range(2):
            x, y, matrix = state[h]
            shift_ref[pl.ds(base * 4 + 2 * h, SUB, stride=4), :] = x - start[h][0]
            shift_ref[pl.ds(base * 4 + 2 * h + 1, SUB, stride=4), :] = y - start[h][1]
            for e in range(4):
                matrix_ref[pl.ds(base * 8 + 4 * h + e, SUB, stride=8), :] = matrix[e]
        return carry

    lax.fori_loop(0, slots // SUB, body, 0)


def trace(each, lens_weight, tiles, got):
    slots = got.shape[0] * each
    planes, _, pixels = tiles.shape
    return pl.pallas_call(
        functools.partial(trace_kernel, each),
        out_shape=(
            jax.ShapeDtypeStruct((slots * 4, LANES), jnp.float32),
            jax.ShapeDtypeStruct((slots * 8, LANES), jnp.float32),
        ),
        in_specs=[
            pl.BlockSpec(memory_space=pltpu.SMEM),
            pl.BlockSpec(memory_space=pltpu.VMEM),
            pl.BlockSpec(memory_space=pltpu.VMEM),
        ],
        out_specs=(
            pl.BlockSpec(memory_space=pltpu.VMEM),
            pl.BlockSpec(memory_space=pltpu.VMEM),
        ),
        scratch_shapes=[
            pltpu.VMEM((planes, slots, pixels), jnp.float32),
            pltpu.VMEM((slots * 4, LANES), jnp.float32),
            pltpu.VMEM((slots, LANES), jnp.float32),
        ],
        compiler_params=pltpu.CompilerParams(vmem_limit_bytes=48 * 1024 * 1024),
        name="trace",
    )(lens_weight, tiles, got)


def shards(potential, lens_weight, ray_start, patch_index, destination):
    n_sky = lax.axis_size("sky")
    bundles, _, rays = ray_start.shape
    each = max(2, 2 * bundles // n_sky)
    slots = n_sky * each
    halves = rays // LANES
    tiles = lax.all_gather(regroup(potential), "sky", axis=1, tiled=True)
    flat = ray_start.reshape(bundles, 2, halves, LANES).transpose(0, 2, 1, 3).reshape(bundles * 2 * halves, LANES)
    sent = pack(n_sky, each, destination.reshape(1, bundles), patch_index, flat)
    got = lax.all_to_all(sent, "sky", split_axis=0, concat_axis=0, tiled=True)
    shift, matrix = trace(each, lens_weight, tiles, got)
    shift = shift.reshape(slots, halves, 2, LANES).transpose(0, 2, 1, 3).reshape(slots, 2, rays)
    matrix = matrix.reshape(slots, halves, 4, LANES).transpose(0, 2, 1, 3).reshape(slots, 4, rays)
    return shift, matrix


def solution(mesh):
    in_specs = (
        P("groups", "sky", None),
        P(),
        P(("groups", "sky"), None, None),
        P("groups", "sky"),
        P(("groups", "sky"), None),
    )
    out_specs = (P(("groups", "sky"), None, None), P(("groups", "sky"), None, None))
    return jax.shard_map(shards, mesh=mesh, in_specs=in_specs, out_specs=out_specs, check_vma=False)
```

```python
import functools

import jax
import jax.numpy as jnp
from jax import lax
from jax.experimental import pallas as pl
from jax.experimental.pallas import tpu as pltpu
from jax.sharding import PartitionSpec as P

LANES = 128
SUB = 8
SIDE = 32
CHUNKS = 8
EMPTY = -1024.0


def lane_gather(table, idx):
    dims = lax.GatherDimensionNumbers(
        offset_dims=(),
        collapsed_slice_dims=(1,),
        start_index_map=(1,),
        operand_batching_dims=(0,),
        start_indices_batching_dims=(0,),
    )
    return lax.gather(
        table,
        idx[..., None],
        dims,
        slice_sizes=(1, 1),
        mode=lax.GatherScatterMode.PROMISE_IN_BOUNDS,
    )


def split3(value):
    high = value.astype(jnp.bfloat16)
    rest = value - high.astype(jnp.float32)
    middle = rest.astype(jnp.bfloat16)
    low = (rest - middle.astype(jnp.float32)).astype(jnp.bfloat16)
    return high, middle, low


def regroup_kernel(src_ref, dst_ref):
    planes, tiles, _ = src_ref.shape
    lane = lax.broadcasted_iota(jnp.int32, (SUB, LANES), 1)
    source = (lane & 96) + ((lane & 15) << 1) + ((lane >> 4) & 1)
    for plane in range(planes):
        for base in range(0, tiles, SUB):
            parts = [
                lane_gather(src_ref[plane, pl.ds(base, SUB), pl.ds(c * LANES, LANES)], source)
                for c in range(CHUNKS)
            ]
            for step in (1, 2, 4):
                keep = ((lane >> 4) & step) == 0
                for c in range(CHUNKS):
                    if c & step:
                        continue
                    one, two = parts[c], parts[c + step]
                    parts[c] = jnp.where(keep, one, pltpu.roll(two, step * 16, 1))
                    parts[c + step] = jnp.where(keep, pltpu.roll(one, LANES - step * 16, 1), two)
            for c in range(CHUNKS):
                rows = pl.ds((plane * tiles + base) * CHUNKS + c, SUB, stride=CHUNKS)
                dst_ref[rows, :] = parts[c]


def regroup(potential):
    planes, tiles, pixels = potential.shape
    rows = planes * tiles * pixels // LANES
    return pl.pallas_call(
        regroup_kernel,
        out_shape=jax.ShapeDtypeStruct((rows, LANES), potential.dtype),
        in_specs=[pl.BlockSpec(memory_space=pltpu.VMEM)],
        out_specs=pl.BlockSpec(memory_space=pltpu.VMEM),
        name="regroup",
    )(potential)


def pack_kernel(n_sky, each, per_owner, me_ref, dest_ref, ids_ref, rays_ref, *out_refs):
    me = me_ref[0]
    bundles = dest_ref.shape[1]
    planes = ids_ref.shape[0]
    slots = n_sky * each
    dest_row = jnp.broadcast_to(dest_ref[...], (bundles, bundles))
    dest_col = jnp.transpose(dest_row)
    row = lax.broadcasted_iota(jnp.int32, (bundles, bundles), 0)
    col = lax.broadcasted_iota(jnp.int32, (bundles, bundles), 1)
    hits = jnp.where((dest_row == dest_col) & (row < col), 1.0, 0.0)
    rank = jnp.sum(hits, axis=0, keepdims=True).astype(jnp.int32)
    turned = dest_ref[...] ^ me
    slot = turned * each + rank
    place = lax.broadcasted_iota(jnp.int32, (slots, bundles), 0) == slot
    place = jnp.where(place, 1.0, 0.0)
    found = jnp.dot(
        place.astype(jnp.bfloat16),
        jnp.ones((bundles, LANES), jnp.bfloat16),
        preferred_element_type=jnp.float32,
    )
    place3 = jnp.concatenate([place] * 3, axis=1).astype(jnp.bfloat16)
    for part in range(4):
        rays = rays_ref[pl.ds(part, bundles, stride=4), :]
        terms = jnp.concatenate(split3(rays), axis=0)
        sent = jnp.dot(place3, terms, preferred_element_type=jnp.float32)
        if part % 2 == 0:
            sent = jnp.where(found > 0.5, sent, EMPTY)
        for s in range(n_sky):
            out_refs[s][pl.ds(part, each, stride=4), :] = sent[s * each:(s + 1) * each]
    ids = ids_ref[...]
    plane = lax.broadcasted_iota(jnp.int32, ids.shape, 0)
    owner = (ids // per_owner) ^ dest_ref[...]
    spot = (owner * planes + plane) * per_owner + ids % per_owner
    pad = jnp.zeros((SUB - planes, bundles), jnp.float32)
    fine = jnp.concatenate([(spot & 15).astype(jnp.float32), pad], axis=0)
    coarse = jnp.concatenate([(spot >> 4).astype(jnp.float32), pad], axis=0)
    place = place.astype(jnp.bfloat16)
    contract = (((1,), (1,)), ((), ()))
    fine = lax.dot_general(fine.astype(jnp.bfloat16), place, contract, preferred_element_type=jnp.float32)
    coarse = lax.dot_general(coarse.astype(jnp.bfloat16), place, contract, preferred_element_type=jnp.float32)
    numbers = coarse * 16.0 + fine
    for s in range(n_sky):
        first = s * each
        block = numbers[:, first // LANES * LANES:first // LANES * LANES + LANES]
        turn = (LANES - first % LANES) % LANES
        if turn:
            block = pltpu.roll(block, turn, 1)
        out_refs[s][pl.ds(4 * each, SUB), :] = block


def pack(n_sky, each, per_owner, me, dest, ids, rays):
    block = jax.ShapeDtypeStruct((4 * each + SUB, LANES), jnp.float32)
    return pl.pallas_call(
        functools.partial(pack_kernel, n_sky, each, per_owner),
        out_shape=[block] * n_sky,
        in_specs=[pl.BlockSpec(memory_space=pltpu.SMEM)] + [pl.BlockSpec(memory_space=pltpu.VMEM)] * 3,
        out_specs=[pl.BlockSpec(memory_space=pltpu.VMEM)] * n_sky,
        name="pack",
    )(me, dest, ids, rays)


def bilinear(f00, f01, f10, f11, u, v):
    one = f00 + u * (f01 - f00)
    two = f10 + u * (f11 - f10)
    return one + v * (two - one)


def lerp(one, two, t):
    return one + t * (two - one)


def window(tables, pos_x, pos_y):
    ix = (pos_x + float(SIDE)).astype(jnp.int32)
    iy = (pos_y + float(SIDE)).astype(jnp.int32)
    u = pos_x - (ix.astype(jnp.float32) - float(SIDE))
    v = pos_y - (iy.astype(jnp.float32) - float(SIDE))
    odd = (ix - 1) >> 1
    even = ix >> 1
    columns = (((even & 15), ((even + 1) & 15)), ((odd & 15), ((odd + 1) & 15)))
    odd_first = (ix & 1) == 0
    by_two = ((iy - 1) & 2) != 0
    by_one = (iy & 1) == 0
    sorted_columns = []
    for a in range(4):
        line = ((iy + (2 - a)) & 28) << 2
        e0, e1 = [lane_gather(tables[2 * a], line + c) for c in columns[0]]
        o0, o1 = [lane_gather(tables[2 * a + 1], line + c) for c in columns[1]]
        sorted_columns.append((
            jnp.where(odd_first, o0, e0),
            jnp.where(odd_first, e0, o0),
            jnp.where(odd_first, o1, e1),
            jnp.where(odd_first, e1, o1),
        ))
    w = [[None] * 4 for _ in range(4)]
    for k in range(4):
        half = [jnp.where(by_two, sorted_columns[(r + 2) & 3][k], sorted_columns[r][k]) for r in range(4)]
        for r in range(4):
            w[r][k] = jnp.where(by_one, half[(r + 1) & 3], half[r])
    return w, u, v


def trace_step(tables, strength, pos_x, pos_y, matrix):
    w, u, v = window(tables, pos_x, pos_y)
    gx = [lerp(w[1][k + 1] - w[1][k], w[2][k + 1] - w[2][k], v) for k in range(3)]
    gy = [lerp(w[r + 1][1] - w[r][1], w[r + 1][2] - w[r][2], u) for r in range(3)]
    fx2 = lerp(gx[0] + gx[1], gx[1] + gx[2], u)
    fxx = lerp(gx[1] - gx[0], gx[2] - gx[1], u)
    fy2 = lerp(gy[0] + gy[1], gy[1] + gy[2], v)
    fyy = lerp(gy[1] - gy[0], gy[2] - gy[1], v)
    wide = [[w[r][k + 2] - w[r][k] for k in range(2)] for r in range(4)]
    fxy4 = bilinear(
        wide[2][0] - wide[0][0], wide[2][1] - wide[0][1],
        wide[3][0] - wide[1][0], wide[3][1] - wide[1][1], u, v)
    half = 0.5 * strength
    hxx, hxy, hyy = strength * fxx, (0.25 * strength) * fxy4, strength * fyy
    m11, m12, m21, m22 = matrix
    matrix = (
        m11 - (hxx * m11 + hxy * m21),
        m12 - (hxx * m12 + hxy * m22),
        m21 - (hxy * m11 + hyy * m21),
        m22 - (hxy * m12 + hyy * m22),
    )
    return pos_x - half * fx2, pos_y - half * fy2, matrix


def trace_kernel(n_sky, each, planes, together, me_ref, lens_ref, *refs):
    tile_refs, got_refs = refs[:n_sky], refs[n_sky:2 * n_sky]
    shift_ref, matrix_ref, tiles, chosen, rays, places, sems = refs[2 * n_sky:]
    me = me_ref[0]
    slots = n_sky * each
    rows = tile_refs[0].shape[0]
    copies = []
    for s in range(n_sky):
        source = me ^ s
        copies.append((
            pltpu.make_async_copy(
                got_refs[s].at[pl.ds(4 * each, SUB), :],
                places.at[pl.ds(source * SUB, SUB), :],
                sems.at[0, s]),
            pltpu.make_async_copy(tile_refs[s], tiles.at[pl.ds(s * rows, rows), :], sems.at[1, s]),
            pltpu.make_async_copy(
                got_refs[s].at[pl.ds(0, 4 * each), :],
                rays.at[pl.ds(source * 4 * each, 4 * each), :],
                sems.at[2, s]),
        ))
    for kind in range(3):
        for s in range(n_sky):
            copies[s][kind].start()
    for kind in range(3):
        for s in range(n_sky):
            copies[s][kind].wait()

    def choose(slot, carry):
        source = slot // each
        k = slot % each
        for plane in range(planes):
            spot = places[source * SUB + plane, k].astype(jnp.int32)
            tile = tiles[pl.ds(pl.multiple_of(spot * CHUNKS, CHUNKS), CHUNKS), :]
            chosen[pl.ds(plane * CHUNKS * slots + slot, CHUNKS, stride=slots), :] = tile
        return carry

    lax.fori_loop(0, slots, choose, 0, unroll=8)

    def body(step, carry):
        chains = []
        for part in range(together):
            base = pl.multiple_of((step * together + part) * SUB, SUB)
            for h in range(2):
                x0 = rays[pl.ds(base * 4 + 2 * h, SUB, stride=4), :]
                y0 = rays[pl.ds(base * 4 + 2 * h + 1, SUB, stride=4), :]
                one = jnp.ones_like(x0)
                zero = jnp.zeros_like(x0)
                chains.append((base, h, x0, y0, (x0, y0, (one, zero, zero, one))))
        for plane in range(planes):
            strength = lens_ref[plane]
            later = []
            for base, h, x0, y0, state in chains:
                tables = [chosen[pl.ds((plane * CHUNKS + c) * slots + base, SUB), :] for c in range(CHUNKS)]
                later.append((base, h, x0, y0, trace_step(tables, strength, *state)))
            chains = later
        for base, h, x0, y0, (x, y, matrix) in chains:
            used = x0 > EMPTY * 0.5
            shift_ref[pl.ds(base * 4 + 2 * h, SUB, stride=4), :] = jnp.where(used, x - x0, 0.0)
            shift_ref[pl.ds(base * 4 + 2 * h + 1, SUB, stride=4), :] = jnp.where(used, y - y0, 0.0)
            for e in range(4):
                matrix_ref[pl.ds(base * 8 + 4 * h + e, SUB, stride=8), :] = jnp.where(used, matrix[e], 0.0)
        return carry

    lax.fori_loop(0, slots // (SUB * together), body, 0)


def trace(each, planes, me, lens_weight, tiles, got):
    n_sky = len(tiles)
    slots = n_sky * each
    rows = tiles[0].shape[0]
    return pl.pallas_call(
        functools.partial(trace_kernel, n_sky, each, planes, 2),
        out_shape=(
            jax.ShapeDtypeStruct((slots * 4, LANES), jnp.float32),
            jax.ShapeDtypeStruct((slots * 8, LANES), jnp.float32),
        ),
        in_specs=[pl.BlockSpec(memory_space=pltpu.SMEM)] * 2 + [pl.BlockSpec(memory_space=pl.ANY)] * (2 * n_sky),
        out_specs=(
            pl.BlockSpec(memory_space=pltpu.VMEM),
            pl.BlockSpec(memory_space=pltpu.VMEM),
        ),
        scratch_shapes=[
            pltpu.VMEM((n_sky * rows, LANES), jnp.float32),
            pltpu.VMEM((planes * CHUNKS * slots, LANES), jnp.float32),
            pltpu.VMEM((slots * 4, LANES), jnp.float32),
            pltpu.SMEM((n_sky * SUB, LANES), jnp.float32),
            pltpu.SemaphoreType.DMA((3, n_sky)),
        ],
        compiler_params=pltpu.CompilerParams(vmem_limit_bytes=40 * 1024 * 1024),
        name="trace",
    )(me, lens_weight, *tiles, *got)


def flipped(value, n_sky, bits):
    return lax.ppermute(value, "sky", [(i, i ^ bits) for i in range(n_sky)])


def everyone(own, n_sky):
    held = {0: own}
    bit = n_sky // 2
    while bit:
        for s in list(held):
            held[s ^ bit] = flipped(held[s], n_sky, bit)
        bit //= 2
    return [held[s] for s in range(n_sky)]


def shards(potential, lens_weight, ray_start, patch_index, destination):
    n_sky = lax.axis_size("sky")
    me = lax.axis_index("sky").reshape(1)
    planes, per_owner, _ = potential.shape
    bundles, _, rays = ray_start.shape
    each = max(2, 2 * bundles // n_sky)
    slots = n_sky * each
    halves = rays // LANES
    tiles = everyone(regroup(potential), n_sky)
    flat = ray_start.reshape(bundles, 2, halves, LANES).transpose(0, 2, 1, 3).reshape(bundles * 2 * halves, LANES)
    sent = pack(n_sky, each, per_owner, me, destination.reshape(1, bundles), patch_index, flat)
    got = [sent[0]] + [flipped(sent[s], n_sky, s) for s in range(1, n_sky)]
    shift, matrix = trace(each, planes, me, lens_weight, tiles, got)
    shift = shift.reshape(slots, halves, 2, LANES).transpose(0, 2, 1, 3).reshape(slots, 2, rays)
    matrix = matrix.reshape(slots, halves, 4, LANES).transpose(0, 2, 1, 3).reshape(slots, 4, rays)
    return shift, matrix


def solution(mesh):
    in_specs = (
        P("groups", "sky", None),
        P(),
        P(("groups", "sky"), None, None),
        P("groups", "sky"),
        P(("groups", "sky"), None),
    )
    out_specs = (P(("groups", "sky"), None, None), P(("groups", "sky"), None, None))
    return jax.shard_map(shards, mesh=mesh, in_specs=in_specs, out_specs=out_specs, check_vma=False)
```

```python
import functools

import jax
import jax.numpy as jnp
from jax import lax
from jax.experimental import pallas as pl
from jax.experimental.pallas import tpu as pltpu
from jax.sharding import PartitionSpec as P

LANES = 128
SUB = 8
SIDE = 32
CHUNKS = 8
EMPTY = -1024.0


def lane_gather(table, idx):
    dims = lax.GatherDimensionNumbers(
        offset_dims=(),
        collapsed_slice_dims=(1,),
        start_index_map=(1,),
        operand_batching_dims=(0,),
        start_indices_batching_dims=(0,),
    )
    return lax.gather(
        table,
        idx[..., None],
        dims,
        slice_sizes=(1, 1),
        mode=lax.GatherScatterMode.PROMISE_IN_BOUNDS,
    )


def split3(value):
    high = value.astype(jnp.bfloat16)
    rest = value - high.astype(jnp.float32)
    middle = rest.astype(jnp.bfloat16)
    low = (rest - middle.astype(jnp.float32)).astype(jnp.bfloat16)
    return high, middle, low


def regroup_kernel(src_ref, dst_ref):
    planes, tiles, _ = src_ref.shape
    lane = lax.broadcasted_iota(jnp.int32, (SUB, LANES), 1)
    source = (lane & 96) + ((lane & 15) << 1) + ((lane >> 4) & 1)
    for plane in range(planes):
        for base in range(0, tiles, SUB):
            parts = [
                lane_gather(src_ref[plane, pl.ds(base, SUB), pl.ds(c * LANES, LANES)], source)
                for c in range(CHUNKS)
            ]
            for step in (1, 2, 4):
                keep = ((lane >> 4) & step) == 0
                for c in range(CHUNKS):
                    if c & step:
                        continue
                    one, two = parts[c], parts[c + step]
                    parts[c] = jnp.where(keep, one, pltpu.roll(two, step * 16, 1))
                    parts[c + step] = jnp.where(keep, pltpu.roll(one, LANES - step * 16, 1), two)
            for c in range(CHUNKS):
                rows = pl.ds((plane * tiles + base) * CHUNKS + c, SUB, stride=CHUNKS)
                dst_ref[rows, :] = parts[c]


def regroup(potential):
    planes, tiles, pixels = potential.shape
    rows = planes * tiles * pixels // LANES
    return pl.pallas_call(
        regroup_kernel,
        out_shape=jax.ShapeDtypeStruct((rows, LANES), potential.dtype),
        in_specs=[pl.BlockSpec(memory_space=pltpu.VMEM)],
        out_specs=pl.BlockSpec(memory_space=pltpu.VMEM),
        name="regroup",
    )(potential)


def pack_kernel(n_sky, each, per_owner, dest_ref, ids_ref, rays_ref, out_ref):
    bundles = dest_ref.shape[1]
    planes = ids_ref.shape[0]
    slots = n_sky * each
    dest_row = jnp.broadcast_to(dest_ref[...], (bundles, bundles))
    dest_col = jnp.transpose(dest_row)
    row = lax.broadcasted_iota(jnp.int32, (bundles, bundles), 0)
    col = lax.broadcasted_iota(jnp.int32, (bundles, bundles), 1)
    hits = jnp.where((dest_row == dest_col) & (row < col), 1.0, 0.0)
    rank = jnp.sum(hits, axis=0, keepdims=True).astype(jnp.int32)
    slot = dest_ref[...] * each + rank
    place = lax.broadcasted_iota(jnp.int32, (slots, bundles), 0) == slot
    place = jnp.where(place, 1.0, 0.0)
    found = jnp.dot(
        place.astype(jnp.bfloat16),
        jnp.ones((bundles, LANES), jnp.bfloat16),
        preferred_element_type=jnp.float32,
    )
    place3 = jnp.concatenate([place] * 3, axis=1).astype(jnp.bfloat16)
    for part in range(4):
        rays = rays_ref[pl.ds(part, bundles, stride=4), :]
        terms = jnp.concatenate(split3(rays), axis=0)
        sent = jnp.dot(place3, terms, preferred_element_type=jnp.float32)
        if part % 2 == 0:
            sent = jnp.where(found > 0.5, sent, EMPTY)
        for o in range(n_sky):
            out_ref[o, pl.ds(part, each, stride=4), :] = sent[o * each:(o + 1) * each]
    ids = ids_ref[...]
    plane = lax.broadcasted_iota(jnp.int32, ids.shape, 0)
    owner = (ids // per_owner) ^ dest_ref[...]
    spot = (owner * planes + plane) * per_owner + ids % per_owner
    pad = jnp.zeros((SUB - planes, bundles), jnp.float32)
    fine = jnp.concatenate([(spot & 15).astype(jnp.float32), pad], axis=0)
    coarse = jnp.concatenate([(spot >> 4).astype(jnp.float32), pad], axis=0)
    place = place.astype(jnp.bfloat16)
    contract = (((1,), (1,)), ((), ()))
    fine = lax.dot_general(fine.astype(jnp.bfloat16), place, contract, preferred_element_type=jnp.float32)
    coarse = lax.dot_general(coarse.astype(jnp.bfloat16), place, contract, preferred_element_type=jnp.float32)
    numbers = coarse * 16.0 + fine
    for o in range(n_sky):
        first = o * each
        block = numbers[:, first // LANES * LANES:first // LANES * LANES + LANES]
        turn = (LANES - first % LANES) % LANES
        if turn:
            block = pltpu.roll(block, turn, 1)
        out_ref[o, pl.ds(4 * each, SUB), :] = block


def pack(n_sky, each, per_owner, dest, ids, rays):
    return pl.pallas_call(
        functools.partial(pack_kernel, n_sky, each, per_owner),
        out_shape=jax.ShapeDtypeStruct((n_sky, 4 * each + SUB, LANES), jnp.float32),
        in_specs=[pl.BlockSpec(memory_space=pltpu.VMEM)] * 3,
        out_specs=pl.BlockSpec(memory_space=pltpu.VMEM),
        name="pack",
    )(dest, ids, rays)


def bilinear(f00, f01, f10, f11, u, v):
    one = f00 + u * (f01 - f00)
    two = f10 + u * (f11 - f10)
    return one + v * (two - one)


def lerp(one, two, t):
    return one + t * (two - one)


def window(tables, pos_x, pos_y):
    ix = (pos_x + float(SIDE)).astype(jnp.int32)
    iy = (pos_y + float(SIDE)).astype(jnp.int32)
    u = pos_x - (ix.astype(jnp.float32) - float(SIDE))
    v = pos_y - (iy.astype(jnp.float32) - float(SIDE))
    odd = (ix - 1) >> 1
    even = ix >> 1
    columns = (((even & 15), ((even + 1) & 15)), ((odd & 15), ((odd + 1) & 15)))
    odd_first = (ix & 1) == 0
    by_two = ((iy - 1) & 2) != 0
    by_one = (iy & 1) == 0
    sorted_columns = []
    for a in range(4):
        line = ((iy + (2 - a)) & 28) << 2
        e0, e1 = [lane_gather(tables[2 * a], line + c) for c in columns[0]]
        o0, o1 = [lane_gather(tables[2 * a + 1], line + c) for c in columns[1]]
        sorted_columns.append((
            jnp.where(odd_first, o0, e0),
            jnp.where(odd_first, e0, o0),
            jnp.where(odd_first, o1, e1),
            jnp.where(odd_first, e1, o1),
        ))
    w = [[None] * 4 for _ in range(4)]
    for k in range(4):
        half = [jnp.where(by_two, sorted_columns[(r + 2) & 3][k], sorted_columns[r][k]) for r in range(4)]
        for r in range(4):
            w[r][k] = jnp.where(by_one, half[(r + 1) & 3], half[r])
    return w, u, v


def trace_step(tables, strength, pos_x, pos_y, matrix):
    w, u, v = window(tables, pos_x, pos_y)
    gx = [lerp(w[1][k + 1] - w[1][k], w[2][k + 1] - w[2][k], v) for k in range(3)]
    gy = [lerp(w[r + 1][1] - w[r][1], w[r + 1][2] - w[r][2], u) for r in range(3)]
    fx2 = lerp(gx[0] + gx[1], gx[1] + gx[2], u)
    fxx = lerp(gx[1] - gx[0], gx[2] - gx[1], u)
    fy2 = lerp(gy[0] + gy[1], gy[1] + gy[2], v)
    fyy = lerp(gy[1] - gy[0], gy[2] - gy[1], v)
    wide = [[w[r][k + 2] - w[r][k] for k in range(2)] for r in range(4)]
    fxy4 = bilinear(
        wide[2][0] - wide[0][0], wide[2][1] - wide[0][1],
        wide[3][0] - wide[1][0], wide[3][1] - wide[1][1], u, v)
    half = 0.5 * strength
    hxx, hxy, hyy = strength * fxx, (0.25 * strength) * fxy4, strength * fyy
    m11, m12, m21, m22 = matrix
    matrix = (
        m11 - (hxx * m11 + hxy * m21),
        m12 - (hxx * m12 + hxy * m22),
        m21 - (hxy * m11 + hyy * m21),
        m22 - (hxy * m12 + hyy * m22),
    )
    return pos_x - half * fx2, pos_y - half * fy2, matrix


def trace_kernel(n_sky, each, planes, together, lens_ref, got_ref, *refs):
    tile_refs = refs[:n_sky]
    shift_ref, matrix_ref, tiles, chosen, rays, places, sems = refs[n_sky:]
    slots = n_sky * each
    rows = tile_refs[0].shape[0]
    copies = []
    for s in range(n_sky):
        copies.append((
            pltpu.make_async_copy(
                got_ref.at[s, pl.ds(4 * each, SUB), :],
                places.at[pl.ds(s * SUB, SUB), :],
                sems.at[0, s]),
            pltpu.make_async_copy(tile_refs[s], tiles.at[pl.ds(s * rows, rows), :], sems.at[1, s]),
            pltpu.make_async_copy(
                got_ref.at[s, pl.ds(0, 4 * each), :],
                rays.at[pl.ds(s * 4 * each, 4 * each), :],
                sems.at[2, s]),
        ))
    for kind in range(3):
        for s in range(n_sky):
            copies[s][kind].start()
    for kind in range(3):
        for s in range(n_sky):
            copies[s][kind].wait()

    def body(step, carry):
        chains = []
        first = pl.multiple_of(step * (together * SUB), together * SUB)
        for plane in range(planes):
            for part in range(together):
                for k in range(SUB):
                    slot = first + (part * SUB + k)
                    spot = places[slot // each * SUB + plane, slot % each].astype(jnp.int32)
                    tile = tiles[pl.ds(pl.multiple_of(spot * CHUNKS, CHUNKS), CHUNKS), :]
                    chosen[pl.ds((plane * together + part) * CHUNKS * SUB + k, CHUNKS, stride=SUB), :] = tile
        for part in range(together):
            base = first + part * SUB
            for h in range(2):
                x0 = rays[pl.ds(base * 4 + 2 * h, SUB, stride=4), :]
                y0 = rays[pl.ds(base * 4 + 2 * h + 1, SUB, stride=4), :]
                one = jnp.ones_like(x0)
                zero = jnp.zeros_like(x0)
                chains.append((part, h, x0, y0, (x0, y0, (one, zero, zero, one))))
        for plane in range(planes):
            strength = lens_ref[plane]
            later = []
            for part, h, x0, y0, state in chains:
                tables = [
                    chosen[pl.ds(((plane * together + part) * CHUNKS + c) * SUB, SUB), :]
                    for c in range(CHUNKS)
                ]
                later.append((part, h, x0, y0, trace_step(tables, strength, *state)))
            chains = later
        for part, h, x0, y0, (x, y, matrix) in chains:
            base = first + part * SUB
            used = x0 > EMPTY * 0.5
            shift_ref[pl.ds(base * 4 + 2 * h, SUB, stride=4), :] = jnp.where(used, x - x0, 0.0)
            shift_ref[pl.ds(base * 4 + 2 * h + 1, SUB, stride=4), :] = jnp.where(used, y - y0, 0.0)
            for e in range(4):
                matrix_ref[pl.ds(base * 8 + 4 * h + e, SUB, stride=8), :] = jnp.where(used, matrix[e], 0.0)
        return carry

    lax.fori_loop(0, slots // (SUB * together), body, 0)


def trace(each, planes, lens_weight, got, tiles):
    n_sky = len(tiles)
    slots = n_sky * each
    rows = tiles[0].shape[0]
    together = 2
    return pl.pallas_call(
        functools.partial(trace_kernel, n_sky, each, planes, together),
        out_shape=(
            jax.ShapeDtypeStruct((slots * 4, LANES), jnp.float32),
            jax.ShapeDtypeStruct((slots * 8, LANES), jnp.float32),
        ),
        in_specs=[pl.BlockSpec(memory_space=pltpu.SMEM)] + [pl.BlockSpec(memory_space=pl.ANY)] * (1 + n_sky),
        out_specs=(
            pl.BlockSpec(memory_space=pltpu.VMEM),
            pl.BlockSpec(memory_space=pltpu.VMEM),
        ),
        scratch_shapes=[
            pltpu.VMEM((n_sky * rows, LANES), jnp.float32),
            pltpu.VMEM((planes * together * CHUNKS * SUB, LANES), jnp.float32),
            pltpu.VMEM((slots * 4, LANES), jnp.float32),
            pltpu.SMEM((n_sky * SUB, LANES), jnp.float32),
            pltpu.SemaphoreType.DMA((3, n_sky)),
        ],
        compiler_params=pltpu.CompilerParams(vmem_limit_bytes=40 * 1024 * 1024),
        name="trace",
    )(lens_weight, got, *tiles)


def flipped(value, n_sky, bits):
    return lax.ppermute(value, "sky", [(i, i ^ bits) for i in range(n_sky)])


def level(held, n_sky, bit):
    for s in list(held):
        held[s ^ bit] = flipped(held[s], n_sky, bit)


def shards(potential, lens_weight, ray_start, patch_index, destination):
    n_sky = lax.axis_size("sky")
    planes, per_owner, _ = potential.shape
    bundles, _, rays = ray_start.shape
    each = max(2, 2 * bundles // n_sky)
    slots = n_sky * each
    halves = rays // LANES
    bits = [1 << k for k in reversed(range((n_sky - 1).bit_length()))]
    held = {0: regroup(potential)}
    flat = ray_start.reshape(bundles, 2, halves, LANES).transpose(0, 2, 1, 3).reshape(bundles * 2 * halves, LANES)
    sent = pack(n_sky, each, per_owner, destination.reshape(1, bundles), patch_index, flat)
    level(held, n_sky, bits[0])
    sent, held[bits[0]] = lax.optimization_barrier((sent, held[bits[0]]))
    level(held, n_sky, bits[1])
    last = bits[0] ^ bits[1]
    sent, held[last] = lax.optimization_barrier((sent, held[last]))
    got = lax.all_to_all(sent, "sky", split_axis=0, concat_axis=0, tiled=True)
    for bit in bits[2:-1]:
        level(held, n_sky, bit)
    late = sorted(s for s in held if s == last or s & (bits[1] - 1))
    got, *tied = lax.optimization_barrier((got, *[held[s] for s in late]))
    held.update(zip(late, tied))
    level(held, n_sky, bits[-1])
    shift, matrix = trace(each, planes, lens_weight, got, [held[s] for s in range(n_sky)])
    shift = shift.reshape(slots, halves, 2, LANES).transpose(0, 2, 1, 3).reshape(slots, 2, rays)
    matrix = matrix.reshape(slots, halves, 4, LANES).transpose(0, 2, 1, 3).reshape(slots, 4, rays)
    return shift, matrix


def solution(mesh):
    in_specs = (
        P("groups", "sky", None),
        P(),
        P(("groups", "sky"), None, None),
        P("groups", "sky"),
        P(("groups", "sky"), None),
    )
    out_specs = (P(("groups", "sky"), None, None), P(("groups", "sky"), None, None))
    return jax.shard_map(shards, mesh=mesh, in_specs=in_specs, out_specs=out_specs, check_vma=False)
```

```python
import functools

import jax
import jax.numpy as jnp
from jax import lax
from jax.experimental import pallas as pl
from jax.experimental.pallas import tpu as pltpu
from jax.sharding import PartitionSpec as P

LANES = 128
SUB = 8
SIDE = 32
CHUNKS = 8
EMPTY = -1024.0


def lane_gather(table, idx):
    dims = lax.GatherDimensionNumbers(
        offset_dims=(),
        collapsed_slice_dims=(1,),
        start_index_map=(1,),
        operand_batching_dims=(0,),
        start_indices_batching_dims=(0,),
    )
    return lax.gather(
        table,
        idx[..., None],
        dims,
        slice_sizes=(1, 1),
        mode=lax.GatherScatterMode.PROMISE_IN_BOUNDS,
    )


def split3(value):
    high = value.astype(jnp.bfloat16)
    rest = value - high.astype(jnp.float32)
    middle = rest.astype(jnp.bfloat16)
    low = (rest - middle.astype(jnp.float32)).astype(jnp.bfloat16)
    return high, middle, low


def regroup_kernel(src_ref, dst_ref):
    planes, tiles, _ = src_ref.shape
    lane = lax.broadcasted_iota(jnp.int32, (SUB, LANES), 1)
    source = (lane & 96) + ((lane & 15) << 1) + ((lane >> 4) & 1)
    for plane in range(planes):
        for base in range(0, tiles, SUB):
            parts = [
                lane_gather(src_ref[plane, pl.ds(base, SUB), pl.ds(c * LANES, LANES)], source)
                for c in range(CHUNKS)
            ]
            for step in (1, 2, 4):
                keep = ((lane >> 4) & step) == 0
                for c in range(CHUNKS):
                    if c & step:
                        continue
                    one, two = parts[c], parts[c + step]
                    parts[c] = jnp.where(keep, one, pltpu.roll(two, step * 16, 1))
                    parts[c + step] = jnp.where(keep, pltpu.roll(one, LANES - step * 16, 1), two)
            for c in range(CHUNKS):
                rows = pl.ds((plane * tiles + base) * CHUNKS + c, SUB, stride=CHUNKS)
                dst_ref[rows, :] = parts[c]


def regroup(potential):
    planes, tiles, pixels = potential.shape
    rows = planes * tiles * pixels // LANES
    return pl.pallas_call(
        regroup_kernel,
        out_shape=jax.ShapeDtypeStruct((rows, LANES), potential.dtype),
        in_specs=[pl.BlockSpec(memory_space=pltpu.VMEM)],
        out_specs=pl.BlockSpec(memory_space=pltpu.VMEM),
        name="regroup",
    )(potential)


def pack_kernel(n_sky, each, per_owner, dest_ref, ids_ref, rays_ref, out_ref):
    bundles = dest_ref.shape[1]
    planes = ids_ref.shape[0]
    slots = n_sky * each
    dest_row = jnp.broadcast_to(dest_ref[...], (bundles, bundles))
    dest_col = jnp.transpose(dest_row)
    row = lax.broadcasted_iota(jnp.int32, (bundles, bundles), 0)
    col = lax.broadcasted_iota(jnp.int32, (bundles, bundles), 1)
    hits = jnp.where((dest_row == dest_col) & (row < col), 1.0, 0.0)
    rank = jnp.sum(hits, axis=0, keepdims=True).astype(jnp.int32)
    slot = dest_ref[...] * each + rank
    place = lax.broadcasted_iota(jnp.int32, (slots, bundles), 0) == slot
    place = jnp.where(place, 1.0, 0.0)
    found = jnp.dot(
        place.astype(jnp.bfloat16),
        jnp.ones((bundles, LANES), jnp.bfloat16),
        preferred_element_type=jnp.float32,
    )
    place3 = jnp.concatenate([place] * 3, axis=1).astype(jnp.bfloat16)
    for part in range(4):
        rays = rays_ref[pl.ds(part, bundles, stride=4), :]
        terms = jnp.concatenate(split3(rays), axis=0)
        sent = jnp.dot(place3, terms, preferred_element_type=jnp.float32)
        if part % 2 == 0:
            sent = jnp.where(found > 0.5, sent, EMPTY)
        for o in range(n_sky):
            out_ref[o, pl.ds(part, each, stride=4), :] = sent[o * each:(o + 1) * each]
    ids = ids_ref[...]
    plane = lax.broadcasted_iota(jnp.int32, ids.shape, 0)
    owner = (ids // per_owner) ^ dest_ref[...]
    spot = (owner * planes + plane) * per_owner + ids % per_owner
    pad = jnp.zeros((SUB - planes, bundles), jnp.float32)
    fine = jnp.concatenate([(spot & 15).astype(jnp.float32), pad], axis=0)
    coarse = jnp.concatenate([(spot >> 4).astype(jnp.float32), pad], axis=0)
    place = place.astype(jnp.bfloat16)
    contract = (((1,), (1,)), ((), ()))
    fine = lax.dot_general(fine.astype(jnp.bfloat16), place, contract, preferred_element_type=jnp.float32)
    coarse = lax.dot_general(coarse.astype(jnp.bfloat16), place, contract, preferred_element_type=jnp.float32)
    numbers = coarse * 16.0 + fine
    for o in range(n_sky):
        first = o * each
        block = numbers[:, first // LANES * LANES:first // LANES * LANES + LANES]
        turn = (LANES - first % LANES) % LANES
        if turn:
            block = pltpu.roll(block, turn, 1)
        out_ref[o, pl.ds(4 * each, SUB), :] = block


def pack(n_sky, each, per_owner, dest, ids, rays):
    return pl.pallas_call(
        functools.partial(pack_kernel, n_sky, each, per_owner),
        out_shape=jax.ShapeDtypeStruct((n_sky, 4 * each + SUB, LANES), jnp.float32),
        in_specs=[pl.BlockSpec(memory_space=pltpu.VMEM)] * 3,
        out_specs=pl.BlockSpec(memory_space=pltpu.VMEM),
        name="pack",
    )(dest, ids, rays)


def bilinear(f00, f01, f10, f11, u, v):
    one = f00 + u * (f01 - f00)
    two = f10 + u * (f11 - f10)
    return one + v * (two - one)


def lerp(one, two, t):
    return one + t * (two - one)


def window(tables, pos_x, pos_y):
    ix = (pos_x + float(SIDE)).astype(jnp.int32)
    iy = (pos_y + float(SIDE)).astype(jnp.int32)
    u = pos_x - (ix.astype(jnp.float32) - float(SIDE))
    v = pos_y - (iy.astype(jnp.float32) - float(SIDE))
    odd = (ix - 1) >> 1
    even = ix >> 1
    columns = (((even & 15), ((even + 1) & 15)), ((odd & 15), ((odd + 1) & 15)))
    odd_first = (ix & 1) == 0
    by_two = ((iy - 1) & 2) != 0
    by_one = (iy & 1) == 0
    sorted_columns = []
    for a in range(4):
        line = ((iy + (2 - a)) & 28) << 2
        e0, e1 = [lane_gather(tables[2 * a], line + c) for c in columns[0]]
        o0, o1 = [lane_gather(tables[2 * a + 1], line + c) for c in columns[1]]
        sorted_columns.append((
            jnp.where(odd_first, o0, e0),
            jnp.where(odd_first, e0, o0),
            jnp.where(odd_first, o1, e1),
            jnp.where(odd_first, e1, o1),
        ))
    w = [[None] * 4 for _ in range(4)]
    for k in range(4):
        half = [jnp.where(by_two, sorted_columns[(r + 2) & 3][k], sorted_columns[r][k]) for r in range(4)]
        for r in range(4):
            w[r][k] = jnp.where(by_one, half[(r + 1) & 3], half[r])
    return w, u, v


def trace_step(tables, strength, pos_x, pos_y, matrix):
    w, u, v = window(tables, pos_x, pos_y)
    gx = [lerp(w[1][k + 1] - w[1][k], w[2][k + 1] - w[2][k], v) for k in range(3)]
    gy = [lerp(w[r + 1][1] - w[r][1], w[r + 1][2] - w[r][2], u) for r in range(3)]
    fx2 = lerp(gx[0] + gx[1], gx[1] + gx[2], u)
    fxx = lerp(gx[1] - gx[0], gx[2] - gx[1], u)
    fy2 = lerp(gy[0] + gy[1], gy[1] + gy[2], v)
    fyy = lerp(gy[1] - gy[0], gy[2] - gy[1], v)
    wide = [[w[r][k + 2] - w[r][k] for k in range(2)] for r in range(4)]
    fxy4 = bilinear(
        wide[2][0] - wide[0][0], wide[2][1] - wide[0][1],
        wide[3][0] - wide[1][0], wide[3][1] - wide[1][1], u, v)
    half = 0.5 * strength
    hxx, hxy, hyy = strength * fxx, (0.25 * strength) * fxy4, strength * fyy
    m11, m12, m21, m22 = matrix
    matrix = (
        m11 - (hxx * m11 + hxy * m21),
        m12 - (hxx * m12 + hxy * m22),
        m21 - (hxy * m11 + hyy * m21),
        m22 - (hxy * m12 + hyy * m22),
    )
    return pos_x - half * fx2, pos_y - half * fy2, matrix


def trace_kernel(n_sky, each, planes, together, lens_ref, got_ref, *refs):
    tile_refs = refs[:n_sky]
    shift_ref, matrix_ref, tiles, chosen, rays, places, sems = refs[n_sky:]
    slots = n_sky * each
    rows = tile_refs[0].shape[0]
    copies = []
    for s in range(n_sky):
        copies.append((
            pltpu.make_async_copy(
                got_ref.at[s, pl.ds(4 * each, SUB), :],
                places.at[pl.ds(s * SUB, SUB), :],
                sems.at[0, s]),
            pltpu.make_async_copy(tile_refs[s], tiles.at[pl.ds(s * rows, rows), :], sems.at[1, s]),
            pltpu.make_async_copy(
                got_ref.at[s, pl.ds(0, 4 * each), :],
                rays.at[pl.ds(s * 4 * each, 4 * each), :],
                sems.at[2, s]),
        ))
    for kind in range(3):
        for s in range(n_sky):
            copies[s][kind].start()
    for kind in range(3):
        for s in range(n_sky):
            copies[s][kind].wait()

    def body(step, carry):
        chains = []
        first = pl.multiple_of(step * (together * SUB), together * SUB)
        for plane in range(planes):
            for part in range(together):
                for k in range(SUB):
                    slot = first + (part * SUB + k)
                    spot = places[slot // each * SUB + plane, slot % each].astype(jnp.int32)
                    tile = tiles[pl.ds(pl.multiple_of(spot * CHUNKS, CHUNKS), CHUNKS), :]
                    chosen[pl.ds((plane * together + part) * CHUNKS * SUB + k, CHUNKS, stride=SUB), :] = tile
        for part in range(together):
            base = first + part * SUB
            for h in range(2):
                x0 = rays[pl.ds(base * 4 + 2 * h, SUB, stride=4), :]
                y0 = rays[pl.ds(base * 4 + 2 * h + 1, SUB, stride=4), :]
                one = jnp.ones_like(x0)
                zero = jnp.zeros_like(x0)
                chains.append((part, h, x0, y0, (x0, y0, (one, zero, zero, one))))
        for plane in range(planes):
            strength = lens_ref[plane]
            later = []
            for part, h, x0, y0, state in chains:
                tables = [
                    chosen[pl.ds(((plane * together + part) * CHUNKS + c) * SUB, SUB), :]
                    for c in range(CHUNKS)
                ]
                later.append((part, h, x0, y0, trace_step(tables, strength, *state)))
            chains = later
        for part, h, x0, y0, (x, y, matrix) in chains:
            base = first + part * SUB
            used = x0 > EMPTY * 0.5
            shift_ref[pl.ds(base * 4 + 2 * h, SUB, stride=4), :] = jnp.where(used, x - x0, 0.0)
            shift_ref[pl.ds(base * 4 + 2 * h + 1, SUB, stride=4), :] = jnp.where(used, y - y0, 0.0)
            for e in range(4):
                matrix_ref[pl.ds(base * 8 + 4 * h + e, SUB, stride=8), :] = jnp.where(used, matrix[e], 0.0)
        return carry

    lax.fori_loop(0, slots // (SUB * together), body, 0)


def trace(each, planes, lens_weight, got, tiles):
    n_sky = len(tiles)
    slots = n_sky * each
    rows = tiles[0].shape[0]
    together = 1
    return pl.pallas_call(
        functools.partial(trace_kernel, n_sky, each, planes, together),
        out_shape=(
            jax.ShapeDtypeStruct((slots * 4, LANES), jnp.float32),
            jax.ShapeDtypeStruct((slots * 8, LANES), jnp.float32),
        ),
        in_specs=[pl.BlockSpec(memory_space=pltpu.SMEM)] + [pl.BlockSpec(memory_space=pl.ANY)] * (1 + n_sky),
        out_specs=(
            pl.BlockSpec(memory_space=pltpu.VMEM),
            pl.BlockSpec(memory_space=pltpu.VMEM),
        ),
        scratch_shapes=[
            pltpu.VMEM((n_sky * rows, LANES), jnp.float32),
            pltpu.VMEM((planes * together * CHUNKS * SUB, LANES), jnp.float32),
            pltpu.VMEM((slots * 4, LANES), jnp.float32),
            pltpu.SMEM((n_sky * SUB, LANES), jnp.float32),
            pltpu.SemaphoreType.DMA((3, n_sky)),
        ],
        compiler_params=pltpu.CompilerParams(vmem_limit_bytes=40 * 1024 * 1024),
        name="trace",
    )(lens_weight, got, *tiles)


def flipped(value, n_sky, bits):
    return lax.ppermute(value, "sky", [(i, i ^ bits) for i in range(n_sky)])


def spread(held, n_sky, bits):
    for bit in bits:
        for s in [s for s in held if s & (2 * bit - 1) == 0]:
            if s ^ bit not in held:
                held[s ^ bit] = flipped(held[s], n_sky, bit)


def shards(potential, lens_weight, ray_start, patch_index, destination):
    n_sky = lax.axis_size("sky")
    planes, per_owner, _ = potential.shape
    bundles, _, rays = ray_start.shape
    each = max(2, 2 * bundles // n_sky)
    slots = n_sky * each
    halves = rays // LANES
    bits = [1 << k for k in reversed(range((n_sky - 1).bit_length()))]
    held = {0: regroup(potential)}
    flat = ray_start.reshape(bundles, 2, halves, LANES).transpose(0, 2, 1, 3).reshape(bundles * 2 * halves, LANES)
    sent = pack(n_sky, each, per_owner, destination.reshape(1, bundles), patch_index, flat)
    near = [bit for bit in bits[:3] if bit > 1]
    for bit in near:
        held[bit] = flipped(held[0], n_sky, bit)
    sent, *first = lax.optimization_barrier((sent, *[held[bit] for bit in near]))
    held.update(zip(near, first))
    got = lax.all_to_all(sent, "sky", split_axis=0, concat_axis=0, tiled=True)
    spread(held, n_sky, bits)
    shift, matrix = trace(each, planes, lens_weight, got, [held[s] for s in range(n_sky)])
    shift = shift.reshape(slots, halves, 2, LANES).transpose(0, 2, 1, 3).reshape(slots, 2, rays)
    matrix = matrix.reshape(slots, halves, 4, LANES).transpose(0, 2, 1, 3).reshape(slots, 4, rays)
    return shift, matrix


def solution(mesh):
    in_specs = (
        P("groups", "sky", None),
        P(),
        P(("groups", "sky"), None, None),
        P("groups", "sky"),
        P(("groups", "sky"), None),
    )
    out_specs = (P(("groups", "sky"), None, None), P(("groups", "sky"), None, None))
    return jax.shard_map(shards, mesh=mesh, in_specs=in_specs, out_specs=out_specs, check_vma=False)
```

```python
import functools

import jax
import jax.numpy as jnp
from jax import lax
from jax.experimental import pallas as pl
from jax.experimental.pallas import tpu as pltpu
from jax.sharding import PartitionSpec as P

LANES = 128
SUB = 8
SIDE = 32
CHUNKS = 8
EMPTY = -1024.0


def lane_gather(table, idx):
    dims = lax.GatherDimensionNumbers(
        offset_dims=(),
        collapsed_slice_dims=(1,),
        start_index_map=(1,),
        operand_batching_dims=(0,),
        start_indices_batching_dims=(0,),
    )
    return lax.gather(
        table,
        idx[..., None],
        dims,
        slice_sizes=(1, 1),
        mode=lax.GatherScatterMode.PROMISE_IN_BOUNDS,
    )


def split3(value):
    high = value.astype(jnp.bfloat16)
    rest = value - high.astype(jnp.float32)
    middle = rest.astype(jnp.bfloat16)
    low = (rest - middle.astype(jnp.float32)).astype(jnp.bfloat16)
    return high, middle, low


def regroup_kernel(src_ref, dst_ref):
    planes, tiles, _ = src_ref.shape
    lane = lax.broadcasted_iota(jnp.int32, (SUB, LANES), 1)
    source = (lane & 96) + ((lane & 15) << 1) + ((lane >> 4) & 1)
    for plane in range(planes):
        for base in range(0, tiles, SUB):
            parts = [
                lane_gather(src_ref[plane, pl.ds(base, SUB), pl.ds(c * LANES, LANES)], source)
                for c in range(CHUNKS)
            ]
            for step in (1, 2, 4):
                keep = ((lane >> 4) & step) == 0
                for c in range(CHUNKS):
                    if c & step:
                        continue
                    one, two = parts[c], parts[c + step]
                    parts[c] = jnp.where(keep, one, pltpu.roll(two, step * 16, 1))
                    parts[c + step] = jnp.where(keep, pltpu.roll(one, LANES - step * 16, 1), two)
            for c in range(CHUNKS):
                rows = pl.ds((plane * tiles + base) * CHUNKS + c, SUB, stride=CHUNKS)
                dst_ref[rows, :] = parts[c]


def regroup(potential):
    planes, tiles, pixels = potential.shape
    rows = planes * tiles * pixels // LANES
    return pl.pallas_call(
        regroup_kernel,
        out_shape=jax.ShapeDtypeStruct((rows, LANES), potential.dtype),
        in_specs=[pl.BlockSpec(memory_space=pltpu.VMEM)],
        out_specs=pl.BlockSpec(memory_space=pltpu.VMEM),
        name="regroup",
    )(potential)


def pack_kernel(n_sky, each, per_owner, dest_ref, ids_ref, rays_ref, out_ref):
    bundles = dest_ref.shape[1]
    planes = ids_ref.shape[0]
    slots = n_sky * each
    dest_row = jnp.broadcast_to(dest_ref[...], (bundles, bundles))
    dest_col = jnp.transpose(dest_row)
    row = lax.broadcasted_iota(jnp.int32, (bundles, bundles), 0)
    col = lax.broadcasted_iota(jnp.int32, (bundles, bundles), 1)
    hits = jnp.where((dest_row == dest_col) & (row < col), 1.0, 0.0)
    rank = jnp.sum(hits, axis=0, keepdims=True).astype(jnp.int32)
    slot = dest_ref[...] * each + rank
    place = lax.broadcasted_iota(jnp.int32, (slots, bundles), 0) == slot
    place = jnp.where(place, 1.0, 0.0)
    found = jnp.dot(
        place.astype(jnp.bfloat16),
        jnp.ones((bundles, LANES), jnp.bfloat16),
        preferred_element_type=jnp.float32,
    )
    place3 = jnp.concatenate([place] * 3, axis=1).astype(jnp.bfloat16)
    for part in range(4):
        rays = rays_ref[pl.ds(part, bundles, stride=4), :]
        terms = jnp.concatenate(split3(rays), axis=0)
        sent = jnp.dot(place3, terms, preferred_element_type=jnp.float32)
        if part % 2 == 0:
            sent = jnp.where(found > 0.5, sent, EMPTY)
        for o in range(n_sky):
            out_ref[o, pl.ds(part, each, stride=4), :] = sent[o * each:(o + 1) * each]
    ids = ids_ref[...]
    plane = lax.broadcasted_iota(jnp.int32, ids.shape, 0)
    owner = (ids // per_owner) ^ dest_ref[...]
    spot = (owner * planes + plane) * per_owner + ids % per_owner
    pad = jnp.zeros((SUB - planes, bundles), jnp.float32)
    fine = jnp.concatenate([(spot & 15).astype(jnp.float32), pad], axis=0)
    coarse = jnp.concatenate([(spot >> 4).astype(jnp.float32), pad], axis=0)
    place = place.astype(jnp.bfloat16)
    contract = (((1,), (1,)), ((), ()))
    fine = lax.dot_general(fine.astype(jnp.bfloat16), place, contract, preferred_element_type=jnp.float32)
    coarse = lax.dot_general(coarse.astype(jnp.bfloat16), place, contract, preferred_element_type=jnp.float32)
    numbers = coarse * 16.0 + fine
    for o in range(n_sky):
        first = o * each
        block = numbers[:, first // LANES * LANES:first // LANES * LANES + LANES]
        turn = (LANES - first % LANES) % LANES
        if turn:
            block = pltpu.roll(block, turn, 1)
        out_ref[o, pl.ds(4 * each, SUB), :] = block


def pack(n_sky, each, per_owner, dest, ids, rays):
    return pl.pallas_call(
        functools.partial(pack_kernel, n_sky, each, per_owner),
        out_shape=jax.ShapeDtypeStruct((n_sky, 4 * each + SUB, LANES), jnp.float32),
        in_specs=[pl.BlockSpec(memory_space=pltpu.VMEM)] * 3,
        out_specs=pl.BlockSpec(memory_space=pltpu.VMEM),
        name="pack",
    )(dest, ids, rays)


def bilinear(f00, f01, f10, f11, u, v):
    one = f00 + u * (f01 - f00)
    two = f10 + u * (f11 - f10)
    return one + v * (two - one)


def lerp(one, two, t):
    return one + t * (two - one)


def window(tables, pos_x, pos_y):
    ix = (pos_x + float(SIDE)).astype(jnp.int32)
    iy = (pos_y + float(SIDE)).astype(jnp.int32)
    u = pos_x - (ix.astype(jnp.float32) - float(SIDE))
    v = pos_y - (iy.astype(jnp.float32) - float(SIDE))
    odd = (ix - 1) >> 1
    even = ix >> 1
    columns = (((even & 15), ((even + 1) & 15)), ((odd & 15), ((odd + 1) & 15)))
    odd_first = (ix & 1) == 0
    by_two = ((iy - 1) & 2) != 0
    by_one = (iy & 1) == 0
    sorted_columns = []
    for a in range(4):
        line = ((iy + (2 - a)) & 28) << 2
        e0, e1 = [lane_gather(tables[2 * a], line + c) for c in columns[0]]
        o0, o1 = [lane_gather(tables[2 * a + 1], line + c) for c in columns[1]]
        sorted_columns.append((
            jnp.where(odd_first, o0, e0),
            jnp.where(odd_first, e0, o0),
            jnp.where(odd_first, o1, e1),
            jnp.where(odd_first, e1, o1),
        ))
    w = [[None] * 4 for _ in range(4)]
    for k in range(4):
        half = [jnp.where(by_two, sorted_columns[(r + 2) & 3][k], sorted_columns[r][k]) for r in range(4)]
        for r in range(4):
            w[r][k] = jnp.where(by_one, half[(r + 1) & 3], half[r])
    return w, u, v


def trace_step(tables, strength, pos_x, pos_y, matrix):
    w, u, v = window(tables, pos_x, pos_y)
    gx = [lerp(w[1][k + 1] - w[1][k], w[2][k + 1] - w[2][k], v) for k in range(3)]
    gy = [lerp(w[r + 1][1] - w[r][1], w[r + 1][2] - w[r][2], u) for r in range(3)]
    fx2 = lerp(gx[0] + gx[1], gx[1] + gx[2], u)
    fxx = lerp(gx[1] - gx[0], gx[2] - gx[1], u)
    fy2 = lerp(gy[0] + gy[1], gy[1] + gy[2], v)
    fyy = lerp(gy[1] - gy[0], gy[2] - gy[1], v)
    wide = [[w[r][k + 2] - w[r][k] for k in range(2)] for r in range(4)]
    fxy4 = bilinear(
        wide[2][0] - wide[0][0], wide[2][1] - wide[0][1],
        wide[3][0] - wide[1][0], wide[3][1] - wide[1][1], u, v)
    half = 0.5 * strength
    hxx, hxy, hyy = strength * fxx, (0.25 * strength) * fxy4, strength * fyy
    m11, m12, m21, m22 = matrix
    matrix = (
        m11 - (hxx * m11 + hxy * m21),
        m12 - (hxx * m12 + hxy * m22),
        m21 - (hxy * m11 + hyy * m21),
        m22 - (hxy * m12 + hyy * m22),
    )
    return pos_x - half * fx2, pos_y - half * fy2, matrix


def trace_kernel(n_sky, each, planes, together, lens_ref, got_ref, *refs):
    tile_refs = refs[:n_sky]
    shift_ref, matrix_ref, tiles, chosen, rays, places, sems = refs[n_sky:]
    slots = n_sky * each
    rows = tile_refs[0].shape[0]
    copies = []
    for s in range(n_sky):
        copies.append((
            pltpu.make_async_copy(
                got_ref.at[s, pl.ds(4 * each, SUB), :],
                places.at[pl.ds(s * SUB, SUB), :],
                sems.at[0, s]),
            pltpu.make_async_copy(tile_refs[s], tiles.at[pl.ds(s * rows, rows), :], sems.at[1, s]),
            pltpu.make_async_copy(
                got_ref.at[s, pl.ds(0, 4 * each), :],
                rays.at[pl.ds(s * 4 * each, 4 * each), :],
                sems.at[2, s]),
        ))
    for kind in range(3):
        for s in range(n_sky):
            copies[s][kind].start()
    for kind in range(3):
        for s in range(n_sky):
            copies[s][kind].wait()

    def body(step, carry):
        chains = []
        first = pl.multiple_of(step * (together * SUB), together * SUB)
        for plane in range(planes):
            for part in range(together):
                for k in range(SUB):
                    slot = first + (part * SUB + k)
                    spot = places[slot // each * SUB + plane, slot % each].astype(jnp.int32)
                    tile = tiles[pl.ds(pl.multiple_of(spot * CHUNKS, CHUNKS), CHUNKS), :]
                    chosen[pl.ds((plane * together + part) * CHUNKS * SUB + k, CHUNKS, stride=SUB), :] = tile
        for part in range(together):
            base = first + part * SUB
            for h in range(2):
                x0 = rays[pl.ds(base * 4 + 2 * h, SUB, stride=4), :]
                y0 = rays[pl.ds(base * 4 + 2 * h + 1, SUB, stride=4), :]
                one = jnp.ones_like(x0)
                zero = jnp.zeros_like(x0)
                chains.append((part, h, x0, y0, (x0, y0, (one, zero, zero, one))))
        for plane in range(planes):
            strength = lens_ref[plane]
            later = []
            for part, h, x0, y0, state in chains:
                tables = [
                    chosen[pl.ds(((plane * together + part) * CHUNKS + c) * SUB, SUB), :]
                    for c in range(CHUNKS)
                ]
                later.append((part, h, x0, y0, trace_step(tables, strength, *state)))
            chains = later
        for part, h, x0, y0, (x, y, matrix) in chains:
            base = first + part * SUB
            used = x0 > EMPTY * 0.5
            shift_ref[pl.ds(base * 4 + 2 * h, SUB, stride=4), :] = jnp.where(used, x - x0, 0.0)
            shift_ref[pl.ds(base * 4 + 2 * h + 1, SUB, stride=4), :] = jnp.where(used, y - y0, 0.0)
            for e in range(4):
                matrix_ref[pl.ds(base * 8 + 4 * h + e, SUB, stride=8), :] = jnp.where(used, matrix[e], 0.0)
        return carry

    lax.fori_loop(0, slots // (SUB * together), body, 0)


def trace(each, planes, lens_weight, got, tiles):
    n_sky = len(tiles)
    slots = n_sky * each
    rows = tiles[0].shape[0]
    together = 4
    return pl.pallas_call(
        functools.partial(trace_kernel, n_sky, each, planes, together),
        out_shape=(
            jax.ShapeDtypeStruct((slots * 4, LANES), jnp.float32),
            jax.ShapeDtypeStruct((slots * 8, LANES), jnp.float32),
        ),
        in_specs=[pl.BlockSpec(memory_space=pltpu.SMEM)] + [pl.BlockSpec(memory_space=pl.ANY)] * (1 + n_sky),
        out_specs=(
            pl.BlockSpec(memory_space=pltpu.VMEM),
            pl.BlockSpec(memory_space=pltpu.VMEM),
        ),
        scratch_shapes=[
            pltpu.VMEM((n_sky * rows, LANES), jnp.float32),
            pltpu.VMEM((planes * together * CHUNKS * SUB, LANES), jnp.float32),
            pltpu.VMEM((slots * 4, LANES), jnp.float32),
            pltpu.SMEM((n_sky * SUB, LANES), jnp.float32),
            pltpu.SemaphoreType.DMA((3, n_sky)),
        ],
        compiler_params=pltpu.CompilerParams(vmem_limit_bytes=40 * 1024 * 1024),
        name="trace",
    )(lens_weight, got, *tiles)


def flipped(value, n_sky, bits):
    return lax.ppermute(value, "sky", [(i, i ^ bits) for i in range(n_sky)])


def spread(held, n_sky, bits):
    for bit in bits:
        for s in [s for s in held if s & (2 * bit - 1) == 0]:
            if s ^ bit not in held:
                held[s ^ bit] = flipped(held[s], n_sky, bit)


def shards(potential, lens_weight, ray_start, patch_index, destination):
    n_sky = lax.axis_size("sky")
    planes, per_owner, _ = potential.shape
    bundles, _, rays = ray_start.shape
    each = max(2, 2 * bundles // n_sky)
    slots = n_sky * each
    halves = rays // LANES
    bits = [1 << k for k in reversed(range((n_sky - 1).bit_length()))]
    held = {0: regroup(potential)}
    flat = ray_start.reshape(bundles, 2, halves, LANES).transpose(0, 2, 1, 3).reshape(bundles * 2 * halves, LANES)
    sent = pack(n_sky, each, per_owner, destination.reshape(1, bundles), patch_index, flat)
    near = [bit for bit in bits[1:3] if bit > 1]
    for bit in near:
        held[bit] = flipped(held[0], n_sky, bit)
    sent, *first = lax.optimization_barrier((sent, *[held[bit] for bit in near]))
    held.update(zip(near, first))
    got = lax.all_to_all(sent, "sky", split_axis=0, concat_axis=0, tiled=True)
    spread(held, n_sky, bits)
    shift, matrix = trace(each, planes, lens_weight, got, [held[s] for s in range(n_sky)])
    shift = shift.reshape(slots, halves, 2, LANES).transpose(0, 2, 1, 3).reshape(slots, 2, rays)
    matrix = matrix.reshape(slots, halves, 4, LANES).transpose(0, 2, 1, 3).reshape(slots, 4, rays)
    return shift, matrix


def solution(mesh):
    in_specs = (
        P("groups", "sky", None),
        P(),
        P(("groups", "sky"), None, None),
        P("groups", "sky"),
        P(("groups", "sky"), None),
    )
    out_specs = (P(("groups", "sky"), None, None), P(("groups", "sky"), None, None))
    return jax.shard_map(shards, mesh=mesh, in_specs=in_specs, out_specs=out_specs, check_vma=False)
```

```python
import functools

import jax
import jax.numpy as jnp
from jax import lax
from jax.experimental import pallas as pl
from jax.experimental.pallas import tpu as pltpu
from jax.sharding import PartitionSpec as P

LANES = 128
SUB = 8
SIDE = 32
CHUNKS = 8
EMPTY = -1024.0
NEAR = 4


def lane_gather(table, idx):
    dims = lax.GatherDimensionNumbers(
        offset_dims=(),
        collapsed_slice_dims=(1,),
        start_index_map=(1,),
        operand_batching_dims=(0,),
        start_indices_batching_dims=(0,),
    )
    return lax.gather(
        table,
        idx[..., None],
        dims,
        slice_sizes=(1, 1),
        mode=lax.GatherScatterMode.PROMISE_IN_BOUNDS,
    )


def split3(value):
    high = value.astype(jnp.bfloat16)
    rest = value - high.astype(jnp.float32)
    middle = rest.astype(jnp.bfloat16)
    low = (rest - middle.astype(jnp.float32)).astype(jnp.bfloat16)
    return high, middle, low


def regroup_kernel(src_ref, dst_ref):
    planes, tiles, _ = src_ref.shape
    lane = lax.broadcasted_iota(jnp.int32, (SUB, LANES), 1)
    source = (lane & 96) + ((lane & 15) << 1) + ((lane >> 4) & 1)
    for plane in range(planes):
        for base in range(0, tiles, SUB):
            parts = [
                lane_gather(src_ref[plane, pl.ds(base, SUB), pl.ds(c * LANES, LANES)], source)
                for c in range(CHUNKS)
            ]
            for step in (1, 2, 4):
                keep = ((lane >> 4) & step) == 0
                for c in range(CHUNKS):
                    if c & step:
                        continue
                    one, two = parts[c], parts[c + step]
                    parts[c] = jnp.where(keep, one, pltpu.roll(two, step * 16, 1))
                    parts[c + step] = jnp.where(keep, pltpu.roll(one, LANES - step * 16, 1), two)
            for c in range(CHUNKS):
                rows = pl.ds((plane * tiles + base) * CHUNKS + c, SUB, stride=CHUNKS)
                dst_ref[rows, :] = parts[c]


def regroup(potential):
    planes, tiles, pixels = potential.shape
    rows = planes * tiles * pixels // LANES
    return pl.pallas_call(
        regroup_kernel,
        out_shape=jax.ShapeDtypeStruct((rows, LANES), potential.dtype),
        in_specs=[pl.BlockSpec(memory_space=pltpu.VMEM)],
        out_specs=pl.BlockSpec(memory_space=pltpu.VMEM),
        name="regroup",
    )(potential)


def pack_kernel(n_sky, each, per_owner, me_ref, dest_ref, ids_ref, rays_ref, *out_refs):
    me = me_ref[0]
    bundles = dest_ref.shape[1]
    planes = ids_ref.shape[0]
    slots = n_sky * each
    size = 4 * each + SUB
    dest_row = jnp.broadcast_to(dest_ref[...], (bundles, bundles))
    dest_col = jnp.transpose(dest_row)
    row = lax.broadcasted_iota(jnp.int32, (bundles, bundles), 0)
    col = lax.broadcasted_iota(jnp.int32, (bundles, bundles), 1)
    hits = jnp.where((dest_row == dest_col) & (row < col), 1.0, 0.0)
    rank = jnp.sum(hits, axis=0, keepdims=True).astype(jnp.int32)
    slot = (dest_ref[...] ^ me) * each + rank
    place = lax.broadcasted_iota(jnp.int32, (slots, bundles), 0) == slot
    place = jnp.where(place, 1.0, 0.0)
    found = jnp.dot(
        place.astype(jnp.bfloat16),
        jnp.ones((bundles, LANES), jnp.bfloat16),
        preferred_element_type=jnp.float32,
    )
    place3 = jnp.concatenate([place] * 3, axis=1).astype(jnp.bfloat16)
    for part in range(4):
        rays = rays_ref[pl.ds(part, bundles, stride=4), :]
        terms = jnp.concatenate(split3(rays), axis=0)
        sent = jnp.dot(place3, terms, preferred_element_type=jnp.float32)
        if part % 2 == 0:
            sent = jnp.where(found > 0.5, sent, EMPTY)
        for s in range(n_sky):
            rows = pl.ds(s // NEAR * size + part, each, stride=4)
            out_refs[s % NEAR][rows, :] = sent[s * each:(s + 1) * each]
    ids = ids_ref[...]
    plane = lax.broadcasted_iota(jnp.int32, ids.shape, 0)
    owner = (ids // per_owner) ^ dest_ref[...]
    spot = (owner * planes + plane) * per_owner + ids % per_owner
    pad = jnp.zeros((SUB - planes, bundles), jnp.float32)
    fine = jnp.concatenate([(spot & 15).astype(jnp.float32), pad], axis=0)
    coarse = jnp.concatenate([(spot >> 4).astype(jnp.float32), pad], axis=0)
    place = place.astype(jnp.bfloat16)
    contract = (((1,), (1,)), ((), ()))
    fine = lax.dot_general(fine.astype(jnp.bfloat16), place, contract, preferred_element_type=jnp.float32)
    coarse = lax.dot_general(coarse.astype(jnp.bfloat16), place, contract, preferred_element_type=jnp.float32)
    numbers = coarse * 16.0 + fine
    for s in range(n_sky):
        first = s * each
        block = numbers[:, first // LANES * LANES:first // LANES * LANES + LANES]
        turn = (LANES - first % LANES) % LANES
        if turn:
            block = pltpu.roll(block, turn, 1)
        out_refs[s % NEAR][pl.ds(s // NEAR * size + 4 * each, SUB), :] = block


def pack(n_sky, each, per_owner, me, dest, ids, rays):
    part = jax.ShapeDtypeStruct((n_sky // NEAR * (4 * each + SUB), LANES), jnp.float32)
    return pl.pallas_call(
        functools.partial(pack_kernel, n_sky, each, per_owner),
        out_shape=[part] * NEAR,
        in_specs=[pl.BlockSpec(memory_space=pltpu.SMEM)] + [pl.BlockSpec(memory_space=pltpu.VMEM)] * 3,
        out_specs=[pl.BlockSpec(memory_space=pltpu.VMEM)] * NEAR,
        name="pack",
    )(me, dest, ids, rays)


def turn_kernel(size, *refs):
    far = len(refs) - NEAR
    for f in range(far):
        for c in range(NEAR):
            refs[NEAR + f][pl.ds(c * size, size), :] = refs[c][pl.ds(f * size, size), :]


def turn(size, parts):
    far = parts[0].shape[0] // size
    block = jax.ShapeDtypeStruct((NEAR * size, LANES), jnp.float32)
    return pl.pallas_call(
        functools.partial(turn_kernel, size),
        out_shape=[block] * far,
        in_specs=[pl.BlockSpec(memory_space=pltpu.VMEM)] * NEAR,
        out_specs=[pl.BlockSpec(memory_space=pltpu.VMEM)] * far,
        name="turn",
    )(*parts)


def bilinear(f00, f01, f10, f11, u, v):
    one = f00 + u * (f01 - f00)
    two = f10 + u * (f11 - f10)
    return one + v * (two - one)


def lerp(one, two, t):
    return one + t * (two - one)


def window(tables, pos_x, pos_y):
    ix = (pos_x + float(SIDE)).astype(jnp.int32)
    iy = (pos_y + float(SIDE)).astype(jnp.int32)
    u = pos_x - (ix.astype(jnp.float32) - float(SIDE))
    v = pos_y - (iy.astype(jnp.float32) - float(SIDE))
    odd = (ix - 1) >> 1
    even = ix >> 1
    columns = (((even & 15), ((even + 1) & 15)), ((odd & 15), ((odd + 1) & 15)))
    odd_first = (ix & 1) == 0
    by_two = ((iy - 1) & 2) != 0
    by_one = (iy & 1) == 0
    sorted_columns = []
    for a in range(4):
        line = ((iy + (2 - a)) & 28) << 2
        e0, e1 = [lane_gather(tables[2 * a], line + c) for c in columns[0]]
        o0, o1 = [lane_gather(tables[2 * a + 1], line + c) for c in columns[1]]
        sorted_columns.append((
            jnp.where(odd_first, o0, e0),
            jnp.where(odd_first, e0, o0),
            jnp.where(odd_first, o1, e1),
            jnp.where(odd_first, e1, o1),
        ))
    w = [[None] * 4 for _ in range(4)]
    for k in range(4):
        half = [jnp.where(by_two, sorted_columns[(r + 2) & 3][k], sorted_columns[r][k]) for r in range(4)]
        for r in range(4):
            w[r][k] = jnp.where(by_one, half[(r + 1) & 3], half[r])
    return w, u, v


def trace_step(tables, strength, pos_x, pos_y, matrix):
    w, u, v = window(tables, pos_x, pos_y)
    gx = [lerp(w[1][k + 1] - w[1][k], w[2][k + 1] - w[2][k], v) for k in range(3)]
    gy = [lerp(w[r + 1][1] - w[r][1], w[r + 1][2] - w[r][2], u) for r in range(3)]
    fx2 = lerp(gx[0] + gx[1], gx[1] + gx[2], u)
    fxx = lerp(gx[1] - gx[0], gx[2] - gx[1], u)
    fy2 = lerp(gy[0] + gy[1], gy[1] + gy[2], v)
    fyy = lerp(gy[1] - gy[0], gy[2] - gy[1], v)
    wide = [[w[r][k + 2] - w[r][k] for k in range(2)] for r in range(4)]
    fxy4 = bilinear(
        wide[2][0] - wide[0][0], wide[2][1] - wide[0][1],
        wide[3][0] - wide[1][0], wide[3][1] - wide[1][1], u, v)
    half = 0.5 * strength
    hxx, hxy, hyy = strength * fxx, (0.25 * strength) * fxy4, strength * fyy
    m11, m12, m21, m22 = matrix
    matrix = (
        m11 - (hxx * m11 + hxy * m21),
        m12 - (hxx * m12 + hxy * m22),
        m21 - (hxy * m11 + hyy * m21),
        m22 - (hxy * m12 + hyy * m22),
    )
    return pos_x - half * fx2, pos_y - half * fy2, matrix


def trace_kernel(n_sky, each, planes, together, me_ref, lens_ref, *refs):
    far = n_sky // NEAR
    size = 4 * each + SUB
    tile_refs, got_refs = refs[:n_sky], refs[n_sky:n_sky + far]
    shift_ref, matrix_ref, tiles, chosen, rays, places, sems = refs[n_sky + far:]
    me = me_ref[0]
    slots = n_sky * each
    rows = tile_refs[0].shape[0]
    copies = []
    for s in range(n_sky):
        source = me ^ s
        got_ref, first = got_refs[s // NEAR], s % NEAR * size
        copies.append((
            pltpu.make_async_copy(
                got_ref.at[pl.ds(first + 4 * each, SUB), :],
                places.at[pl.ds(source * SUB, SUB), :],
                sems.at[0, s]),
            pltpu.make_async_copy(tile_refs[s], tiles.at[pl.ds(s * rows, rows), :], sems.at[1, s]),
            pltpu.make_async_copy(
                got_ref.at[pl.ds(first, 4 * each), :],
                rays.at[pl.ds(source * 4 * each, 4 * each), :],
                sems.at[2, s]),
        ))
    for kind in range(3):
        for s in range(n_sky):
            copies[s][kind].start()
    for kind in range(3):
        for s in range(n_sky):
            copies[s][kind].wait()

    def body(step, carry):
        chains = []
        first = pl.multiple_of(step * (together * SUB), together * SUB)
        for plane in range(planes):
            for part in range(together):
                for k in range(SUB):
                    slot = first + (part * SUB + k)
                    spot = places[slot // each * SUB + plane, slot % each].astype(jnp.int32)
                    tile = tiles[pl.ds(pl.multiple_of(spot * CHUNKS, CHUNKS), CHUNKS), :]
                    chosen[pl.ds((plane * together + part) * CHUNKS * SUB + k, CHUNKS, stride=SUB), :] = tile
        for part in range(together):
            base = first + part * SUB
            for h in range(2):
                x0 = rays[pl.ds(base * 4 + 2 * h, SUB, stride=4), :]
                y0 = rays[pl.ds(base * 4 + 2 * h + 1, SUB, stride=4), :]
                one = jnp.ones_like(x0)
                zero = jnp.zeros_like(x0)
                chains.append((part, h, x0, y0, (x0, y0, (one, zero, zero, one))))
        for plane in range(planes):
            strength = lens_ref[plane]
            later = []
            for part, h, x0, y0, state in chains:
                tables = [
                    chosen[pl.ds(((plane * together + part) * CHUNKS + c) * SUB, SUB), :]
                    for c in range(CHUNKS)
                ]
                later.append((part, h, x0, y0, trace_step(tables, strength, *state)))
            chains = later
        for part, h, x0, y0, (x, y, matrix) in chains:
            base = first + part * SUB
            used = x0 > EMPTY * 0.5
            shift_ref[pl.ds(base * 4 + 2 * h, SUB, stride=4), :] = jnp.where(used, x - x0, 0.0)
            shift_ref[pl.ds(base * 4 + 2 * h + 1, SUB, stride=4), :] = jnp.where(used, y - y0, 0.0)
            for e in range(4):
                matrix_ref[pl.ds(base * 8 + 4 * h + e, SUB, stride=8), :] = jnp.where(used, matrix[e], 0.0)
        return carry

    lax.fori_loop(0, slots // (SUB * together), body, 0)


def trace(each, planes, me, lens_weight, tiles, got):
    n_sky = len(tiles)
    slots = n_sky * each
    rows = tiles[0].shape[0]
    together = 4
    return pl.pallas_call(
        functools.partial(trace_kernel, n_sky, each, planes, together),
        out_shape=(
            jax.ShapeDtypeStruct((slots * 4, LANES), jnp.float32),
            jax.ShapeDtypeStruct((slots * 8, LANES), jnp.float32),
        ),
        in_specs=[pl.BlockSpec(memory_space=pltpu.SMEM)] * 2 + [pl.BlockSpec(memory_space=pl.ANY)] * (n_sky + len(got)),
        out_specs=(
            pl.BlockSpec(memory_space=pltpu.VMEM),
            pl.BlockSpec(memory_space=pltpu.VMEM),
        ),
        scratch_shapes=[
            pltpu.VMEM((n_sky * rows, LANES), jnp.float32),
            pltpu.VMEM((planes * together * CHUNKS * SUB, LANES), jnp.float32),
            pltpu.VMEM((slots * 4, LANES), jnp.float32),
            pltpu.SMEM((n_sky * SUB, LANES), jnp.float32),
            pltpu.SemaphoreType.DMA((3, n_sky)),
        ],
        compiler_params=pltpu.CompilerParams(vmem_limit_bytes=40 * 1024 * 1024),
        name="trace",
    )(me, lens_weight, *tiles, *got)


def flipped(value, n_sky, bits):
    return lax.ppermute(value, "sky", [(i, i ^ bits) for i in range(n_sky)])


def spread(held, n_sky, bits):
    for bit in bits:
        for s in [s for s in held if s & (2 * bit - 1) == 0]:
            if s ^ bit not in held:
                held[s ^ bit] = flipped(held[s], n_sky, bit)


def shards(potential, lens_weight, ray_start, patch_index, destination):
    n_sky = lax.axis_size("sky")
    me = lax.axis_index("sky").reshape(1)
    planes, per_owner, _ = potential.shape
    bundles, _, rays = ray_start.shape
    each = max(2, 2 * bundles // n_sky)
    slots = n_sky * each
    halves = rays // LANES
    bits = [1 << k for k in reversed(range((n_sky - 1).bit_length()))]
    flat = ray_start.reshape(bundles, 2, halves, LANES).transpose(0, 2, 1, 3).reshape(bundles * 2 * halves, LANES)
    own = regroup(potential)
    held = {0: own}
    for bit in bits[:2]:
        held[bit] = flipped(own, n_sky, bit)
    own, flat = lax.optimization_barrier((own, flat))
    sent = pack(n_sky, each, per_owner, me, destination.reshape(1, bundles), patch_index, flat)
    sent = [sent[0]] + [flipped(sent[s], n_sky, s) for s in range(1, NEAR)]
    held[bits[0] ^ bits[1]] = flipped(held[bits[0]], n_sky, bits[1])
    got = turn(4 * each + SUB, sent)
    early = [0, bits[0], bits[1]]
    *got, a, b, c = lax.optimization_barrier((*got, *[held[s] for s in early]))
    held.update(zip(early, (a, b, c)))
    got = [got[0]] + [flipped(got[f], n_sky, f * NEAR) for f in range(1, len(got))]
    spread(held, n_sky, bits[:-1])
    mid, *evens = lax.optimization_barrier((got[len(got) // 2], *[held[s] for s in range(0, n_sky, 2)]))
    got[len(got) // 2] = mid
    held.update(zip(range(0, n_sky, 2), evens))
    spread(held, n_sky, bits)
    shift, matrix = trace(each, planes, me, lens_weight, [held[s] for s in range(n_sky)], got)
    shift = shift.reshape(slots, halves, 2, LANES).transpose(0, 2, 1, 3).reshape(slots, 2, rays)
    matrix = matrix.reshape(slots, halves, 4, LANES).transpose(0, 2, 1, 3).reshape(slots, 4, rays)
    return shift, matrix


def solution(mesh):
    in_specs = (
        P("groups", "sky", None),
        P(),
        P(("groups", "sky"), None, None),
        P("groups", "sky"),
        P(("groups", "sky"), None),
    )
    out_specs = (P(("groups", "sky"), None, None), P(("groups", "sky"), None, None))
    return jax.shard_map(shards, mesh=mesh, in_specs=in_specs, out_specs=out_specs, check_vma=False)
```

```python
import functools

import jax
import jax.numpy as jnp
from jax import lax
from jax.experimental import pallas as pl
from jax.experimental.pallas import tpu as pltpu
from jax.sharding import PartitionSpec as P

LANES = 128
SUB = 8
SIDE = 32
CHUNKS = 8
EMPTY = -1024.0
NEAR = 4


def lane_gather(table, idx):
    dims = lax.GatherDimensionNumbers(
        offset_dims=(),
        collapsed_slice_dims=(1,),
        start_index_map=(1,),
        operand_batching_dims=(0,),
        start_indices_batching_dims=(0,),
    )
    return lax.gather(
        table,
        idx[..., None],
        dims,
        slice_sizes=(1, 1),
        mode=lax.GatherScatterMode.PROMISE_IN_BOUNDS,
    )


def split3(value):
    high = value.astype(jnp.bfloat16)
    rest = value - high.astype(jnp.float32)
    middle = rest.astype(jnp.bfloat16)
    low = (rest - middle.astype(jnp.float32)).astype(jnp.bfloat16)
    return high, middle, low


def regroup_kernel(src_ref, dst_ref):
    planes, tiles, _ = src_ref.shape
    lane = lax.broadcasted_iota(jnp.int32, (SUB, LANES), 1)
    source = (lane & 96) + ((lane & 15) << 1) + ((lane >> 4) & 1)
    for plane in range(planes):
        for base in range(0, tiles, SUB):
            parts = [
                lane_gather(src_ref[plane, pl.ds(base, SUB), pl.ds(c * LANES, LANES)], source)
                for c in range(CHUNKS)
            ]
            for step in (1, 2, 4):
                keep = ((lane >> 4) & step) == 0
                for c in range(CHUNKS):
                    if c & step:
                        continue
                    one, two = parts[c], parts[c + step]
                    parts[c] = jnp.where(keep, one, pltpu.roll(two, step * 16, 1))
                    parts[c + step] = jnp.where(keep, pltpu.roll(one, LANES - step * 16, 1), two)
            for c in range(CHUNKS):
                rows = pl.ds((plane * tiles + base) * CHUNKS + c, SUB, stride=CHUNKS)
                dst_ref[rows, :] = parts[c]


def pack_kernel(n_sky, each, per_owner, me_ref, dest_ref, ids_ref, rays_ref, *out_refs):
    me = me_ref[0]
    bundles = dest_ref.shape[1]
    planes = ids_ref.shape[0]
    slots = n_sky * each
    size = 4 * each + SUB
    dest_row = jnp.broadcast_to(dest_ref[...], (bundles, bundles))
    dest_col = jnp.transpose(dest_row)
    row = lax.broadcasted_iota(jnp.int32, (bundles, bundles), 0)
    col = lax.broadcasted_iota(jnp.int32, (bundles, bundles), 1)
    hits = jnp.where((dest_row == dest_col) & (row < col), 1.0, 0.0)
    rank = jnp.sum(hits, axis=0, keepdims=True).astype(jnp.int32)
    slot = (dest_ref[...] ^ me) * each + rank
    place = lax.broadcasted_iota(jnp.int32, (slots, bundles), 0) == slot
    place = jnp.where(place, 1.0, 0.0)
    found = jnp.dot(
        place.astype(jnp.bfloat16),
        jnp.ones((bundles, LANES), jnp.bfloat16),
        preferred_element_type=jnp.float32,
    )
    place3 = jnp.concatenate([place] * 3, axis=1).astype(jnp.bfloat16)
    for part in range(4):
        rays = rays_ref[pl.ds(part, bundles, stride=4), :]
        terms = jnp.concatenate(split3(rays), axis=0)
        sent = jnp.dot(place3, terms, preferred_element_type=jnp.float32)
        if part % 2 == 0:
            sent = jnp.where(found > 0.5, sent, EMPTY)
        for s in range(n_sky):
            rows = pl.ds(s // NEAR * size + part, each, stride=4)
            out_refs[s % NEAR][rows, :] = sent[s * each:(s + 1) * each]
    ids = ids_ref[...]
    plane = lax.broadcasted_iota(jnp.int32, ids.shape, 0)
    owner = (ids // per_owner) ^ dest_ref[...]
    spot = (owner * planes + plane) * per_owner + ids % per_owner
    pad = jnp.zeros((SUB - planes, bundles), jnp.float32)
    fine = jnp.concatenate([(spot & 15).astype(jnp.float32), pad], axis=0)
    coarse = jnp.concatenate([(spot >> 4).astype(jnp.float32), pad], axis=0)
    place = place.astype(jnp.bfloat16)
    contract = (((1,), (1,)), ((), ()))
    fine = lax.dot_general(fine.astype(jnp.bfloat16), place, contract, preferred_element_type=jnp.float32)
    coarse = lax.dot_general(coarse.astype(jnp.bfloat16), place, contract, preferred_element_type=jnp.float32)
    numbers = coarse * 16.0 + fine
    for s in range(n_sky):
        first = s * each
        block = numbers[:, first // LANES * LANES:first // LANES * LANES + LANES]
        turn = (LANES - first % LANES) % LANES
        if turn:
            block = pltpu.roll(block, turn, 1)
        out_refs[s % NEAR][pl.ds(s // NEAR * size + 4 * each, SUB), :] = block


def prepare_kernel(n_sky, each, me_ref, dest_ref, ids_ref, rays_ref, src_ref, dst_ref, *out_refs):
    regroup_kernel(src_ref, dst_ref)
    pack_kernel(n_sky, each, src_ref.shape[1], me_ref, dest_ref, ids_ref, rays_ref, *out_refs)


def prepare(n_sky, each, me, dest, ids, rays, potential):
    planes, tiles, pixels = potential.shape
    part = jax.ShapeDtypeStruct((n_sky // NEAR * (4 * each + SUB), LANES), jnp.float32)
    own = jax.ShapeDtypeStruct((planes * tiles * pixels // LANES, LANES), jnp.float32)
    own, *sent = pl.pallas_call(
        functools.partial(prepare_kernel, n_sky, each),
        out_shape=[own] + [part] * NEAR,
        in_specs=[pl.BlockSpec(memory_space=pltpu.SMEM)] + [pl.BlockSpec(memory_space=pltpu.VMEM)] * 4,
        out_specs=[pl.BlockSpec(memory_space=pltpu.VMEM)] * (1 + NEAR),
        name="prepare",
    )(me, dest, ids, rays, potential)
    return own, sent


def turn_kernel(size, *refs):
    far = len(refs) - NEAR
    for f in range(far):
        for c in range(NEAR):
            refs[NEAR + f][pl.ds(c * size, size), :] = refs[c][pl.ds(f * size, size), :]


def turn(size, parts):
    far = parts[0].shape[0] // size
    block = jax.ShapeDtypeStruct((NEAR * size, LANES), jnp.float32)
    return pl.pallas_call(
        functools.partial(turn_kernel, size),
        out_shape=[block] * far,
        in_specs=[pl.BlockSpec(memory_space=pltpu.VMEM)] * NEAR,
        out_specs=[pl.BlockSpec(memory_space=pltpu.VMEM)] * far,
        name="turn",
    )(*parts)


def bilinear(f00, f01, f10, f11, u, v):
    one = f00 + u * (f01 - f00)
    two = f10 + u * (f11 - f10)
    return one + v * (two - one)


def lerp(one, two, t):
    return one + t * (two - one)


def window(tables, pos_x, pos_y):
    ix = (pos_x + float(SIDE)).astype(jnp.int32)
    iy = (pos_y + float(SIDE)).astype(jnp.int32)
    u = pos_x - (ix.astype(jnp.float32) - float(SIDE))
    v = pos_y - (iy.astype(jnp.float32) - float(SIDE))
    odd = (ix - 1) >> 1
    even = ix >> 1
    columns = (((even & 15), ((even + 1) & 15)), ((odd & 15), ((odd + 1) & 15)))
    odd_first = (ix & 1) == 0
    by_two = ((iy - 1) & 2) != 0
    by_one = (iy & 1) == 0
    sorted_columns = []
    for a in range(4):
        line = ((iy + (2 - a)) & 28) << 2
        e0, e1 = [lane_gather(tables[2 * a], line + c) for c in columns[0]]
        o0, o1 = [lane_gather(tables[2 * a + 1], line + c) for c in columns[1]]
        sorted_columns.append((
            jnp.where(odd_first, o0, e0),
            jnp.where(odd_first, e0, o0),
            jnp.where(odd_first, o1, e1),
            jnp.where(odd_first, e1, o1),
        ))
    w = [[None] * 4 for _ in range(4)]
    for k in range(4):
        half = [jnp.where(by_two, sorted_columns[(r + 2) & 3][k], sorted_columns[r][k]) for r in range(4)]
        for r in range(4):
            w[r][k] = jnp.where(by_one, half[(r + 1) & 3], half[r])
    return w, u, v


def trace_step(tables, strength, pos_x, pos_y, matrix):
    w, u, v = window(tables, pos_x, pos_y)
    gx = [lerp(w[1][k + 1] - w[1][k], w[2][k + 1] - w[2][k], v) for k in range(3)]
    gy = [lerp(w[r + 1][1] - w[r][1], w[r + 1][2] - w[r][2], u) for r in range(3)]
    fx2 = lerp(gx[0] + gx[1], gx[1] + gx[2], u)
    fxx = lerp(gx[1] - gx[0], gx[2] - gx[1], u)
    fy2 = lerp(gy[0] + gy[1], gy[1] + gy[2], v)
    fyy = lerp(gy[1] - gy[0], gy[2] - gy[1], v)
    wide = [[w[r][k + 2] - w[r][k] for k in range(2)] for r in range(4)]
    fxy4 = bilinear(
        wide[2][0] - wide[0][0], wide[2][1] - wide[0][1],
        wide[3][0] - wide[1][0], wide[3][1] - wide[1][1], u, v)
    half = 0.5 * strength
    hxx, hxy, hyy = strength * fxx, (0.25 * strength) * fxy4, strength * fyy
    m11, m12, m21, m22 = matrix
    matrix = (
        m11 - (hxx * m11 + hxy * m21),
        m12 - (hxx * m12 + hxy * m22),
        m21 - (hxy * m11 + hyy * m21),
        m22 - (hxy * m12 + hyy * m22),
    )
    return pos_x - half * fx2, pos_y - half * fy2, matrix


def trace_kernel(n_sky, each, planes, together, me_ref, lens_ref, *refs):
    far = n_sky // NEAR
    size = 4 * each + SUB
    tile_refs, got_refs = refs[:n_sky], refs[n_sky:n_sky + far]
    shift_ref, matrix_ref, tiles, chosen, rays, places, sems = refs[n_sky + far:]
    me = me_ref[0]
    slots = n_sky * each
    rows = tile_refs[0].shape[0]
    copies = []
    for s in range(n_sky):
        source = me ^ s
        got_ref, first = got_refs[s // NEAR], s % NEAR * size
        copies.append((
            pltpu.make_async_copy(
                got_ref.at[pl.ds(first + 4 * each, SUB), :],
                places.at[pl.ds(source * SUB, SUB), :],
                sems.at[0, s]),
            pltpu.make_async_copy(tile_refs[s], tiles.at[pl.ds(s * rows, rows), :], sems.at[1, s]),
            pltpu.make_async_copy(
                got_ref.at[pl.ds(first, 4 * each), :],
                rays.at[pl.ds(source * 4 * each, 4 * each), :],
                sems.at[2, s]),
        ))
    for kind in range(3):
        for s in range(n_sky):
            copies[s][kind].start()
    for kind in range(3):
        for s in range(n_sky):
            copies[s][kind].wait()

    def body(step, carry):
        chains = []
        first = pl.multiple_of(step * (together * SUB), together * SUB)
        for plane in range(planes):
            for part in range(together):
                for k in range(SUB):
                    slot = first + (part * SUB + k)
                    spot = places[slot // each * SUB + plane, slot % each].astype(jnp.int32)
                    tile = tiles[pl.ds(pl.multiple_of(spot * CHUNKS, CHUNKS), CHUNKS), :]
                    chosen[pl.ds((plane * together + part) * CHUNKS * SUB + k, CHUNKS, stride=SUB), :] = tile
        for part in range(together):
            base = first + part * SUB
            for h in range(2):
                x0 = rays[pl.ds(base * 4 + 2 * h, SUB, stride=4), :]
                y0 = rays[pl.ds(base * 4 + 2 * h + 1, SUB, stride=4), :]
                one = jnp.ones_like(x0)
                zero = jnp.zeros_like(x0)
                chains.append((part, h, x0, y0, (x0, y0, (one, zero, zero, one))))
        for plane in range(planes):
            strength = lens_ref[plane]
            later = []
            for part, h, x0, y0, state in chains:
                tables = [
                    chosen[pl.ds(((plane * together + part) * CHUNKS + c) * SUB, SUB), :]
                    for c in range(CHUNKS)
                ]
                later.append((part, h, x0, y0, trace_step(tables, strength, *state)))
            chains = later
        for part, h, x0, y0, (x, y, matrix) in chains:
            base = first + part * SUB
            used = x0 > EMPTY * 0.5
            shift_ref[pl.ds(base * 4 + 2 * h, SUB, stride=4), :] = jnp.where(used, x - x0, 0.0)
            shift_ref[pl.ds(base * 4 + 2 * h + 1, SUB, stride=4), :] = jnp.where(used, y - y0, 0.0)
            for e in range(4):
                matrix_ref[pl.ds(base * 8 + 4 * h + e, SUB, stride=8), :] = jnp.where(used, matrix[e], 0.0)
        return carry

    lax.fori_loop(0, slots // (SUB * together), body, 0)


def trace(each, planes, me, lens_weight, tiles, got):
    n_sky = len(tiles)
    slots = n_sky * each
    rows = tiles[0].shape[0]
    together = 4
    return pl.pallas_call(
        functools.partial(trace_kernel, n_sky, each, planes, together),
        out_shape=(
            jax.ShapeDtypeStruct((slots * 4, LANES), jnp.float32),
            jax.ShapeDtypeStruct((slots * 8, LANES), jnp.float32),
        ),
        in_specs=[pl.BlockSpec(memory_space=pltpu.SMEM)] * 2 + [pl.BlockSpec(memory_space=pl.ANY)] * (n_sky + len(got)),
        out_specs=(
            pl.BlockSpec(memory_space=pltpu.VMEM),
            pl.BlockSpec(memory_space=pltpu.VMEM),
        ),
        scratch_shapes=[
            pltpu.VMEM((n_sky * rows, LANES), jnp.float32),
            pltpu.VMEM((planes * together * CHUNKS * SUB, LANES), jnp.float32),
            pltpu.VMEM((slots * 4, LANES), jnp.float32),
            pltpu.SMEM((n_sky * SUB, LANES), jnp.float32),
            pltpu.SemaphoreType.DMA((3, n_sky)),
        ],
        compiler_params=pltpu.CompilerParams(vmem_limit_bytes=40 * 1024 * 1024),
        name="trace",
    )(me, lens_weight, *tiles, *got)


def flipped(value, n_sky, bits):
    return lax.ppermute(value, "sky", [(i, i ^ bits) for i in range(n_sky)])


def spread(held, n_sky, bits):
    for bit in bits:
        for s in [s for s in held if s & (2 * bit - 1) == 0]:
            if s ^ bit not in held:
                held[s ^ bit] = flipped(held[s], n_sky, bit)


def shards(potential, lens_weight, ray_start, patch_index, destination):
    n_sky = lax.axis_size("sky")
    me = lax.axis_index("sky").reshape(1)
    planes = potential.shape[0]
    bundles, _, rays = ray_start.shape
    each = max(2, 2 * bundles // n_sky)
    slots = n_sky * each
    halves = rays // LANES
    bits = [1 << k for k in reversed(range((n_sky - 1).bit_length()))]
    flat = ray_start.reshape(bundles, 2, halves, LANES).transpose(0, 2, 1, 3).reshape(bundles * 2 * halves, LANES)
    own, sent = prepare(n_sky, each, me, destination.reshape(1, bundles), patch_index, flat, potential)
    sent = [sent[0]] + [flipped(sent[s], n_sky, s) for s in range(1, NEAR)]
    held = {0: own}
    for bit in bits[:2]:
        held[bit] = flipped(own, n_sky, bit)
    held[bits[0] ^ bits[1]] = flipped(held[bits[0]], n_sky, bits[1])
    got = turn(4 * each + SUB, sent)
    early = [0, bits[0], bits[1]]
    *got, a, b, c = lax.optimization_barrier((*got, *[held[s] for s in early]))
    held.update(zip(early, (a, b, c)))
    got = [got[0]] + [flipped(got[f], n_sky, f * NEAR) for f in range(1, len(got))]
    spread(held, n_sky, bits[:-1])
    half = len(got) // 2
    for mid, low in ((half, 0), (half + 1, n_sky // 2)):
        some = range(low, low + n_sky // 2, 2)
        got[mid], *evens = lax.optimization_barrier((got[mid], *[held[s] for s in some]))
        held.update(zip(some, evens))
    spread(held, n_sky, bits)
    shift, matrix = trace(each, planes, me, lens_weight, [held[s] for s in range(n_sky)], got)
    shift = shift.reshape(slots, halves, 2, LANES).transpose(0, 2, 1, 3).reshape(slots, 2, rays)
    matrix = matrix.reshape(slots, halves, 4, LANES).transpose(0, 2, 1, 3).reshape(slots, 4, rays)
    return shift, matrix


def solution(mesh):
    in_specs = (
        P("groups", "sky", None),
        P(),
        P(("groups", "sky"), None, None),
        P("groups", "sky"),
        P(("groups", "sky"), None),
    )
    out_specs = (P(("groups", "sky"), None, None), P(("groups", "sky"), None, None))
    return jax.shard_map(shards, mesh=mesh, in_specs=in_specs, out_specs=out_specs, check_vma=False)
```

```python
import functools

import jax
import jax.numpy as jnp
from jax import lax
from jax.experimental import pallas as pl
from jax.experimental.pallas import tpu as pltpu
from jax.sharding import PartitionSpec as P

LANES = 128
SUB = 8
SIDE = 32
CHUNKS = 8
EMPTY = -1024.0
NEAR = 4


def lane_gather(table, idx):
    dims = lax.GatherDimensionNumbers(
        offset_dims=(),
        collapsed_slice_dims=(1,),
        start_index_map=(1,),
        operand_batching_dims=(0,),
        start_indices_batching_dims=(0,),
    )
    return lax.gather(
        table,
        idx[..., None],
        dims,
        slice_sizes=(1, 1),
        mode=lax.GatherScatterMode.PROMISE_IN_BOUNDS,
    )


def split3(value):
    high = value.astype(jnp.bfloat16)
    rest = value - high.astype(jnp.float32)
    middle = rest.astype(jnp.bfloat16)
    low = (rest - middle.astype(jnp.float32)).astype(jnp.bfloat16)
    return high, middle, low


def regroup_kernel(src_ref, dst_ref):
    planes, tiles, _ = src_ref.shape
    lane = lax.broadcasted_iota(jnp.int32, (SUB, LANES), 1)
    source = (lane & 96) + ((lane & 15) << 1) + ((lane >> 4) & 1)
    for plane in range(planes):
        for base in range(0, tiles, SUB):
            parts = [
                lane_gather(src_ref[plane, pl.ds(base, SUB), pl.ds(c * LANES, LANES)], source)
                for c in range(CHUNKS)
            ]
            for step in (1, 2, 4):
                keep = ((lane >> 4) & step) == 0
                for c in range(CHUNKS):
                    if c & step:
                        continue
                    one, two = parts[c], parts[c + step]
                    parts[c] = jnp.where(keep, one, pltpu.roll(two, step * 16, 1))
                    parts[c + step] = jnp.where(keep, pltpu.roll(one, LANES - step * 16, 1), two)
            for c in range(CHUNKS):
                rows = pl.ds((plane * tiles + base) * CHUNKS + c, SUB, stride=CHUNKS)
                dst_ref[rows, :] = parts[c]


def pack_kernel(n_sky, each, per_owner, me_ref, dest_ref, ids_ref, rays_ref, *out_refs):
    me = me_ref[0]
    bundles = dest_ref.shape[1]
    planes = ids_ref.shape[0]
    slots = n_sky * each
    size = 4 * each + SUB
    dest_row = jnp.broadcast_to(dest_ref[...], (bundles, bundles))
    dest_col = jnp.transpose(dest_row)
    row = lax.broadcasted_iota(jnp.int32, (bundles, bundles), 0)
    col = lax.broadcasted_iota(jnp.int32, (bundles, bundles), 1)
    hits = jnp.where((dest_row == dest_col) & (row < col), 1.0, 0.0)
    rank = jnp.sum(hits, axis=0, keepdims=True).astype(jnp.int32)
    slot = (dest_ref[...] ^ me) * each + rank
    place = lax.broadcasted_iota(jnp.int32, (slots, bundles), 0) == slot
    place = jnp.where(place, 1.0, 0.0)
    found = jnp.dot(
        place.astype(jnp.bfloat16),
        jnp.ones((bundles, LANES), jnp.bfloat16),
        preferred_element_type=jnp.float32,
    )
    place3 = jnp.concatenate([place] * 3, axis=1).astype(jnp.bfloat16)
    for part in range(4):
        rays = rays_ref[pl.ds(part, bundles, stride=4), :]
        terms = jnp.concatenate(split3(rays), axis=0)
        sent = jnp.dot(place3, terms, preferred_element_type=jnp.float32)
        if part % 2 == 0:
            sent = jnp.where(found > 0.5, sent, EMPTY)
        for s in range(n_sky):
            rows = pl.ds(s // NEAR * size + part, each, stride=4)
            out_refs[s % NEAR][rows, :] = sent[s * each:(s + 1) * each]
    ids = ids_ref[...]
    plane = lax.broadcasted_iota(jnp.int32, ids.shape, 0)
    owner = (ids // per_owner) ^ dest_ref[...]
    spot = (owner * planes + plane) * per_owner + ids % per_owner
    pad = jnp.zeros((SUB - planes, bundles), jnp.float32)
    fine = jnp.concatenate([(spot & 15).astype(jnp.float32), pad], axis=0)
    coarse = jnp.concatenate([(spot >> 4).astype(jnp.float32), pad], axis=0)
    place = place.astype(jnp.bfloat16)
    contract = (((1,), (1,)), ((), ()))
    fine = lax.dot_general(fine.astype(jnp.bfloat16), place, contract, preferred_element_type=jnp.float32)
    coarse = lax.dot_general(coarse.astype(jnp.bfloat16), place, contract, preferred_element_type=jnp.float32)
    numbers = coarse * 16.0 + fine
    for s in range(n_sky):
        first = s * each
        block = numbers[:, first // LANES * LANES:first // LANES * LANES + LANES]
        turn = (LANES - first % LANES) % LANES
        if turn:
            block = pltpu.roll(block, turn, 1)
        out_refs[s % NEAR][pl.ds(s // NEAR * size + 4 * each, SUB), :] = block


def prepare_kernel(n_sky, each, me_ref, dest_ref, ids_ref, rays_ref, src_ref, dst_ref, *out_refs):
    regroup_kernel(src_ref, dst_ref)
    pack_kernel(n_sky, each, src_ref.shape[1], me_ref, dest_ref, ids_ref, rays_ref, *out_refs)


def prepare(n_sky, each, me, dest, ids, rays, potential):
    planes, tiles, pixels = potential.shape
    part = jax.ShapeDtypeStruct((n_sky // NEAR * (4 * each + SUB), LANES), jnp.float32)
    own = jax.ShapeDtypeStruct((planes * tiles * pixels // LANES, LANES), jnp.float32)
    own, *sent = pl.pallas_call(
        functools.partial(prepare_kernel, n_sky, each),
        out_shape=[own] + [part] * NEAR,
        in_specs=[pl.BlockSpec(memory_space=pltpu.SMEM)] + [pl.BlockSpec(memory_space=pltpu.VMEM)] * 4,
        out_specs=[pl.BlockSpec(memory_space=pltpu.VMEM)] * (1 + NEAR),
        name="prepare",
    )(me, dest, ids, rays, potential)
    return own, sent


def turn_kernel(size, *refs):
    far = len(refs) - NEAR
    for f in range(far):
        for c in range(NEAR):
            refs[NEAR + f][pl.ds(c * size, size), :] = refs[c][pl.ds(f * size, size), :]


def turn(size, parts):
    far = parts[0].shape[0] // size
    block = jax.ShapeDtypeStruct((NEAR * size, LANES), jnp.float32)
    return pl.pallas_call(
        functools.partial(turn_kernel, size),
        out_shape=[block] * far,
        in_specs=[pl.BlockSpec(memory_space=pltpu.VMEM)] * NEAR,
        out_specs=[pl.BlockSpec(memory_space=pltpu.VMEM)] * far,
        name="turn",
    )(*parts)


def bilinear(f00, f01, f10, f11, u, v):
    one = f00 + u * (f01 - f00)
    two = f10 + u * (f11 - f10)
    return one + v * (two - one)


def lerp(one, two, t):
    return one + t * (two - one)


def window(tables, pos_x, pos_y):
    ix = (pos_x + float(SIDE)).astype(jnp.int32)
    iy = (pos_y + float(SIDE)).astype(jnp.int32)
    u = pos_x - (ix.astype(jnp.float32) - float(SIDE))
    v = pos_y - (iy.astype(jnp.float32) - float(SIDE))
    odd = (ix - 1) >> 1
    even = ix >> 1
    columns = (((even & 15), ((even + 1) & 15)), ((odd & 15), ((odd + 1) & 15)))
    odd_first = (ix & 1) == 0
    by_two = ((iy - 1) & 2) != 0
    by_one = (iy & 1) == 0
    sorted_columns = []
    for a in range(4):
        line = ((iy + (2 - a)) & 28) << 2
        e0, e1 = [lane_gather(tables[2 * a], line + c) for c in columns[0]]
        o0, o1 = [lane_gather(tables[2 * a + 1], line + c) for c in columns[1]]
        sorted_columns.append((
            jnp.where(odd_first, o0, e0),
            jnp.where(odd_first, e0, o0),
            jnp.where(odd_first, o1, e1),
            jnp.where(odd_first, e1, o1),
        ))
    w = [[None] * 4 for _ in range(4)]
    for k in range(4):
        half = [jnp.where(by_two, sorted_columns[(r + 2) & 3][k], sorted_columns[r][k]) for r in range(4)]
        for r in range(4):
            w[r][k] = jnp.where(by_one, half[(r + 1) & 3], half[r])
    return w, u, v


def trace_step(tables, strength, pos_x, pos_y, matrix):
    w, u, v = window(tables, pos_x, pos_y)
    gx = [lerp(w[1][k + 1] - w[1][k], w[2][k + 1] - w[2][k], v) for k in range(3)]
    gy = [lerp(w[r + 1][1] - w[r][1], w[r + 1][2] - w[r][2], u) for r in range(3)]
    fx2 = lerp(gx[0] + gx[1], gx[1] + gx[2], u)
    fxx = lerp(gx[1] - gx[0], gx[2] - gx[1], u)
    fy2 = lerp(gy[0] + gy[1], gy[1] + gy[2], v)
    fyy = lerp(gy[1] - gy[0], gy[2] - gy[1], v)
    wide = [[w[r][k + 2] - w[r][k] for k in range(2)] for r in range(4)]
    fxy4 = bilinear(
        wide[2][0] - wide[0][0], wide[2][1] - wide[0][1],
        wide[3][0] - wide[1][0], wide[3][1] - wide[1][1], u, v)
    half = 0.5 * strength
    hxx, hxy, hyy = strength * fxx, (0.25 * strength) * fxy4, strength * fyy
    m11, m12, m21, m22 = matrix
    matrix = (
        m11 - (hxx * m11 + hxy * m21),
        m12 - (hxx * m12 + hxy * m22),
        m21 - (hxy * m11 + hyy * m21),
        m22 - (hxy * m12 + hyy * m22),
    )
    return pos_x - half * fx2, pos_y - half * fy2, matrix


def store_kernel(*refs):
    *tile_refs, store_ref, sems = refs
    rows = tile_refs[0].shape[0]
    copies = [
        pltpu.make_async_copy(tile_ref, store_ref.at[pl.ds(s * rows, rows), :], sems.at[s])
        for s, tile_ref in enumerate(tile_refs)
    ]
    for copy in copies:
        copy.start()
    for copy in copies:
        copy.wait()


def store(tiles):
    rows = tiles[0].shape[0]
    return pl.pallas_call(
        store_kernel,
        out_shape=jax.ShapeDtypeStruct((len(tiles) * rows, LANES), jnp.float32),
        in_specs=[pl.BlockSpec(memory_space=pl.ANY)] * len(tiles),
        out_specs=pl.BlockSpec(memory_space=pltpu.VMEM),
        scratch_shapes=[pltpu.SemaphoreType.DMA((len(tiles),))],
        compiler_params=pltpu.CompilerParams(vmem_limit_bytes=40 * 1024 * 1024),
        name="store",
    )(*tiles)


def trace_kernel(f, each, planes, together, me_ref, lens_ref, tiles, got_ref, *refs):
    shift_ref, matrix_ref, chosen, rays, places, shift, matrix, sems = refs[-8:]
    me = me_ref[0]
    slots = NEAR * each
    size = 4 * each + SUB
    numbers = [
        pltpu.make_async_copy(
            got_ref.at[pl.ds(c * size + 4 * each, SUB), :],
            places.at[pl.ds(c * SUB, SUB), :],
            sems.at[0, c])
        for c in range(NEAR)
    ]
    for copy in numbers:
        copy.start()
    for c in range(NEAR):
        rays[pl.ds(c * 4 * each, 4 * each), :] = got_ref[pl.ds(c * size, 4 * each), :]
    for copy in numbers:
        copy.wait()

    def body(step, carry):
        chains = []
        first = pl.multiple_of(step * (together * SUB), together * SUB)
        for plane in range(planes):
            for part in range(together):
                for k in range(SUB):
                    slot = first + (part * SUB + k)
                    spot = places[slot // each * SUB + plane, slot % each].astype(jnp.int32)
                    tile = tiles[pl.ds(pl.multiple_of(spot * CHUNKS, CHUNKS), CHUNKS), :]
                    chosen[pl.ds((plane * together + part) * CHUNKS * SUB + k, CHUNKS, stride=SUB), :] = tile
        for part in range(together):
            base = first + part * SUB
            for h in range(2):
                x0 = rays[pl.ds(base * 4 + 2 * h, SUB, stride=4), :]
                y0 = rays[pl.ds(base * 4 + 2 * h + 1, SUB, stride=4), :]
                one = jnp.ones_like(x0)
                zero = jnp.zeros_like(x0)
                chains.append((part, h, x0, y0, (x0, y0, (one, zero, zero, one))))
        for plane in range(planes):
            strength = lens_ref[plane]
            later = []
            for part, h, x0, y0, state in chains:
                tables = [
                    chosen[pl.ds(((plane * together + part) * CHUNKS + c) * SUB, SUB), :]
                    for c in range(CHUNKS)
                ]
                later.append((part, h, x0, y0, trace_step(tables, strength, *state)))
            chains = later
        for part, h, x0, y0, (x, y, entries) in chains:
            base = first + part * SUB
            used = x0 > EMPTY * 0.5
            shift[pl.ds(base * 4 + 2 * h, SUB, stride=4), :] = jnp.where(used, x - x0, 0.0)
            shift[pl.ds(base * 4 + 2 * h + 1, SUB, stride=4), :] = jnp.where(used, y - y0, 0.0)
            for e in range(4):
                matrix[pl.ds(base * 8 + 4 * h + e, SUB, stride=8), :] = jnp.where(used, entries[e], 0.0)
        return carry

    lax.fori_loop(0, slots // (SUB * together), body, 0)
    copies = []
    for c in range(NEAR):
        source = me ^ (f * NEAR + c)
        for kind, (block, out_ref, rows) in enumerate(((shift, shift_ref, 4 * each), (matrix, matrix_ref, 8 * each))):
            copies.append(pltpu.make_async_copy(
                block.at[pl.ds(c * rows, rows), :],
                out_ref.at[pl.ds(source * rows, rows), :],
                sems.at[1 + kind, c]))
    for copy in copies:
        copy.start()
    for copy in copies:
        copy.wait()


def trace(f, each, planes, me, lens_weight, tiles, got, n_sky, outs):
    slots = NEAR * each
    together = min(4, slots // SUB)
    return pl.pallas_call(
        functools.partial(trace_kernel, f, each, planes, together),
        out_shape=(
            jax.ShapeDtypeStruct((n_sky * each * 4, LANES), jnp.float32),
            jax.ShapeDtypeStruct((n_sky * each * 8, LANES), jnp.float32),
        ),
        in_specs=(
            [pl.BlockSpec(memory_space=pltpu.SMEM)] * 2
            + [pl.BlockSpec(memory_space=pltpu.VMEM)] * 2
            + [pl.BlockSpec(memory_space=pl.ANY)] * len(outs)
        ),
        out_specs=(
            pl.BlockSpec(memory_space=pl.ANY),
            pl.BlockSpec(memory_space=pl.ANY),
        ),
        scratch_shapes=[
            pltpu.VMEM((planes * together * CHUNKS * SUB, LANES), jnp.float32),
            pltpu.VMEM((slots * 4, LANES), jnp.float32),
            pltpu.SMEM((NEAR * SUB, LANES), jnp.float32),
            pltpu.VMEM((slots * 4, LANES), jnp.float32),
            pltpu.VMEM((slots * 8, LANES), jnp.float32),
            pltpu.SemaphoreType.DMA((3, NEAR)),
        ],
        input_output_aliases={4 + k: k for k in range(len(outs))},
        compiler_params=pltpu.CompilerParams(vmem_limit_bytes=40 * 1024 * 1024),
        name="trace",
    )(me, lens_weight, tiles, got, *outs)


def flipped(value, n_sky, bits):
    return lax.ppermute(value, "sky", [(i, i ^ bits) for i in range(n_sky)])


def spread(held, n_sky, bits):
    for bit in bits:
        for s in [s for s in held if s & (2 * bit - 1) == 0]:
            if s ^ bit not in held:
                held[s ^ bit] = flipped(held[s], n_sky, bit)


def shards(potential, lens_weight, ray_start, patch_index, destination):
    n_sky = lax.axis_size("sky")
    me = lax.axis_index("sky").reshape(1)
    planes = potential.shape[0]
    bundles, _, rays = ray_start.shape
    each = max(2, 2 * bundles // n_sky)
    slots = n_sky * each
    halves = rays // LANES
    bits = [1 << k for k in reversed(range((n_sky - 1).bit_length()))]
    flat = ray_start.reshape(bundles, 2, halves, LANES).transpose(0, 2, 1, 3).reshape(bundles * 2 * halves, LANES)
    own, sent = prepare(n_sky, each, me, destination.reshape(1, bundles), patch_index, flat, potential)
    sent = [sent[0]] + [flipped(sent[s], n_sky, s) for s in range(1, NEAR)]
    held = {0: own}
    for bit in bits[:2]:
        held[bit] = flipped(own, n_sky, bit)
    held[bits[0] ^ bits[1]] = flipped(held[bits[0]], n_sky, bits[1])
    got = turn(4 * each + SUB, sent)
    early = [0, bits[0], bits[1]]
    *got, a, b, c = lax.optimization_barrier((*got, *[held[s] for s in early]))
    held.update(zip(early, (a, b, c)))
    got = [got[0]] + [flipped(got[f], n_sky, f * NEAR) for f in range(1, len(got))]
    spread(held, n_sky, bits)
    tiles = store([held[s] for s in range(n_sky)])
    outs = ()
    for f in range(len(got)):
        outs = trace(f, each, planes, me, lens_weight, tiles, got[f], n_sky, outs)
    shift, matrix = outs
    shift = shift.reshape(slots, halves, 2, LANES).transpose(0, 2, 1, 3).reshape(slots, 2, rays)
    matrix = matrix.reshape(slots, halves, 4, LANES).transpose(0, 2, 1, 3).reshape(slots, 4, rays)
    return shift, matrix


def solution(mesh):
    in_specs = (
        P("groups", "sky", None),
        P(),
        P(("groups", "sky"), None, None),
        P("groups", "sky"),
        P(("groups", "sky"), None),
    )
    out_specs = (P(("groups", "sky"), None, None), P(("groups", "sky"), None, None))
    return jax.shard_map(shards, mesh=mesh, in_specs=in_specs, out_specs=out_specs, check_vma=False)
```

```python
import functools

import jax
import jax.numpy as jnp
from jax import lax
from jax.experimental import pallas as pl
from jax.experimental.pallas import tpu as pltpu
from jax.sharding import PartitionSpec as P

LANES = 128
SUB = 8
SIDE = 32
CHUNKS = 8
EMPTY = -1024.0
NEAR = 4


def lane_gather(table, idx):
    dims = lax.GatherDimensionNumbers(
        offset_dims=(),
        collapsed_slice_dims=(1,),
        start_index_map=(1,),
        operand_batching_dims=(0,),
        start_indices_batching_dims=(0,),
    )
    return lax.gather(
        table,
        idx[..., None],
        dims,
        slice_sizes=(1, 1),
        mode=lax.GatherScatterMode.PROMISE_IN_BOUNDS,
    )


def split3(value):
    high = value.astype(jnp.bfloat16)
    rest = value - high.astype(jnp.float32)
    middle = rest.astype(jnp.bfloat16)
    low = (rest - middle.astype(jnp.float32)).astype(jnp.bfloat16)
    return high, middle, low


def regroup_kernel(src_ref, dst_ref):
    planes, tiles, _ = src_ref.shape
    lane = lax.broadcasted_iota(jnp.int32, (SUB, LANES), 1)
    source = (lane & 96) + ((lane & 15) << 1) + ((lane >> 4) & 1)
    for plane in range(planes):
        for base in range(0, tiles, SUB):
            parts = [
                lane_gather(src_ref[plane, pl.ds(base, SUB), pl.ds(c * LANES, LANES)], source)
                for c in range(CHUNKS)
            ]
            for step in (1, 2, 4):
                keep = ((lane >> 4) & step) == 0
                for c in range(CHUNKS):
                    if c & step:
                        continue
                    one, two = parts[c], parts[c + step]
                    parts[c] = jnp.where(keep, one, pltpu.roll(two, step * 16, 1))
                    parts[c + step] = jnp.where(keep, pltpu.roll(one, LANES - step * 16, 1), two)
            for c in range(CHUNKS):
                rows = pl.ds((plane * tiles + base) * CHUNKS + c, SUB, stride=CHUNKS)
                dst_ref[rows, :] = parts[c]


def pack_kernel(n_sky, each, per_owner, me_ref, dest_ref, ids_ref, rays_ref, *out_refs):
    me = me_ref[0]
    bundles = dest_ref.shape[1]
    planes = ids_ref.shape[0]
    slots = n_sky * each
    size = 4 * each + SUB
    dest_row = jnp.broadcast_to(dest_ref[...], (bundles, bundles))
    dest_col = jnp.transpose(dest_row)
    row = lax.broadcasted_iota(jnp.int32, (bundles, bundles), 0)
    col = lax.broadcasted_iota(jnp.int32, (bundles, bundles), 1)
    hits = jnp.where((dest_row == dest_col) & (row < col), 1.0, 0.0)
    rank = jnp.sum(hits, axis=0, keepdims=True).astype(jnp.int32)
    slot = (dest_ref[...] ^ me) * each + rank
    place = lax.broadcasted_iota(jnp.int32, (slots, bundles), 0) == slot
    place = jnp.where(place, 1.0, 0.0)
    found = jnp.dot(
        place.astype(jnp.bfloat16),
        jnp.ones((bundles, LANES), jnp.bfloat16),
        preferred_element_type=jnp.float32,
    )
    place3 = jnp.concatenate([place] * 3, axis=1).astype(jnp.bfloat16)
    for part in range(4):
        rays = rays_ref[pl.ds(part, bundles, stride=4), :]
        terms = jnp.concatenate(split3(rays), axis=0)
        sent = jnp.dot(place3, terms, preferred_element_type=jnp.float32)
        if part % 2 == 0:
            sent = jnp.where(found > 0.5, sent, EMPTY)
        for s in range(n_sky):
            rows = pl.ds(s // NEAR * size + part, each, stride=4)
            out_refs[s % NEAR][rows, :] = sent[s * each:(s + 1) * each]
    ids = ids_ref[...]
    plane = lax.broadcasted_iota(jnp.int32, ids.shape, 0)
    owner = (ids // per_owner) ^ dest_ref[...]
    owner = (owner % (n_sky // 2)) * 2 + owner // (n_sky // 2)
    spot = (owner * planes + plane) * per_owner + ids % per_owner
    pad = jnp.zeros((SUB - planes, bundles), jnp.float32)
    fine = jnp.concatenate([(spot & 15).astype(jnp.float32), pad], axis=0)
    coarse = jnp.concatenate([(spot >> 4).astype(jnp.float32), pad], axis=0)
    place = place.astype(jnp.bfloat16)
    contract = (((1,), (1,)), ((), ()))
    fine = lax.dot_general(fine.astype(jnp.bfloat16), place, contract, preferred_element_type=jnp.float32)
    coarse = lax.dot_general(coarse.astype(jnp.bfloat16), place, contract, preferred_element_type=jnp.float32)
    numbers = coarse * 16.0 + fine
    for s in range(n_sky):
        first = s * each
        block = numbers[:, first // LANES * LANES:first // LANES * LANES + LANES]
        turn = (LANES - first % LANES) % LANES
        if turn:
            block = pltpu.roll(block, turn, 1)
        out_refs[s % NEAR][pl.ds(s // NEAR * size + 4 * each, SUB), :] = block


def prepare_kernel(n_sky, each, me_ref, dest_ref, ids_ref, rays_ref, src_ref, dst_ref, *out_refs):
    regroup_kernel(src_ref, dst_ref)
    pack_kernel(n_sky, each, src_ref.shape[1], me_ref, dest_ref, ids_ref, rays_ref, *out_refs)


def prepare(n_sky, each, me, dest, ids, rays, potential):
    planes, tiles, pixels = potential.shape
    part = jax.ShapeDtypeStruct((n_sky // NEAR * (4 * each + SUB), LANES), jnp.float32)
    own = jax.ShapeDtypeStruct((planes * tiles * pixels // LANES, LANES), jnp.float32)
    own, *sent = pl.pallas_call(
        functools.partial(prepare_kernel, n_sky, each),
        out_shape=[own] + [part] * NEAR,
        in_specs=[pl.BlockSpec(memory_space=pltpu.SMEM)] + [pl.BlockSpec(memory_space=pltpu.VMEM)] * 4,
        out_specs=[pl.BlockSpec(memory_space=pltpu.VMEM)] * (1 + NEAR),
        name="prepare",
    )(me, dest, ids, rays, potential)
    return own, sent


def turn_kernel(size, *refs):
    far = len(refs) - NEAR
    for f in range(far):
        for c in range(NEAR):
            refs[NEAR + f][pl.ds(c * size, size), :] = refs[c][pl.ds(f * size, size), :]


def turn(size, parts):
    far = parts[0].shape[0] // size
    block = jax.ShapeDtypeStruct((NEAR * size, LANES), jnp.float32)
    return pl.pallas_call(
        functools.partial(turn_kernel, size),
        out_shape=[block] * far,
        in_specs=[pl.BlockSpec(memory_space=pltpu.VMEM)] * NEAR,
        out_specs=[pl.BlockSpec(memory_space=pltpu.VMEM)] * far,
        name="turn",
    )(*parts)


def bilinear(f00, f01, f10, f11, u, v):
    one = f00 + u * (f01 - f00)
    two = f10 + u * (f11 - f10)
    return one + v * (two - one)


def lerp(one, two, t):
    return one + t * (two - one)


def window(tables, pos_x, pos_y):
    ix = (pos_x + float(SIDE)).astype(jnp.int32)
    iy = (pos_y + float(SIDE)).astype(jnp.int32)
    u = pos_x - (ix.astype(jnp.float32) - float(SIDE))
    v = pos_y - (iy.astype(jnp.float32) - float(SIDE))
    odd = (ix - 1) >> 1
    even = ix >> 1
    columns = (((even & 15), ((even + 1) & 15)), ((odd & 15), ((odd + 1) & 15)))
    odd_first = (ix & 1) == 0
    by_two = ((iy - 1) & 2) != 0
    by_one = (iy & 1) == 0
    sorted_columns = []
    for a in range(4):
        line = ((iy + (2 - a)) & 28) << 2
        e0, e1 = [lane_gather(tables[2 * a], line + c) for c in columns[0]]
        o0, o1 = [lane_gather(tables[2 * a + 1], line + c) for c in columns[1]]
        sorted_columns.append((
            jnp.where(odd_first, o0, e0),
            jnp.where(odd_first, e0, o0),
            jnp.where(odd_first, o1, e1),
            jnp.where(odd_first, e1, o1),
        ))
    w = [[None] * 4 for _ in range(4)]
    for k in range(4):
        half = [jnp.where(by_two, sorted_columns[(r + 2) & 3][k], sorted_columns[r][k]) for r in range(4)]
        for r in range(4):
            w[r][k] = jnp.where(by_one, half[(r + 1) & 3], half[r])
    return w, u, v


def trace_step(tables, strength, pos_x, pos_y, matrix):
    w, u, v = window(tables, pos_x, pos_y)
    gx = [lerp(w[1][k + 1] - w[1][k], w[2][k + 1] - w[2][k], v) for k in range(3)]
    gy = [lerp(w[r + 1][1] - w[r][1], w[r + 1][2] - w[r][2], u) for r in range(3)]
    fx2 = lerp(gx[0] + gx[1], gx[1] + gx[2], u)
    fxx = lerp(gx[1] - gx[0], gx[2] - gx[1], u)
    fy2 = lerp(gy[0] + gy[1], gy[1] + gy[2], v)
    fyy = lerp(gy[1] - gy[0], gy[2] - gy[1], v)
    wide = [[w[r][k + 2] - w[r][k] for k in range(2)] for r in range(4)]
    fxy4 = bilinear(
        wide[2][0] - wide[0][0], wide[2][1] - wide[0][1],
        wide[3][0] - wide[1][0], wide[3][1] - wide[1][1], u, v)
    half = 0.5 * strength
    hxx, hxy, hyy = strength * fxx, (0.25 * strength) * fxy4, strength * fyy
    m11, m12, m21, m22 = matrix
    matrix = (
        m11 - (hxx * m11 + hxy * m21),
        m12 - (hxx * m12 + hxy * m22),
        m21 - (hxy * m11 + hyy * m21),
        m22 - (hxy * m12 + hyy * m22),
    )
    return pos_x - half * fx2, pos_y - half * fy2, matrix


def trace_kernel(n_sky, each, planes, together, me_ref, lens_ref, *refs):
    far = n_sky // NEAR
    pairs = n_sky // 2
    size = 4 * each + SUB
    tile_refs, got_refs = refs[:pairs], refs[pairs:pairs + far]
    shift_ref, matrix_ref, tiles, chosen, rays, places, sems = refs[pairs + far:]
    me = me_ref[0]
    slots = n_sky * each
    rows = tile_refs[0].shape[0]
    copies = [
        pltpu.make_async_copy(tile_ref, tiles.at[pl.ds(k * rows, rows), :], sems.at[0, k])
        for k, tile_ref in enumerate(tile_refs)
    ]
    for s in range(n_sky):
        source = me ^ s
        got_ref, first = got_refs[s // NEAR], s % NEAR * size
        copies.append(pltpu.make_async_copy(
            got_ref.at[pl.ds(first + 4 * each, SUB), :],
            places.at[pl.ds(source * SUB, SUB), :],
            sems.at[1, s]))
        copies.append(pltpu.make_async_copy(
            got_ref.at[pl.ds(first, 4 * each), :],
            rays.at[pl.ds(source * 4 * each, 4 * each), :],
            sems.at[2, s]))
    for copy in copies:
        copy.start()
    for copy in copies:
        copy.wait()

    def body(step, carry):
        chains = []
        first = pl.multiple_of(step * (together * SUB), together * SUB)
        for plane in range(planes):
            for part in range(together):
                for k in range(SUB):
                    slot = first + (part * SUB + k)
                    spot = places[slot // each * SUB + plane, slot % each].astype(jnp.int32)
                    tile = tiles[pl.ds(pl.multiple_of(spot * CHUNKS, CHUNKS), CHUNKS), :]
                    chosen[pl.ds((plane * together + part) * CHUNKS * SUB + k, CHUNKS, stride=SUB), :] = tile
        for part in range(together):
            base = first + part * SUB
            for h in range(2):
                x0 = rays[pl.ds(base * 4 + 2 * h, SUB, stride=4), :]
                y0 = rays[pl.ds(base * 4 + 2 * h + 1, SUB, stride=4), :]
                one = jnp.ones_like(x0)
                zero = jnp.zeros_like(x0)
                chains.append((part, h, x0, y0, (x0, y0, (one, zero, zero, one))))
        for plane in range(planes):
            strength = lens_ref[plane]
            later = []
            for part, h, x0, y0, state in chains:
                tables = [
                    chosen[pl.ds(((plane * together + part) * CHUNKS + c) * SUB, SUB), :]
                    for c in range(CHUNKS)
                ]
                later.append((part, h, x0, y0, trace_step(tables, strength, *state)))
            chains = later
        for part, h, x0, y0, (x, y, matrix) in chains:
            base = first + part * SUB
            used = x0 > EMPTY * 0.5
            shift_ref[pl.ds(base * 4 + 2 * h, SUB, stride=4), :] = jnp.where(used, x - x0, 0.0)
            shift_ref[pl.ds(base * 4 + 2 * h + 1, SUB, stride=4), :] = jnp.where(used, y - y0, 0.0)
            for e in range(4):
                matrix_ref[pl.ds(base * 8 + 4 * h + e, SUB, stride=8), :] = jnp.where(used, matrix[e], 0.0)
        return carry

    lax.fori_loop(0, slots // (SUB * together), body, 0)


def trace(each, planes, me, lens_weight, tiles, got):
    n_sky = 2 * len(tiles)
    slots = n_sky * each
    rows = tiles[0].shape[0]
    together = 4
    return pl.pallas_call(
        functools.partial(trace_kernel, n_sky, each, planes, together),
        out_shape=(
            jax.ShapeDtypeStruct((slots * 4, LANES), jnp.float32),
            jax.ShapeDtypeStruct((slots * 8, LANES), jnp.float32),
        ),
        in_specs=[pl.BlockSpec(memory_space=pltpu.SMEM)] * 2 + [pl.BlockSpec(memory_space=pl.ANY)] * (len(tiles) + len(got)),
        out_specs=(
            pl.BlockSpec(memory_space=pltpu.VMEM),
            pl.BlockSpec(memory_space=pltpu.VMEM),
        ),
        scratch_shapes=[
            pltpu.VMEM((len(tiles) * rows, LANES), jnp.float32),
            pltpu.VMEM((planes * together * CHUNKS * SUB, LANES), jnp.float32),
            pltpu.VMEM((slots * 4, LANES), jnp.float32),
            pltpu.SMEM((n_sky * SUB, LANES), jnp.float32),
            pltpu.SemaphoreType.DMA((3, n_sky)),
        ],
        compiler_params=pltpu.CompilerParams(vmem_limit_bytes=40 * 1024 * 1024),
        name="trace",
    )(me, lens_weight, *tiles, *got)


def flipped(value, n_sky, bits):
    return lax.ppermute(value, "sky", [(i, i ^ bits) for i in range(n_sky)])


def shards(potential, lens_weight, ray_start, patch_index, destination):
    n_sky = lax.axis_size("sky")
    me = lax.axis_index("sky").reshape(1)
    planes = potential.shape[0]
    bundles, _, rays = ray_start.shape
    each = max(2, 2 * bundles // n_sky)
    slots = n_sky * each
    halves = rays // LANES
    bits = [1 << k for k in reversed(range((n_sky - 1).bit_length()))]
    flat = ray_start.reshape(bundles, 2, halves, LANES).transpose(0, 2, 1, 3).reshape(bundles * 2 * halves, LANES)
    own, sent = prepare(n_sky, each, me, destination.reshape(1, bundles), patch_index, flat, potential)
    sent = [sent[0]] + [flipped(sent[s], n_sky, s) for s in range(1, NEAR)]
    across = flipped(own, n_sky, bits[0])
    across, *sent = lax.optimization_barrier((across, *sent))
    pair = jnp.concatenate([own, across], axis=0)
    got = list(turn(4 * each + SUB, sent))
    held = {0: pair, bits[1]: flipped(pair, n_sky, bits[1])}
    got[0], held[bits[1]] = lax.optimization_barrier((got[0], held[bits[1]]))
    for bit in bits[2:-1]:
        for s in list(held):
            held[s ^ bit] = flipped(held[s], n_sky, bit)
    got = [got[0]] + [flipped(got[f], n_sky, f * NEAR) for f in range(1, len(got))]
    half = len(got) // 2
    keys = sorted(held)
    for mids, some in ((list(range(1, half + 1)), keys[:len(keys) // 2]), (list(range(half + 1, len(got))), keys[len(keys) // 2:])):
        tied = lax.optimization_barrier([got[mid] for mid in mids] + [held[s] for s in some])
        for mid in mids:
            got[mid] = tied.pop(0)
        held.update(zip(some, tied))
    for s in keys:
        held[s ^ 1] = flipped(held[s], n_sky, 1)
    shift, matrix = trace(each, planes, me, lens_weight, [held[s] for s in range(n_sky // 2)], got)
    shift = shift.reshape(slots, halves, 2, LANES).transpose(0, 2, 1, 3).reshape(slots, 2, rays)
    matrix = matrix.reshape(slots, halves, 4, LANES).transpose(0, 2, 1, 3).reshape(slots, 4, rays)
    return shift, matrix


def solution(mesh):
    in_specs = (
        P("groups", "sky", None),
        P(),
        P(("groups", "sky"), None, None),
        P("groups", "sky"),
        P(("groups", "sky"), None),
    )
    out_specs = (P(("groups", "sky"), None, None), P(("groups", "sky"), None, None))
    return jax.shard_map(shards, mesh=mesh, in_specs=in_specs, out_specs=out_specs, check_vma=False)
```

```python
import functools

import jax
import jax.numpy as jnp
from jax import lax
from jax.experimental import pallas as pl
from jax.experimental.pallas import tpu as pltpu
from jax.sharding import PartitionSpec as P

LANES = 128
SUB = 8
SIDE = 32
CHUNKS = 8
EMPTY = -1024.0
NEAR = 4


def lane_gather(table, idx):
    dims = lax.GatherDimensionNumbers(
        offset_dims=(),
        collapsed_slice_dims=(1,),
        start_index_map=(1,),
        operand_batching_dims=(0,),
        start_indices_batching_dims=(0,),
    )
    return lax.gather(
        table,
        idx[..., None],
        dims,
        slice_sizes=(1, 1),
        mode=lax.GatherScatterMode.PROMISE_IN_BOUNDS,
    )


def split3(value):
    high = value.astype(jnp.bfloat16)
    rest = value - high.astype(jnp.float32)
    middle = rest.astype(jnp.bfloat16)
    low = (rest - middle.astype(jnp.float32)).astype(jnp.bfloat16)
    return high, middle, low


def regroup_kernel(src_ref, dst_ref):
    planes, tiles, _ = src_ref.shape
    lane = lax.broadcasted_iota(jnp.int32, (SUB, LANES), 1)
    source = (lane & 96) + ((lane & 15) << 1) + ((lane >> 4) & 1)
    for plane in range(planes):
        for base in range(0, tiles, SUB):
            parts = [
                lane_gather(src_ref[plane, pl.ds(base, SUB), pl.ds(c * LANES, LANES)], source)
                for c in range(CHUNKS)
            ]
            for step in (1, 2, 4):
                keep = ((lane >> 4) & step) == 0
                for c in range(CHUNKS):
                    if c & step:
                        continue
                    one, two = parts[c], parts[c + step]
                    parts[c] = jnp.where(keep, one, pltpu.roll(two, step * 16, 1))
                    parts[c + step] = jnp.where(keep, pltpu.roll(one, LANES - step * 16, 1), two)
            for c in range(CHUNKS):
                rows = pl.ds((plane * tiles + base) * CHUNKS + c, SUB, stride=CHUNKS)
                dst_ref[rows, :] = parts[c]


def pack_kernel(n_sky, each, per_owner, me_ref, dest_ref, ids_ref, rays_ref, *out_refs):
    me = me_ref[0]
    bundles = dest_ref.shape[1]
    planes = ids_ref.shape[0]
    slots = n_sky * each
    size = 4 * each + SUB
    dest_row = jnp.broadcast_to(dest_ref[...], (bundles, bundles))
    dest_col = jnp.transpose(dest_row)
    row = lax.broadcasted_iota(jnp.int32, (bundles, bundles), 0)
    col = lax.broadcasted_iota(jnp.int32, (bundles, bundles), 1)
    hits = jnp.where((dest_row == dest_col) & (row < col), 1.0, 0.0)
    rank = jnp.sum(hits, axis=0, keepdims=True).astype(jnp.int32)
    slot = (dest_ref[...] ^ me) * each + rank
    place = lax.broadcasted_iota(jnp.int32, (slots, bundles), 0) == slot
    place = jnp.where(place, 1.0, 0.0)
    found = jnp.dot(
        place.astype(jnp.bfloat16),
        jnp.ones((bundles, LANES), jnp.bfloat16),
        preferred_element_type=jnp.float32,
    )
    place3 = jnp.concatenate([place] * 3, axis=1).astype(jnp.bfloat16)
    for part in range(4):
        rays = rays_ref[pl.ds(part, bundles, stride=4), :]
        terms = jnp.concatenate(split3(rays), axis=0)
        sent = jnp.dot(place3, terms, preferred_element_type=jnp.float32)
        if part % 2 == 0:
            sent = jnp.where(found > 0.5, sent, EMPTY)
        for s in range(n_sky):
            rows = pl.ds(s % NEAR * size + part, each, stride=4)
            out_refs[s // NEAR][rows, :] = sent[s * each:(s + 1) * each]
    ids = ids_ref[...]
    plane = lax.broadcasted_iota(jnp.int32, ids.shape, 0)
    owner = (ids // per_owner) ^ dest_ref[...]
    owner = (owner % (n_sky // 2)) * 2 + owner // (n_sky // 2)
    spot = (owner * planes + plane) * per_owner + ids % per_owner
    pad = jnp.zeros((SUB - planes, bundles), jnp.float32)
    fine = jnp.concatenate([(spot & 15).astype(jnp.float32), pad], axis=0)
    coarse = jnp.concatenate([(spot >> 4).astype(jnp.float32), pad], axis=0)
    place = place.astype(jnp.bfloat16)
    contract = (((1,), (1,)), ((), ()))
    fine = lax.dot_general(fine.astype(jnp.bfloat16), place, contract, preferred_element_type=jnp.float32)
    coarse = lax.dot_general(coarse.astype(jnp.bfloat16), place, contract, preferred_element_type=jnp.float32)
    numbers = coarse * 16.0 + fine
    for s in range(n_sky):
        first = s * each
        block = numbers[:, first // LANES * LANES:first // LANES * LANES + LANES]
        turn = (LANES - first % LANES) % LANES
        if turn:
            block = pltpu.roll(block, turn, 1)
        out_refs[s // NEAR][pl.ds(s % NEAR * size + 4 * each, SUB), :] = block


def prepare_kernel(n_sky, each, me_ref, dest_ref, ids_ref, rays_ref, src_ref, dst_ref, *out_refs):
    regroup_kernel(src_ref, dst_ref)
    pack_kernel(n_sky, each, src_ref.shape[1], me_ref, dest_ref, ids_ref, rays_ref, *out_refs)


def prepare(n_sky, each, me, dest, ids, rays, potential):
    planes, tiles, pixels = potential.shape
    far = n_sky // NEAR
    part = jax.ShapeDtypeStruct((NEAR * (4 * each + SUB), LANES), jnp.float32)
    own = jax.ShapeDtypeStruct((planes * tiles * pixels // LANES, LANES), jnp.float32)
    own, *sent = pl.pallas_call(
        functools.partial(prepare_kernel, n_sky, each),
        out_shape=[own] + [part] * far,
        in_specs=[pl.BlockSpec(memory_space=pltpu.SMEM)] + [pl.BlockSpec(memory_space=pltpu.VMEM)] * 4,
        out_specs=[pl.BlockSpec(memory_space=pltpu.VMEM)] * (1 + far),
        name="prepare",
    )(me, dest, ids, rays, potential)
    return own, sent


def turn_kernel(size, *refs):
    *refs, sems = refs
    far = len(refs) - NEAR
    copies = [
        pltpu.make_async_copy(
            refs[f].at[pl.ds(c * size, size), :],
            refs[far + c].at[pl.ds(f * size, size), :],
            sems.at[f, c])
        for f in range(far)
        for c in range(NEAR)
    ]
    for copy in copies:
        copy.start()
    for copy in copies:
        copy.wait()


def turn(size, parts):
    far = len(parts)
    block = jax.ShapeDtypeStruct((far * size, LANES), jnp.float32)
    return pl.pallas_call(
        functools.partial(turn_kernel, size),
        out_shape=[block] * NEAR,
        in_specs=[pl.BlockSpec(memory_space=pl.ANY)] * far,
        out_specs=[pl.BlockSpec(memory_space=pltpu.VMEM)] * NEAR,
        scratch_shapes=[pltpu.SemaphoreType.DMA((far, NEAR))],
        name="turn",
    )(*parts)


def bilinear(f00, f01, f10, f11, u, v):
    one = f00 + u * (f01 - f00)
    two = f10 + u * (f11 - f10)
    return one + v * (two - one)


def lerp(one, two, t):
    return one + t * (two - one)


def window(tables, pos_x, pos_y):
    ix = (pos_x + float(SIDE)).astype(jnp.int32)
    iy = (pos_y + float(SIDE)).astype(jnp.int32)
    u = pos_x - (ix.astype(jnp.float32) - float(SIDE))
    v = pos_y - (iy.astype(jnp.float32) - float(SIDE))
    odd = (ix - 1) >> 1
    even = ix >> 1
    columns = (((even & 15), ((even + 1) & 15)), ((odd & 15), ((odd + 1) & 15)))
    odd_first = (ix & 1) == 0
    by_two = ((iy - 1) & 2) != 0
    by_one = (iy & 1) == 0
    sorted_columns = []
    for a in range(4):
        line = ((iy + (2 - a)) & 28) << 2
        e0, e1 = [lane_gather(tables[2 * a], line + c) for c in columns[0]]
        o0, o1 = [lane_gather(tables[2 * a + 1], line + c) for c in columns[1]]
        sorted_columns.append((
            jnp.where(odd_first, o0, e0),
            jnp.where(odd_first, e0, o0),
            jnp.where(odd_first, o1, e1),
            jnp.where(odd_first, e1, o1),
        ))
    w = [[None] * 4 for _ in range(4)]
    for k in range(4):
        half = [jnp.where(by_two, sorted_columns[(r + 2) & 3][k], sorted_columns[r][k]) for r in range(4)]
        for r in range(4):
            w[r][k] = jnp.where(by_one, half[(r + 1) & 3], half[r])
    return w, u, v


def trace_step(tables, strength, pos_x, pos_y, matrix):
    w, u, v = window(tables, pos_x, pos_y)
    gx = [lerp(w[1][k + 1] - w[1][k], w[2][k + 1] - w[2][k], v) for k in range(3)]
    gy = [lerp(w[r + 1][1] - w[r][1], w[r + 1][2] - w[r][2], u) for r in range(3)]
    fx2 = lerp(gx[0] + gx[1], gx[1] + gx[2], u)
    fxx = lerp(gx[1] - gx[0], gx[2] - gx[1], u)
    fy2 = lerp(gy[0] + gy[1], gy[1] + gy[2], v)
    fyy = lerp(gy[1] - gy[0], gy[2] - gy[1], v)
    wide = [[w[r][k + 2] - w[r][k] for k in range(2)] for r in range(4)]
    fxy4 = bilinear(
        wide[2][0] - wide[0][0], wide[2][1] - wide[0][1],
        wide[3][0] - wide[1][0], wide[3][1] - wide[1][1], u, v)
    half = 0.5 * strength
    hxx, hxy, hyy = strength * fxx, (0.25 * strength) * fxy4, strength * fyy
    m11, m12, m21, m22 = matrix
    matrix = (
        m11 - (hxx * m11 + hxy * m21),
        m12 - (hxx * m12 + hxy * m22),
        m21 - (hxy * m11 + hyy * m21),
        m22 - (hxy * m12 + hyy * m22),
    )
    return pos_x - half * fx2, pos_y - half * fy2, matrix


def trace_kernel(n_sky, each, planes, together, me_ref, lens_ref, *refs):
    pairs = n_sky // 2
    size = 4 * each + SUB
    tile_refs, got_refs = refs[:pairs], refs[pairs:pairs + NEAR]
    shift_ref, matrix_ref, tiles, chosen, rays, places, sems = refs[pairs + NEAR:]
    me = me_ref[0]
    slots = n_sky * each
    rows = tile_refs[0].shape[0]
    copies = [
        pltpu.make_async_copy(tile_ref, tiles.at[pl.ds(k * rows, rows), :], sems.at[0, k])
        for k, tile_ref in enumerate(tile_refs)
    ]
    for s in range(n_sky):
        source = me ^ s
        got_ref, first = got_refs[s % NEAR], s // NEAR * size
        copies.append(pltpu.make_async_copy(
            got_ref.at[pl.ds(first + 4 * each, SUB), :],
            places.at[pl.ds(source * SUB, SUB), :],
            sems.at[1, s]))
        copies.append(pltpu.make_async_copy(
            got_ref.at[pl.ds(first, 4 * each), :],
            rays.at[pl.ds(source * 4 * each, 4 * each), :],
            sems.at[2, s]))
    for copy in copies:
        copy.start()
    for copy in copies:
        copy.wait()

    def body(step, carry):
        chains = []
        first = pl.multiple_of(step * (together * SUB), together * SUB)
        for plane in range(planes):
            for part in range(together):
                for k in range(SUB):
                    slot = first + (part * SUB + k)
                    spot = places[slot // each * SUB + plane, slot % each].astype(jnp.int32)
                    tile = tiles[pl.ds(pl.multiple_of(spot * CHUNKS, CHUNKS), CHUNKS), :]
                    chosen[pl.ds((plane * together + part) * CHUNKS * SUB + k, CHUNKS, stride=SUB), :] = tile
        for part in range(together):
            base = first + part * SUB
            for h in range(2):
                x0 = rays[pl.ds(base * 4 + 2 * h, SUB, stride=4), :]
                y0 = rays[pl.ds(base * 4 + 2 * h + 1, SUB, stride=4), :]
                one = jnp.ones_like(x0)
                zero = jnp.zeros_like(x0)
                chains.append((part, h, x0, y0, (x0, y0, (one, zero, zero, one))))
        for plane in range(planes):
            strength = lens_ref[plane]
            later = []
            for part, h, x0, y0, state in chains:
                tables = [
                    chosen[pl.ds(((plane * together + part) * CHUNKS + c) * SUB, SUB), :]
                    for c in range(CHUNKS)
                ]
                later.append((part, h, x0, y0, trace_step(tables, strength, *state)))
            chains = later
        for part, h, x0, y0, (x, y, matrix) in chains:
            base = first + part * SUB
            used = x0 > EMPTY * 0.5
            shift_ref[pl.ds(base * 4 + 2 * h, SUB, stride=4), :] = jnp.where(used, x - x0, 0.0)
            shift_ref[pl.ds(base * 4 + 2 * h + 1, SUB, stride=4), :] = jnp.where(used, y - y0, 0.0)
            for e in range(4):
                matrix_ref[pl.ds(base * 8 + 4 * h + e, SUB, stride=8), :] = jnp.where(used, matrix[e], 0.0)
        return carry

    lax.fori_loop(0, slots // (SUB * together), body, 0)


def trace(each, planes, me, lens_weight, tiles, got):
    n_sky = 2 * len(tiles)
    slots = n_sky * each
    rows = tiles[0].shape[0]
    together = 4
    return pl.pallas_call(
        functools.partial(trace_kernel, n_sky, each, planes, together),
        out_shape=(
            jax.ShapeDtypeStruct((slots * 4, LANES), jnp.float32),
            jax.ShapeDtypeStruct((slots * 8, LANES), jnp.float32),
        ),
        in_specs=[pl.BlockSpec(memory_space=pltpu.SMEM)] * 2 + [pl.BlockSpec(memory_space=pl.ANY)] * (len(tiles) + len(got)),
        out_specs=(
            pl.BlockSpec(memory_space=pltpu.VMEM),
            pl.BlockSpec(memory_space=pltpu.VMEM),
        ),
        scratch_shapes=[
            pltpu.VMEM((len(tiles) * rows, LANES), jnp.float32),
            pltpu.VMEM((planes * together * CHUNKS * SUB, LANES), jnp.float32),
            pltpu.VMEM((slots * 4, LANES), jnp.float32),
            pltpu.SMEM((n_sky * SUB, LANES), jnp.float32),
            pltpu.SemaphoreType.DMA((3, n_sky)),
        ],
        compiler_params=pltpu.CompilerParams(vmem_limit_bytes=40 * 1024 * 1024),
        name="trace",
    )(me, lens_weight, *tiles, *got)


def flipped(value, n_sky, bits):
    return lax.ppermute(value, "sky", [(i, i ^ bits) for i in range(n_sky)])


def shards(potential, lens_weight, ray_start, patch_index, destination):
    n_sky = lax.axis_size("sky")
    me = lax.axis_index("sky").reshape(1)
    planes = potential.shape[0]
    bundles, _, rays = ray_start.shape
    each = max(2, 2 * bundles // n_sky)
    slots = n_sky * each
    halves = rays // LANES
    bits = [1 << k for k in reversed(range((n_sky - 1).bit_length()))]
    flat = ray_start.reshape(bundles, 2, halves, LANES).transpose(0, 2, 1, 3).reshape(bundles * 2 * halves, LANES)
    own, sent = prepare(n_sky, each, me, destination.reshape(1, bundles), patch_index, flat, potential)
    across = flipped(own, n_sky, bits[0])
    sent = [sent[0]] + [flipped(sent[f], n_sky, f * NEAR) for f in range(1, len(sent))]
    held = {0: jnp.concatenate([own, across], axis=0)}
    for bit in bits[1:-1]:
        for s in list(held):
            held[s ^ bit] = flipped(held[s], n_sky, bit)
    got = turn(4 * each + SUB, sent)
    got = [got[0]] + [flipped(got[c], n_sky, c) for c in range(1, NEAR)]
    keys = sorted(held)
    half = len(keys) // 2
    for c, some in ((2, keys[:half]), (3, keys[half:])):
        got[c], *tied = lax.optimization_barrier((got[c], *[held[s] for s in some]))
        for s, value in zip(some, tied):
            held[s], held[s ^ 1] = value, flipped(value, n_sky, 1)
    shift, matrix = trace(each, planes, me, lens_weight, [held[s] for s in range(n_sky // 2)], got)
    shift = shift.reshape(slots, halves, 2, LANES).transpose(0, 2, 1, 3).reshape(slots, 2, rays)
    matrix = matrix.reshape(slots, halves, 4, LANES).transpose(0, 2, 1, 3).reshape(slots, 4, rays)
    return shift, matrix


def solution(mesh):
    in_specs = (
        P("groups", "sky", None),
        P(),
        P(("groups", "sky"), None, None),
        P("groups", "sky"),
        P(("groups", "sky"), None),
    )
    out_specs = (P(("groups", "sky"), None, None), P(("groups", "sky"), None, None))
    return jax.shard_map(shards, mesh=mesh, in_specs=in_specs, out_specs=out_specs, check_vma=False)
```

```python
import functools

import jax
import jax.numpy as jnp
from jax import lax
from jax.experimental import pallas as pl
from jax.experimental.pallas import tpu as pltpu
from jax.sharding import PartitionSpec as P

LANES = 128
SUB = 8
SIDE = 32
CHUNKS = 8
EMPTY = -1024.0
NEAR = 4


def lane_gather(table, idx):
    dims = lax.GatherDimensionNumbers(
        offset_dims=(),
        collapsed_slice_dims=(1,),
        start_index_map=(1,),
        operand_batching_dims=(0,),
        start_indices_batching_dims=(0,),
    )
    return lax.gather(
        table,
        idx[..., None],
        dims,
        slice_sizes=(1, 1),
        mode=lax.GatherScatterMode.PROMISE_IN_BOUNDS,
    )


def split3(value):
    high = value.astype(jnp.bfloat16)
    rest = value - high.astype(jnp.float32)
    middle = rest.astype(jnp.bfloat16)
    low = (rest - middle.astype(jnp.float32)).astype(jnp.bfloat16)
    return high, middle, low


def regroup_kernel(src_ref, dst_ref):
    planes, tiles, _ = src_ref.shape
    lane = lax.broadcasted_iota(jnp.int32, (SUB, LANES), 1)
    source = (lane & 96) + ((lane & 15) << 1) + ((lane >> 4) & 1)
    for plane in range(planes):
        for base in range(0, tiles, SUB):
            parts = [
                lane_gather(src_ref[plane, pl.ds(base, SUB), pl.ds(c * LANES, LANES)], source)
                for c in range(CHUNKS)
            ]
            for step in (1, 2, 4):
                keep = ((lane >> 4) & step) == 0
                for c in range(CHUNKS):
                    if c & step:
                        continue
                    one, two = parts[c], parts[c + step]
                    parts[c] = jnp.where(keep, one, pltpu.roll(two, step * 16, 1))
                    parts[c + step] = jnp.where(keep, pltpu.roll(one, LANES - step * 16, 1), two)
            for c in range(CHUNKS):
                rows = pl.ds((plane * tiles + base) * CHUNKS + c, SUB, stride=CHUNKS)
                dst_ref[rows, :] = parts[c]


def pack_kernel(n_sky, each, per_owner, me_ref, dest_ref, ids_ref, rays_ref, *out_refs):
    me = me_ref[0]
    bundles = dest_ref.shape[1]
    planes = ids_ref.shape[0]
    slots = n_sky * each
    size = 4 * each + SUB
    dest_row = jnp.broadcast_to(dest_ref[...], (bundles, bundles))
    dest_col = jnp.transpose(dest_row)
    row = lax.broadcasted_iota(jnp.int32, (bundles, bundles), 0)
    col = lax.broadcasted_iota(jnp.int32, (bundles, bundles), 1)
    hits = jnp.where((dest_row == dest_col) & (row < col), 1.0, 0.0)
    rank = jnp.sum(hits, axis=0, keepdims=True).astype(jnp.int32)
    slot = (dest_ref[...] ^ me) * each + rank
    place = lax.broadcasted_iota(jnp.int32, (slots, bundles), 0) == slot
    place = jnp.where(place, 1.0, 0.0)
    found = jnp.dot(
        place.astype(jnp.bfloat16),
        jnp.ones((bundles, LANES), jnp.bfloat16),
        preferred_element_type=jnp.float32,
    )
    place3 = jnp.concatenate([place] * 3, axis=1).astype(jnp.bfloat16)
    for part in range(4):
        rays = rays_ref[pl.ds(part, bundles, stride=4), :]
        terms = jnp.concatenate(split3(rays), axis=0)
        sent = jnp.dot(place3, terms, preferred_element_type=jnp.float32)
        if part % 2 == 0:
            sent = jnp.where(found > 0.5, sent, EMPTY)
        for s in range(n_sky):
            rows = pl.ds(s // NEAR * size + part, each, stride=4)
            out_refs[s % NEAR][rows, :] = sent[s * each:(s + 1) * each]
    ids = ids_ref[...]
    plane = lax.broadcasted_iota(jnp.int32, ids.shape, 0)
    owner = (ids // per_owner) ^ dest_ref[...]
    spot = (owner * planes + plane) * per_owner + ids % per_owner
    pad = jnp.zeros((SUB - planes, bundles), jnp.float32)
    fine = jnp.concatenate([(spot & 15).astype(jnp.float32), pad], axis=0)
    coarse = jnp.concatenate([(spot >> 4).astype(jnp.float32), pad], axis=0)
    place = place.astype(jnp.bfloat16)
    contract = (((1,), (1,)), ((), ()))
    fine = lax.dot_general(fine.astype(jnp.bfloat16), place, contract, preferred_element_type=jnp.float32)
    coarse = lax.dot_general(coarse.astype(jnp.bfloat16), place, contract, preferred_element_type=jnp.float32)
    numbers = coarse * 16.0 + fine
    for s in range(n_sky):
        first = s * each
        block = numbers[:, first // LANES * LANES:first // LANES * LANES + LANES]
        turn = (LANES - first % LANES) % LANES
        if turn:
            block = pltpu.roll(block, turn, 1)
        out_refs[s % NEAR][pl.ds(s // NEAR * size + 4 * each, SUB), :] = block


def prepare_kernel(n_sky, each, me_ref, dest_ref, ids_ref, rays_ref, src_ref, dst_ref, *out_refs):
    regroup_kernel(src_ref, dst_ref)
    pack_kernel(n_sky, each, src_ref.shape[1], me_ref, dest_ref, ids_ref, rays_ref, *out_refs)


def prepare(n_sky, each, me, dest, ids, rays, potential):
    planes, tiles, pixels = potential.shape
    part = jax.ShapeDtypeStruct((n_sky // NEAR * (4 * each + SUB), LANES), jnp.float32)
    own = jax.ShapeDtypeStruct((planes * tiles * pixels // LANES, LANES), jnp.float32)
    own, *sent = pl.pallas_call(
        functools.partial(prepare_kernel, n_sky, each),
        out_shape=[own] + [part] * NEAR,
        in_specs=[pl.BlockSpec(memory_space=pltpu.SMEM)] + [pl.BlockSpec(memory_space=pltpu.VMEM)] * 4,
        out_specs=[pl.BlockSpec(memory_space=pltpu.VMEM)] * (1 + NEAR),
        compiler_params=pltpu.CompilerParams(vmem_limit_bytes=16 * 1024 * 1024),
        name="prepare",
    )(me, dest, ids, rays, potential)
    return own, sent


def turn_kernel(size, *refs):
    far = len(refs) - NEAR
    for f in range(far):
        for c in range(NEAR):
            refs[NEAR + f][pl.ds(c * size, size), :] = refs[c][pl.ds(f * size, size), :]


def turn(size, parts):
    far = parts[0].shape[0] // size
    block = jax.ShapeDtypeStruct((NEAR * size, LANES), jnp.float32)
    return pl.pallas_call(
        functools.partial(turn_kernel, size),
        out_shape=[block] * far,
        in_specs=[pl.BlockSpec(memory_space=pltpu.VMEM)] * NEAR,
        out_specs=[pl.BlockSpec(memory_space=pltpu.VMEM)] * far,
        compiler_params=pltpu.CompilerParams(vmem_limit_bytes=4 * 1024 * 1024),
        name="turn",
    )(*parts)


def bilinear(f00, f01, f10, f11, u, v):
    one = f00 + u * (f01 - f00)
    two = f10 + u * (f11 - f10)
    return one + v * (two - one)


def lerp(one, two, t):
    return one + t * (two - one)


def window(tables, pos_x, pos_y):
    ix = (pos_x + float(SIDE)).astype(jnp.int32)
    iy = (pos_y + float(SIDE)).astype(jnp.int32)
    u = pos_x - (ix.astype(jnp.float32) - float(SIDE))
    v = pos_y - (iy.astype(jnp.float32) - float(SIDE))
    odd = (ix - 1) >> 1
    even = ix >> 1
    columns = (((even & 15), ((even + 1) & 15)), ((odd & 15), ((odd + 1) & 15)))
    odd_first = (ix & 1) == 0
    by_two = ((iy - 1) & 2) != 0
    by_one = (iy & 1) == 0
    sorted_columns = []
    for a in range(4):
        line = ((iy + (2 - a)) & 28) << 2
        e0, e1 = [lane_gather(tables[2 * a], line + c) for c in columns[0]]
        o0, o1 = [lane_gather(tables[2 * a + 1], line + c) for c in columns[1]]
        sorted_columns.append((
            jnp.where(odd_first, o0, e0),
            jnp.where(odd_first, e0, o0),
            jnp.where(odd_first, o1, e1),
            jnp.where(odd_first, e1, o1),
        ))
    w = [[None] * 4 for _ in range(4)]
    for k in range(4):
        half = [jnp.where(by_two, sorted_columns[(r + 2) & 3][k], sorted_columns[r][k]) for r in range(4)]
        for r in range(4):
            w[r][k] = jnp.where(by_one, half[(r + 1) & 3], half[r])
    return w, u, v


def trace_step(tables, strength, pos_x, pos_y, matrix):
    w, u, v = window(tables, pos_x, pos_y)
    gx = [lerp(w[1][k + 1] - w[1][k], w[2][k + 1] - w[2][k], v) for k in range(3)]
    gy = [lerp(w[r + 1][1] - w[r][1], w[r + 1][2] - w[r][2], u) for r in range(3)]
    fx2 = lerp(gx[0] + gx[1], gx[1] + gx[2], u)
    fxx = lerp(gx[1] - gx[0], gx[2] - gx[1], u)
    fy2 = lerp(gy[0] + gy[1], gy[1] + gy[2], v)
    fyy = lerp(gy[1] - gy[0], gy[2] - gy[1], v)
    wide = [[w[r][k + 2] - w[r][k] for k in range(2)] for r in range(4)]
    fxy4 = bilinear(
        wide[2][0] - wide[0][0], wide[2][1] - wide[0][1],
        wide[3][0] - wide[1][0], wide[3][1] - wide[1][1], u, v)
    half = 0.5 * strength
    hxx, hxy, hyy = strength * fxx, (0.25 * strength) * fxy4, strength * fyy
    m11, m12, m21, m22 = matrix
    matrix = (
        m11 - (hxx * m11 + hxy * m21),
        m12 - (hxx * m12 + hxy * m22),
        m21 - (hxy * m11 + hyy * m21),
        m22 - (hxy * m12 + hyy * m22),
    )
    return pos_x - half * fx2, pos_y - half * fy2, matrix


def trace_kernel(n_sky, each, planes, together, me_ref, lens_ref, *refs):
    far = n_sky // NEAR
    size = 4 * each + SUB
    tile_refs, got_refs = refs[:n_sky], refs[n_sky:n_sky + far]
    shift_ref, matrix_ref, tiles, chosen, rays, places, sems = refs[n_sky + far:]
    me = me_ref[0]
    slots = n_sky * each
    rows = tile_refs[0].shape[0]
    copies = []
    for s in range(n_sky):
        source = me ^ s
        got_ref, first = got_refs[s // NEAR], s % NEAR * size
        copies.append((
            pltpu.make_async_copy(
                got_ref.at[pl.ds(first + 4 * each, SUB), :],
                places.at[pl.ds(source * SUB, SUB), :],
                sems.at[0, s]),
            pltpu.make_async_copy(tile_refs[s], tiles.at[pl.ds(s * rows, rows), :], sems.at[1, s]),
            pltpu.make_async_copy(
                got_ref.at[pl.ds(first, 4 * each), :],
                rays.at[pl.ds(source * 4 * each, 4 * each), :],
                sems.at[2, s]),
        ))
    for kind in (1, 0, 2):
        for s in range(n_sky):
            copies[s][kind].start()
    for kind in (0, 2, 1):
        for s in range(n_sky):
            copies[s][kind].wait()

    def body(step, carry):
        chains = []
        first = pl.multiple_of(step * (together * SUB), together * SUB)
        for plane in range(planes):
            for part in range(together):
                for k in range(SUB):
                    slot = first + (part * SUB + k)
                    spot = places[slot // each * SUB + plane, slot % each].astype(jnp.int32)
                    tile = tiles[pl.ds(pl.multiple_of(spot * CHUNKS, CHUNKS), CHUNKS), :]
                    chosen[pl.ds((plane * together + part) * CHUNKS * SUB + k, CHUNKS, stride=SUB), :] = tile
        for part in range(together):
            base = first + part * SUB
            for h in range(2):
                x0 = rays[pl.ds(base * 4 + 2 * h, SUB, stride=4), :]
                y0 = rays[pl.ds(base * 4 + 2 * h + 1, SUB, stride=4), :]
                one = jnp.ones_like(x0)
                zero = jnp.zeros_like(x0)
                chains.append((part, h, x0, y0, (x0, y0, (one, zero, zero, one))))
        for plane in range(planes):
            strength = lens_ref[plane]
            later = []
            for part, h, x0, y0, state in chains:
                tables = [
                    chosen[pl.ds(((plane * together + part) * CHUNKS + c) * SUB, SUB), :]
                    for c in range(CHUNKS)
                ]
                later.append((part, h, x0, y0, trace_step(tables, strength, *state)))
            chains = later
        for part, h, x0, y0, (x, y, matrix) in chains:
            base = first + part * SUB
            used = x0 > EMPTY * 0.5
            shift_ref[pl.ds(base * 4 + 2 * h, SUB, stride=4), :] = jnp.where(used, x - x0, 0.0)
            shift_ref[pl.ds(base * 4 + 2 * h + 1, SUB, stride=4), :] = jnp.where(used, y - y0, 0.0)
            for e in range(4):
                matrix_ref[pl.ds(base * 8 + 4 * h + e, SUB, stride=8), :] = jnp.where(used, matrix[e], 0.0)
        return carry

    lax.fori_loop(0, slots // (SUB * together), body, 0)


def trace(each, planes, me, lens_weight, tiles, got):
    n_sky = len(tiles)
    slots = n_sky * each
    rows = tiles[0].shape[0]
    together = 4
    return pl.pallas_call(
        functools.partial(trace_kernel, n_sky, each, planes, together),
        out_shape=(
            jax.ShapeDtypeStruct((slots * 4, LANES), jnp.float32),
            jax.ShapeDtypeStruct((slots * 8, LANES), jnp.float32),
        ),
        in_specs=[pl.BlockSpec(memory_space=pltpu.SMEM)] * 2 + [pl.BlockSpec(memory_space=pl.ANY)] * (n_sky + len(got)),
        out_specs=(
            pl.BlockSpec(memory_space=pltpu.VMEM),
            pl.BlockSpec(memory_space=pltpu.VMEM),
        ),
        scratch_shapes=[
            pltpu.VMEM((n_sky * rows, LANES), jnp.float32),
            pltpu.VMEM((planes * together * CHUNKS * SUB, LANES), jnp.float32),
            pltpu.VMEM((slots * 4, LANES), jnp.float32),
            pltpu.SMEM((n_sky * SUB, LANES), jnp.float32),
            pltpu.SemaphoreType.DMA((3, n_sky)),
        ],
        compiler_params=pltpu.CompilerParams(vmem_limit_bytes=20 * 1024 * 1024),
        name="trace",
    )(me, lens_weight, *tiles, *got)


def flipped(value, n_sky, bits):
    return lax.ppermute(value, "sky", [(i, i ^ bits) for i in range(n_sky)])


def spread(held, n_sky, bits):
    for bit in bits:
        for s in [s for s in held if s & (2 * bit - 1) == 0]:
            if s ^ bit not in held:
                held[s ^ bit] = flipped(held[s], n_sky, bit)


def shards(potential, lens_weight, ray_start, patch_index, destination):
    n_sky = lax.axis_size("sky")
    me = lax.axis_index("sky").reshape(1)
    planes = potential.shape[0]
    bundles, _, rays = ray_start.shape
    each = max(2, 2 * bundles // n_sky)
    slots = n_sky * each
    halves = rays // LANES
    bits = [1 << k for k in reversed(range((n_sky - 1).bit_length()))]
    flat = ray_start.reshape(bundles, 2, halves, LANES).transpose(0, 2, 1, 3).reshape(bundles * 2 * halves, LANES)
    own, sent = prepare(n_sky, each, me, destination.reshape(1, bundles), patch_index, flat, potential)
    sent = [sent[0]] + [flipped(sent[s], n_sky, s) for s in range(1, NEAR)]
    held = {0: own}
    for bit in bits[:2]:
        held[bit] = flipped(own, n_sky, bit)
    held[bits[0] ^ bits[1]] = flipped(held[bits[0]], n_sky, bits[1])
    got = turn(4 * each + SUB, sent)
    early = [0, bits[0], bits[1]]
    *got, a, b, c = lax.optimization_barrier((*got, *[held[s] for s in early]))
    held.update(zip(early, (a, b, c)))
    got = [got[0]] + [flipped(got[f], n_sky, f * NEAR) for f in range(1, len(got))]
    spread(held, n_sky, bits[:-1])
    half = len(got) // 2
    for mid, low in ((half, 0), (half + 1, n_sky // 2)):
        some = range(low, low + n_sky // 2, 2)
        got[mid], *evens = lax.optimization_barrier((got[mid], *[held[s] for s in some]))
        held.update(zip(some, evens))
    spread(held, n_sky, bits)
    shift, matrix = trace(each, planes, me, lens_weight, [held[s] for s in range(n_sky)], got)
    shift = shift.reshape(slots, halves, 2, LANES).transpose(0, 2, 1, 3).reshape(slots, 2, rays)
    matrix = matrix.reshape(slots, halves, 4, LANES).transpose(0, 2, 1, 3).reshape(slots, 4, rays)
    return shift, matrix


def solution(mesh):
    in_specs = (
        P("groups", "sky", None),
        P(),
        P(("groups", "sky"), None, None),
        P("groups", "sky"),
        P(("groups", "sky"), None),
    )
    out_specs = (P(("groups", "sky"), None, None), P(("groups", "sky"), None, None))
    return jax.shard_map(shards, mesh=mesh, in_specs=in_specs, out_specs=out_specs, check_vma=False)
```

```python
import functools

import jax
import jax.numpy as jnp
from jax import lax
from jax.experimental import pallas as pl
from jax.experimental.pallas import tpu as pltpu
from jax.sharding import PartitionSpec as P

LANES = 128
SUB = 8
SIDE = 32
CHUNKS = 8
EMPTY = -1024.0
NEAR = 4


def lane_gather(table, idx):
    dims = lax.GatherDimensionNumbers(
        offset_dims=(),
        collapsed_slice_dims=(1,),
        start_index_map=(1,),
        operand_batching_dims=(0,),
        start_indices_batching_dims=(0,),
    )
    return lax.gather(
        table,
        idx[..., None],
        dims,
        slice_sizes=(1, 1),
        mode=lax.GatherScatterMode.PROMISE_IN_BOUNDS,
    )


def split3(value):
    high = value.astype(jnp.bfloat16)
    rest = value - high.astype(jnp.float32)
    middle = rest.astype(jnp.bfloat16)
    low = (rest - middle.astype(jnp.float32)).astype(jnp.bfloat16)
    return high, middle, low


def regroup_kernel(src_ref, dst_ref):
    planes, tiles, _ = src_ref.shape
    lane = lax.broadcasted_iota(jnp.int32, (SUB, LANES), 1)
    source = (lane & 96) + ((lane & 15) << 1) + ((lane >> 4) & 1)
    for plane in range(planes):
        for base in range(0, tiles, SUB):
            parts = [
                lane_gather(src_ref[plane, pl.ds(base, SUB), pl.ds(c * LANES, LANES)], source)
                for c in range(CHUNKS)
            ]
            for step in (1, 2, 4):
                keep = ((lane >> 4) & step) == 0
                for c in range(CHUNKS):
                    if c & step:
                        continue
                    one, two = parts[c], parts[c + step]
                    parts[c] = jnp.where(keep, one, pltpu.roll(two, step * 16, 1))
                    parts[c + step] = jnp.where(keep, pltpu.roll(one, LANES - step * 16, 1), two)
            for c in range(CHUNKS):
                rows = pl.ds((plane * tiles + base) * CHUNKS + c, SUB, stride=CHUNKS)
                dst_ref[rows, :] = parts[c]


def pack_kernel(n_sky, each, per_owner, me_ref, dest_ref, ids_ref, rays_ref, *out_refs):
    me = me_ref[0]
    bundles = dest_ref.shape[1]
    planes = ids_ref.shape[0]
    slots = n_sky * each
    size = 4 * each + SUB
    dest_row = jnp.broadcast_to(dest_ref[...], (bundles, bundles))
    dest_col = jnp.transpose(dest_row)
    row = lax.broadcasted_iota(jnp.int32, (bundles, bundles), 0)
    col = lax.broadcasted_iota(jnp.int32, (bundles, bundles), 1)
    hits = jnp.where((dest_row == dest_col) & (row < col), 1.0, 0.0)
    rank = jnp.sum(hits, axis=0, keepdims=True).astype(jnp.int32)
    slot = (dest_ref[...] ^ me) * each + rank
    place = lax.broadcasted_iota(jnp.int32, (slots, bundles), 0) == slot
    place = jnp.where(place, 1.0, 0.0)
    found = jnp.dot(
        place.astype(jnp.bfloat16),
        jnp.ones((bundles, LANES), jnp.bfloat16),
        preferred_element_type=jnp.float32,
    )
    place3 = jnp.concatenate([place] * 3, axis=1).astype(jnp.bfloat16)
    for part in range(4):
        rays = rays_ref[pl.ds(part, bundles, stride=4), :]
        terms = jnp.concatenate(split3(rays), axis=0)
        sent = jnp.dot(place3, terms, preferred_element_type=jnp.float32)
        if part % 2 == 0:
            sent = jnp.where(found > 0.5, sent, EMPTY)
        for s in range(n_sky):
            rows = pl.ds(s // NEAR * size + part, each, stride=4)
            out_refs[s % NEAR][rows, :] = sent[s * each:(s + 1) * each]
    ids = ids_ref[...]
    plane = lax.broadcasted_iota(jnp.int32, ids.shape, 0)
    owner = (ids // per_owner) ^ dest_ref[...]
    spot = (owner * planes + plane) * per_owner + ids % per_owner
    pad = jnp.zeros((SUB - planes, bundles), jnp.float32)
    fine = jnp.concatenate([(spot & 15).astype(jnp.float32), pad], axis=0)
    coarse = jnp.concatenate([(spot >> 4).astype(jnp.float32), pad], axis=0)
    place = place.astype(jnp.bfloat16)
    contract = (((1,), (1,)), ((), ()))
    fine = lax.dot_general(fine.astype(jnp.bfloat16), place, contract, preferred_element_type=jnp.float32)
    coarse = lax.dot_general(coarse.astype(jnp.bfloat16), place, contract, preferred_element_type=jnp.float32)
    numbers = coarse * 16.0 + fine
    for s in range(n_sky):
        first = s * each
        block = numbers[:, first // LANES * LANES:first // LANES * LANES + LANES]
        turn = (LANES - first % LANES) % LANES
        if turn:
            block = pltpu.roll(block, turn, 1)
        out_refs[s % NEAR][pl.ds(s // NEAR * size + 4 * each, SUB), :] = block


def prepare_kernel(n_sky, each, me_ref, dest_ref, ids_ref, rays_ref, src_ref, dst_ref, *out_refs):
    regroup_kernel(src_ref, dst_ref)
    pack_kernel(n_sky, each, src_ref.shape[1], me_ref, dest_ref, ids_ref, rays_ref, *out_refs)


def prepare(n_sky, each, me, dest, ids, rays, potential):
    planes, tiles, pixels = potential.shape
    part = jax.ShapeDtypeStruct((n_sky // NEAR * (4 * each + SUB), LANES), jnp.float32)
    own = jax.ShapeDtypeStruct((planes * tiles * pixels // LANES, LANES), jnp.float32)
    own, *sent = pl.pallas_call(
        functools.partial(prepare_kernel, n_sky, each),
        out_shape=[own] + [part] * NEAR,
        in_specs=[pl.BlockSpec(memory_space=pltpu.SMEM)] + [pl.BlockSpec(memory_space=pltpu.VMEM)] * 4,
        out_specs=[pl.BlockSpec(memory_space=pltpu.VMEM)] * (1 + NEAR),
        name="prepare",
    )(me, dest, ids, rays, potential)
    return own, sent


def turn_kernel(size, *refs):
    far = len(refs) - NEAR
    for f in range(far):
        for c in range(NEAR):
            refs[NEAR + f][pl.ds(c * size, size), :] = refs[c][pl.ds(f * size, size), :]


def turn(size, parts):
    far = parts[0].shape[0] // size
    block = jax.ShapeDtypeStruct((NEAR * size, LANES), jnp.float32)
    return pl.pallas_call(
        functools.partial(turn_kernel, size),
        out_shape=[block] * far,
        in_specs=[pl.BlockSpec(memory_space=pltpu.VMEM)] * NEAR,
        out_specs=[pl.BlockSpec(memory_space=pltpu.VMEM)] * far,
        compiler_params=pltpu.CompilerParams(vmem_limit_bytes=4 * 1024 * 1024),
        name="turn",
    )(*parts)


def bilinear(f00, f01, f10, f11, u, v):
    one = f00 + u * (f01 - f00)
    two = f10 + u * (f11 - f10)
    return one + v * (two - one)


def lerp(one, two, t):
    return one + t * (two - one)


def window(tables, pos_x, pos_y):
    ix = (pos_x + float(SIDE)).astype(jnp.int32)
    iy = (pos_y + float(SIDE)).astype(jnp.int32)
    u = pos_x - (ix.astype(jnp.float32) - float(SIDE))
    v = pos_y - (iy.astype(jnp.float32) - float(SIDE))
    odd = (ix - 1) >> 1
    even = ix >> 1
    columns = (((even & 15), ((even + 1) & 15)), ((odd & 15), ((odd + 1) & 15)))
    odd_first = (ix & 1) == 0
    by_two = ((iy - 1) & 2) != 0
    by_one = (iy & 1) == 0
    sorted_columns = []
    for a in range(4):
        line = ((iy + (2 - a)) & 28) << 2
        e0, e1 = [lane_gather(tables[2 * a], line + c) for c in columns[0]]
        o0, o1 = [lane_gather(tables[2 * a + 1], line + c) for c in columns[1]]
        sorted_columns.append((
            jnp.where(odd_first, o0, e0),
            jnp.where(odd_first, e0, o0),
            jnp.where(odd_first, o1, e1),
            jnp.where(odd_first, e1, o1),
        ))
    w = [[None] * 4 for _ in range(4)]
    for k in range(4):
        half = [jnp.where(by_two, sorted_columns[(r + 2) & 3][k], sorted_columns[r][k]) for r in range(4)]
        for r in range(4):
            w[r][k] = jnp.where(by_one, half[(r + 1) & 3], half[r])
    return w, u, v


def trace_step(tables, strength, pos_x, pos_y, matrix):
    w, u, v = window(tables, pos_x, pos_y)
    gx = [lerp(w[1][k + 1] - w[1][k], w[2][k + 1] - w[2][k], v) for k in range(3)]
    gy = [lerp(w[r + 1][1] - w[r][1], w[r + 1][2] - w[r][2], u) for r in range(3)]
    fx2 = lerp(gx[0] + gx[1], gx[1] + gx[2], u)
    fxx = lerp(gx[1] - gx[0], gx[2] - gx[1], u)
    fy2 = lerp(gy[0] + gy[1], gy[1] + gy[2], v)
    fyy = lerp(gy[1] - gy[0], gy[2] - gy[1], v)
    wide = [[w[r][k + 2] - w[r][k] for k in range(2)] for r in range(4)]
    fxy4 = bilinear(
        wide[2][0] - wide[0][0], wide[2][1] - wide[0][1],
        wide[3][0] - wide[1][0], wide[3][1] - wide[1][1], u, v)
    half = 0.5 * strength
    hxx, hxy, hyy = strength * fxx, (0.25 * strength) * fxy4, strength * fyy
    m11, m12, m21, m22 = matrix
    matrix = (
        m11 - (hxx * m11 + hxy * m21),
        m12 - (hxx * m12 + hxy * m22),
        m21 - (hxy * m11 + hyy * m21),
        m22 - (hxy * m12 + hyy * m22),
    )
    return pos_x - half * fx2, pos_y - half * fy2, matrix


def trace_kernel(n_sky, each, planes, together, me_ref, lens_ref, *refs):
    far = n_sky // NEAR
    size = 4 * each + SUB
    tile_refs, got_refs = refs[:n_sky], refs[n_sky:n_sky + far]
    shift_ref, matrix_ref, tiles, chosen, rays, places, sems = refs[n_sky + far:]
    me = me_ref[0]
    slots = n_sky * each
    rows = tile_refs[0].shape[0]
    numbers = []
    for s in range(n_sky):
        source = me ^ s
        got_ref, first = got_refs[s // NEAR], s % NEAR * size
        copy = pltpu.make_async_copy(
            got_ref.at[pl.ds(first + 4 * each, SUB), :],
            places.at[pl.ds(source * SUB, SUB), :],
            sems.at[s])
        copy.start()
        numbers.append(copy)
    for s in range(n_sky):
        source = me ^ s
        got_ref, first = got_refs[s // NEAR], s % NEAR * size
        block = pl.ds(pl.multiple_of(source * (4 * each), SUB), 4 * each)
        rays[block, :] = got_ref[pl.ds(first, 4 * each), :]
        tiles[pl.ds(s * rows, rows), :] = tile_refs[s][...]
    for copy in numbers:
        copy.wait()

    def body(step, carry):
        chains = []
        first = pl.multiple_of(step * (together * SUB), together * SUB)
        for plane in range(planes):
            for part in range(together):
                for k in range(SUB):
                    slot = first + (part * SUB + k)
                    spot = places[slot // each * SUB + plane, slot % each].astype(jnp.int32)
                    tile = tiles[pl.ds(pl.multiple_of(spot * CHUNKS, CHUNKS), CHUNKS), :]
                    chosen[pl.ds((plane * together + part) * CHUNKS * SUB + k, CHUNKS, stride=SUB), :] = tile
        for part in range(together):
            base = first + part * SUB
            for h in range(2):
                x0 = rays[pl.ds(base * 4 + 2 * h, SUB, stride=4), :]
                y0 = rays[pl.ds(base * 4 + 2 * h + 1, SUB, stride=4), :]
                one = jnp.ones_like(x0)
                zero = jnp.zeros_like(x0)
                chains.append((part, h, x0, y0, (x0, y0, (one, zero, zero, one))))
        for plane in range(planes):
            strength = lens_ref[plane]
            later = []
            for part, h, x0, y0, state in chains:
                tables = [
                    chosen[pl.ds(((plane * together + part) * CHUNKS + c) * SUB, SUB), :]
                    for c in range(CHUNKS)
                ]
                later.append((part, h, x0, y0, trace_step(tables, strength, *state)))
            chains = later
        for part, h, x0, y0, (x, y, matrix) in chains:
            base = first + part * SUB
            used = x0 > EMPTY * 0.5
            shift_ref[pl.ds(base * 4 + 2 * h, SUB, stride=4), :] = jnp.where(used, x - x0, 0.0)
            shift_ref[pl.ds(base * 4 + 2 * h + 1, SUB, stride=4), :] = jnp.where(used, y - y0, 0.0)
            for e in range(4):
                matrix_ref[pl.ds(base * 8 + 4 * h + e, SUB, stride=8), :] = jnp.where(used, matrix[e], 0.0)
        return carry

    lax.fori_loop(0, slots // (SUB * together), body, 0)


def trace(each, planes, me, lens_weight, tiles, got):
    n_sky = len(tiles)
    slots = n_sky * each
    rows = tiles[0].shape[0]
    together = 4
    return pl.pallas_call(
        functools.partial(trace_kernel, n_sky, each, planes, together),
        out_shape=(
            jax.ShapeDtypeStruct((slots * 4, LANES), jnp.float32),
            jax.ShapeDtypeStruct((slots * 8, LANES), jnp.float32),
        ),
        in_specs=[pl.BlockSpec(memory_space=pltpu.SMEM)] * 2 + [pl.BlockSpec(memory_space=pltpu.VMEM)] * (n_sky + len(got)),
        out_specs=(
            pl.BlockSpec(memory_space=pltpu.VMEM),
            pl.BlockSpec(memory_space=pltpu.VMEM),
        ),
        scratch_shapes=[
            pltpu.VMEM((n_sky * rows, LANES), jnp.float32),
            pltpu.VMEM((planes * together * CHUNKS * SUB, LANES), jnp.float32),
            pltpu.VMEM((slots * 4, LANES), jnp.float32),
            pltpu.SMEM((n_sky * SUB, LANES), jnp.float32),
            pltpu.SemaphoreType.DMA((n_sky,)),
        ],
        compiler_params=pltpu.CompilerParams(vmem_limit_bytes=20 * 1024 * 1024),
        name="trace",
    )(me, lens_weight, *tiles, *got)


def flipped(value, n_sky, bits):
    return lax.ppermute(value, "sky", [(i, i ^ bits) for i in range(n_sky)])


def spread(held, n_sky, bits):
    for bit in bits:
        for s in [s for s in held if s & (2 * bit - 1) == 0]:
            if s ^ bit not in held:
                held[s ^ bit] = flipped(held[s], n_sky, bit)


def shards(potential, lens_weight, ray_start, patch_index, destination):
    n_sky = lax.axis_size("sky")
    me = lax.axis_index("sky").reshape(1)
    planes = potential.shape[0]
    bundles, _, rays = ray_start.shape
    each = max(2, 2 * bundles // n_sky)
    slots = n_sky * each
    halves = rays // LANES
    bits = [1 << k for k in reversed(range((n_sky - 1).bit_length()))]
    flat = ray_start.reshape(bundles, 2, halves, LANES).transpose(0, 2, 1, 3).reshape(bundles * 2 * halves, LANES)
    own, sent = prepare(n_sky, each, me, destination.reshape(1, bundles), patch_index, flat, potential)
    sent = [sent[0]] + [flipped(sent[s], n_sky, s) for s in range(1, NEAR)]
    held = {0: own}
    for bit in bits[:2]:
        held[bit] = flipped(own, n_sky, bit)
    held[bits[0] ^ bits[1]] = flipped(held[bits[0]], n_sky, bits[1])
    got = turn(4 * each + SUB, sent)
    early = [0, bits[0], bits[1]]
    *got, a, b, c = lax.optimization_barrier((*got, *[held[s] for s in early]))
    held.update(zip(early, (a, b, c)))
    got = [got[0]] + [flipped(got[f], n_sky, f * NEAR) for f in range(1, len(got))]
    spread(held, n_sky, bits[:-1])
    half = len(got) // 2
    for mid, low in ((half, 0), (half + 1, n_sky // 2)):
        some = range(low, low + n_sky // 2, 2)
        got[mid], *evens = lax.optimization_barrier((got[mid], *[held[s] for s in some]))
        held.update(zip(some, evens))
    spread(held, n_sky, bits)
    shift, matrix = trace(each, planes, me, lens_weight, [held[s] for s in range(n_sky)], got)
    shift = shift.reshape(slots, halves, 2, LANES).transpose(0, 2, 1, 3).reshape(slots, 2, rays)
    matrix = matrix.reshape(slots, halves, 4, LANES).transpose(0, 2, 1, 3).reshape(slots, 4, rays)
    return shift, matrix


def solution(mesh):
    in_specs = (
        P("groups", "sky", None),
        P(),
        P(("groups", "sky"), None, None),
        P("groups", "sky"),
        P(("groups", "sky"), None),
    )
    out_specs = (P(("groups", "sky"), None, None), P(("groups", "sky"), None, None))
    return jax.shard_map(shards, mesh=mesh, in_specs=in_specs, out_specs=out_specs, check_vma=False)
```

```python
import functools

import jax
import jax.numpy as jnp
from jax import lax
from jax.experimental import pallas as pl
from jax.experimental.pallas import tpu as pltpu
from jax.sharding import PartitionSpec as P

LANES = 128
SUB = 8
SIDE = 32
CHUNKS = 8
EMPTY = -1024.0
NEAR = 4


def lane_gather(table, idx):
    dims = lax.GatherDimensionNumbers(
        offset_dims=(),
        collapsed_slice_dims=(1,),
        start_index_map=(1,),
        operand_batching_dims=(0,),
        start_indices_batching_dims=(0,),
    )
    return lax.gather(
        table,
        idx[..., None],
        dims,
        slice_sizes=(1, 1),
        mode=lax.GatherScatterMode.PROMISE_IN_BOUNDS,
    )


def split3(value):
    high = value.astype(jnp.bfloat16)
    rest = value - high.astype(jnp.float32)
    middle = rest.astype(jnp.bfloat16)
    low = (rest - middle.astype(jnp.float32)).astype(jnp.bfloat16)
    return high, middle, low


def regroup_kernel(src_ref, dst_ref):
    planes, tiles, _ = src_ref.shape
    lane = lax.broadcasted_iota(jnp.int32, (SUB, LANES), 1)
    source = (lane & 96) + ((lane & 15) << 1) + ((lane >> 4) & 1)
    for plane in range(planes):
        for base in range(0, tiles, SUB):
            parts = [
                lane_gather(src_ref[plane, pl.ds(base, SUB), pl.ds(c * LANES, LANES)], source)
                for c in range(CHUNKS)
            ]
            for step in (1, 2, 4):
                keep = ((lane >> 4) & step) == 0
                for c in range(CHUNKS):
                    if c & step:
                        continue
                    one, two = parts[c], parts[c + step]
                    parts[c] = jnp.where(keep, one, pltpu.roll(two, step * 16, 1))
                    parts[c + step] = jnp.where(keep, pltpu.roll(one, LANES - step * 16, 1), two)
            for c in range(CHUNKS):
                rows = pl.ds((plane * tiles + base) * CHUNKS + c, SUB, stride=CHUNKS)
                dst_ref[rows, :] = parts[c]


def pack_kernel(n_sky, each, per_owner, me_ref, dest_ref, ids_ref, rays_ref, *out_refs):
    me = me_ref[0]
    bundles = dest_ref.shape[1]
    planes = ids_ref.shape[0]
    slots = n_sky * each
    size = 4 * each + SUB
    dest_row = jnp.broadcast_to(dest_ref[...], (bundles, bundles))
    dest_col = jnp.transpose(dest_row)
    row = lax.broadcasted_iota(jnp.int32, (bundles, bundles), 0)
    col = lax.broadcasted_iota(jnp.int32, (bundles, bundles), 1)
    hits = jnp.where((dest_row == dest_col) & (row < col), 1.0, 0.0)
    rank = jnp.sum(hits, axis=0, keepdims=True).astype(jnp.int32)
    slot = (dest_ref[...] ^ me) * each + rank
    place = lax.broadcasted_iota(jnp.int32, (slots, bundles), 0) == slot
    place = jnp.where(place, 1.0, 0.0)
    found = jnp.dot(
        place.astype(jnp.bfloat16),
        jnp.ones((bundles, LANES), jnp.bfloat16),
        preferred_element_type=jnp.float32,
    )
    place3 = jnp.concatenate([place] * 3, axis=1).astype(jnp.bfloat16)
    for part in range(4):
        rays = rays_ref[pl.ds(part, bundles, stride=4), :]
        terms = jnp.concatenate(split3(rays), axis=0)
        sent = jnp.dot(place3, terms, preferred_element_type=jnp.float32)
        if part % 2 == 0:
            sent = jnp.where(found > 0.5, sent, EMPTY)
        for s in range(n_sky):
            rows = pl.ds(s // NEAR * size + part, each, stride=4)
            out_refs[s % NEAR][rows, :] = sent[s * each:(s + 1) * each]
    ids = ids_ref[...]
    plane = lax.broadcasted_iota(jnp.int32, ids.shape, 0)
    owner = (ids // per_owner) ^ dest_ref[...]
    spot = (owner * planes + plane) * per_owner + ids % per_owner
    pad = jnp.zeros((SUB - planes, bundles), jnp.float32)
    fine = jnp.concatenate([(spot & 15).astype(jnp.float32), pad], axis=0)
    coarse = jnp.concatenate([(spot >> 4).astype(jnp.float32), pad], axis=0)
    place = place.astype(jnp.bfloat16)
    contract = (((1,), (1,)), ((), ()))
    fine = lax.dot_general(fine.astype(jnp.bfloat16), place, contract, preferred_element_type=jnp.float32)
    coarse = lax.dot_general(coarse.astype(jnp.bfloat16), place, contract, preferred_element_type=jnp.float32)
    numbers = coarse * 16.0 + fine
    for s in range(n_sky):
        first = s * each
        block = numbers[:, first // LANES * LANES:first // LANES * LANES + LANES]
        turn = (LANES - first % LANES) % LANES
        if turn:
            block = pltpu.roll(block, turn, 1)
        out_refs[s % NEAR][pl.ds(s // NEAR * size + 4 * each, SUB), :] = block


def prepare_kernel(n_sky, each, me_ref, dest_ref, ids_ref, rays_ref, src_ref, dst_ref, *out_refs):
    regroup_kernel(src_ref, dst_ref)
    pack_kernel(n_sky, each, src_ref.shape[1], me_ref, dest_ref, ids_ref, rays_ref, *out_refs)


def prepare(n_sky, each, me, dest, ids, rays, potential):
    planes, tiles, pixels = potential.shape
    part = jax.ShapeDtypeStruct((n_sky // NEAR * (4 * each + SUB), LANES), jnp.float32)
    own = jax.ShapeDtypeStruct((planes * tiles * pixels // LANES, LANES), jnp.float32)
    own, *sent = pl.pallas_call(
        functools.partial(prepare_kernel, n_sky, each),
        out_shape=[own] + [part] * NEAR,
        in_specs=[pl.BlockSpec(memory_space=pltpu.SMEM)] + [pl.BlockSpec(memory_space=pltpu.VMEM)] * 4,
        out_specs=[pl.BlockSpec(memory_space=pltpu.VMEM)] * (1 + NEAR),
        compiler_params=pltpu.CompilerParams(vmem_limit_bytes=16 * 1024 * 1024),
        name="prepare",
    )(me, dest, ids, rays, potential)
    return own, sent


def turn_kernel(size, *refs):
    far = len(refs) - NEAR
    for f in range(far):
        for c in range(NEAR):
            refs[NEAR + f][pl.ds(c * size, size), :] = refs[c][pl.ds(f * size, size), :]


def turn(size, parts):
    far = parts[0].shape[0] // size
    block = jax.ShapeDtypeStruct((NEAR * size, LANES), jnp.float32)
    return pl.pallas_call(
        functools.partial(turn_kernel, size),
        out_shape=[block] * far,
        in_specs=[pl.BlockSpec(memory_space=pltpu.VMEM)] * NEAR,
        out_specs=[pl.BlockSpec(memory_space=pltpu.VMEM)] * far,
        compiler_params=pltpu.CompilerParams(vmem_limit_bytes=4 * 1024 * 1024),
        name="turn",
    )(*parts)


def bilinear(f00, f01, f10, f11, u, v):
    one = f00 + u * (f01 - f00)
    two = f10 + u * (f11 - f10)
    return one + v * (two - one)


def lerp(one, two, t):
    return one + t * (two - one)


def window(tables, pos_x, pos_y):
    ix = (pos_x + float(SIDE)).astype(jnp.int32)
    iy = (pos_y + float(SIDE)).astype(jnp.int32)
    u = pos_x - (ix.astype(jnp.float32) - float(SIDE))
    v = pos_y - (iy.astype(jnp.float32) - float(SIDE))
    odd = (ix - 1) >> 1
    even = ix >> 1
    columns = (((even & 15), ((even + 1) & 15)), ((odd & 15), ((odd + 1) & 15)))
    odd_first = (ix & 1) == 0
    by_two = ((iy - 1) & 2) != 0
    by_one = (iy & 1) == 0
    sorted_columns = []
    for a in range(4):
        line = ((iy + (2 - a)) & 28) << 2
        e0, e1 = [lane_gather(tables[2 * a], line + c) for c in columns[0]]
        o0, o1 = [lane_gather(tables[2 * a + 1], line + c) for c in columns[1]]
        sorted_columns.append((
            jnp.where(odd_first, o0, e0),
            jnp.where(odd_first, e0, o0),
            jnp.where(odd_first, o1, e1),
            jnp.where(odd_first, e1, o1),
        ))
    w = [[None] * 4 for _ in range(4)]
    for k in range(4):
        half = [jnp.where(by_two, sorted_columns[(r + 2) & 3][k], sorted_columns[r][k]) for r in range(4)]
        for r in range(4):
            w[r][k] = jnp.where(by_one, half[(r + 1) & 3], half[r])
    return w, u, v


def trace_step(tables, strength, pos_x, pos_y, matrix):
    w, u, v = window(tables, pos_x, pos_y)
    gx = [lerp(w[1][k + 1] - w[1][k], w[2][k + 1] - w[2][k], v) for k in range(3)]
    gy = [lerp(w[r + 1][1] - w[r][1], w[r + 1][2] - w[r][2], u) for r in range(3)]
    fx2 = lerp(gx[0] + gx[1], gx[1] + gx[2], u)
    fxx = lerp(gx[1] - gx[0], gx[2] - gx[1], u)
    fy2 = lerp(gy[0] + gy[1], gy[1] + gy[2], v)
    fyy = lerp(gy[1] - gy[0], gy[2] - gy[1], v)
    wide = [[w[r][k + 2] - w[r][k] for k in range(2)] for r in range(4)]
    fxy4 = bilinear(
        wide[2][0] - wide[0][0], wide[2][1] - wide[0][1],
        wide[3][0] - wide[1][0], wide[3][1] - wide[1][1], u, v)
    half = 0.5 * strength
    hxx, hxy, hyy = strength * fxx, (0.25 * strength) * fxy4, strength * fyy
    m11, m12, m21, m22 = matrix
    matrix = (
        m11 - (hxx * m11 + hxy * m21),
        m12 - (hxx * m12 + hxy * m22),
        m21 - (hxy * m11 + hyy * m21),
        m22 - (hxy * m12 + hyy * m22),
    )
    return pos_x - half * fx2, pos_y - half * fy2, matrix


def trace_kernel(n_sky, each, planes, together, me_ref, lens_ref, *refs):
    far = n_sky // NEAR
    size = 4 * each + SUB
    tile_refs, got_refs = refs[:n_sky], refs[n_sky:n_sky + far]
    shift_ref, matrix_ref, tiles, chosen, rays, places, sems = refs[n_sky + far:]
    me = me_ref[0]
    slots = n_sky * each
    rows = tile_refs[0].shape[0]
    numbers = []
    for s in range(n_sky):
        source = me ^ s
        got_ref, first = got_refs[s // NEAR], s % NEAR * size
        copy = pltpu.make_async_copy(
            got_ref.at[pl.ds(first + 4 * each, SUB), :],
            places.at[pl.ds(source * SUB, SUB), :],
            sems.at[s])
        copy.start()
        numbers.append(copy)
    for s in range(n_sky):
        source = me ^ s
        got_ref, first = got_refs[s // NEAR], s % NEAR * size
        block = pl.ds(pl.multiple_of(source * (4 * each), SUB), 4 * each)
        rays[block, :] = got_ref[pl.ds(first, 4 * each), :]
        tiles[pl.ds(s * rows, rows), :] = tile_refs[s][...]
    for copy in numbers:
        copy.wait()

    def body(step, carry):
        chains = []
        first = pl.multiple_of(step * (together * SUB), together * SUB)
        for plane in range(planes):
            for part in range(together):
                for k in range(SUB):
                    slot = first + (part * SUB + k)
                    spot = places[slot // each * SUB + plane, slot % each].astype(jnp.int32)
                    tile = tiles[pl.ds(pl.multiple_of(spot * CHUNKS, CHUNKS), CHUNKS), :]
                    chosen[pl.ds((plane * together + part) * CHUNKS * SUB + k, CHUNKS, stride=SUB), :] = tile
        for part in range(together):
            base = first + part * SUB
            for h in range(2):
                x0 = rays[pl.ds(base * 4 + 2 * h, SUB, stride=4), :]
                y0 = rays[pl.ds(base * 4 + 2 * h + 1, SUB, stride=4), :]
                one = jnp.ones_like(x0)
                zero = jnp.zeros_like(x0)
                chains.append((part, h, x0, y0, (x0, y0, (one, zero, zero, one))))
        for plane in range(planes):
            strength = lens_ref[plane]
            later = []
            for part, h, x0, y0, state in chains:
                tables = [
                    chosen[pl.ds(((plane * together + part) * CHUNKS + c) * SUB, SUB), :]
                    for c in range(CHUNKS)
                ]
                later.append((part, h, x0, y0, trace_step(tables, strength, *state)))
            chains = later
        for part, h, x0, y0, (x, y, matrix) in chains:
            base = first + part * SUB
            used = x0 > EMPTY * 0.5
            shift_ref[pl.ds(base * 4 + 2 * h, SUB, stride=4), :] = jnp.where(used, x - x0, 0.0)
            shift_ref[pl.ds(base * 4 + 2 * h + 1, SUB, stride=4), :] = jnp.where(used, y - y0, 0.0)
            for e in range(4):
                matrix_ref[pl.ds(base * 8 + 4 * h + e, SUB, stride=8), :] = jnp.where(used, matrix[e], 0.0)
        return carry

    lax.fori_loop(0, slots // (SUB * together), body, 0)


def trace(each, planes, me, lens_weight, tiles, got):
    n_sky = len(tiles)
    slots = n_sky * each
    rows = tiles[0].shape[0]
    together = 4
    return pl.pallas_call(
        functools.partial(trace_kernel, n_sky, each, planes, together),
        out_shape=(
            jax.ShapeDtypeStruct((slots * 4, LANES), jnp.float32),
            jax.ShapeDtypeStruct((slots * 8, LANES), jnp.float32),
        ),
        in_specs=[pl.BlockSpec(memory_space=pltpu.SMEM)] * 2 + [pl.BlockSpec(memory_space=pltpu.VMEM)] * (n_sky + len(got)),
        out_specs=(
            pl.BlockSpec(memory_space=pltpu.VMEM),
            pl.BlockSpec(memory_space=pltpu.VMEM),
        ),
        scratch_shapes=[
            pltpu.VMEM((n_sky * rows, LANES), jnp.float32),
            pltpu.VMEM((planes * together * CHUNKS * SUB, LANES), jnp.float32),
            pltpu.VMEM((slots * 4, LANES), jnp.float32),
            pltpu.SMEM((n_sky * SUB, LANES), jnp.float32),
            pltpu.SemaphoreType.DMA((n_sky,)),
        ],
        compiler_params=pltpu.CompilerParams(vmem_limit_bytes=20 * 1024 * 1024),
        name="trace",
    )(me, lens_weight, *tiles, *got)


def flipped(value, n_sky, bits):
    return lax.ppermute(value, "sky", [(i, i ^ bits) for i in range(n_sky)])


def spread(held, n_sky, bits):
    for bit in bits:
        for s in [s for s in held if s & (2 * bit - 1) == 0]:
            if s ^ bit not in held:
                held[s ^ bit] = flipped(held[s], n_sky, bit)


def shards(potential, lens_weight, ray_start, patch_index, destination):
    n_sky = lax.axis_size("sky")
    me = lax.axis_index("sky").reshape(1)
    planes = potential.shape[0]
    bundles, _, rays = ray_start.shape
    each = max(2, 2 * bundles // n_sky)
    slots = n_sky * each
    halves = rays // LANES
    bits = [1 << k for k in reversed(range((n_sky - 1).bit_length()))]
    flat = ray_start.reshape(bundles, 2, halves, LANES).transpose(0, 2, 1, 3).reshape(bundles * 2 * halves, LANES)
    own, sent = prepare(n_sky, each, me, destination.reshape(1, bundles), patch_index, flat, potential)
    sent = [sent[0]] + [flipped(sent[s], n_sky, s) for s in range(1, NEAR)]
    held = {0: own}
    for bit in bits[:2]:
        held[bit] = flipped(own, n_sky, bit)
    held[bits[0] ^ bits[1]] = flipped(held[bits[0]], n_sky, bits[1])
    got = turn(4 * each + SUB, sent)
    early = [0, bits[0], bits[1]]
    *got, a, b, c = lax.optimization_barrier((*got, *[held[s] for s in early]))
    held.update(zip(early, (a, b, c)))
    got = [got[0]] + [flipped(got[f], n_sky, f * NEAR) for f in range(1, len(got))]
    spread(held, n_sky, bits[:-1])
    half = len(got) // 2
    for mid, low in ((half, 0), (half + 1, n_sky // 2)):
        some = range(low + n_sky // 2 - 2, low + n_sky // 2, 2)
        got[mid], *evens = lax.optimization_barrier((got[mid], *[held[s] for s in some]))
        held.update(zip(some, evens))
    spread(held, n_sky, bits)
    shift, matrix = trace(each, planes, me, lens_weight, [held[s] for s in range(n_sky)], got)
    shift = shift.reshape(slots, halves, 2, LANES).transpose(0, 2, 1, 3).reshape(slots, 2, rays)
    matrix = matrix.reshape(slots, halves, 4, LANES).transpose(0, 2, 1, 3).reshape(slots, 4, rays)
    return shift, matrix


def solution(mesh):
    in_specs = (
        P("groups", "sky", None),
        P(),
        P(("groups", "sky"), None, None),
        P("groups", "sky"),
        P(("groups", "sky"), None),
    )
    out_specs = (P(("groups", "sky"), None, None), P(("groups", "sky"), None, None))
    return jax.shard_map(shards, mesh=mesh, in_specs=in_specs, out_specs=out_specs, check_vma=False)
```

```python
import functools

import jax
import jax.numpy as jnp
from jax import lax
from jax.experimental import pallas as pl
from jax.experimental.pallas import tpu as pltpu
from jax.sharding import PartitionSpec as P

LANES = 128
SUB = 8
SIDE = 32
CHUNKS = 8
EMPTY = -1024.0
NEAR = 4


def lane_gather(table, idx):
    dims = lax.GatherDimensionNumbers(
        offset_dims=(),
        collapsed_slice_dims=(1,),
        start_index_map=(1,),
        operand_batching_dims=(0,),
        start_indices_batching_dims=(0,),
    )
    return lax.gather(
        table,
        idx[..., None],
        dims,
        slice_sizes=(1, 1),
        mode=lax.GatherScatterMode.PROMISE_IN_BOUNDS,
    )


def split3(value):
    high = value.astype(jnp.bfloat16)
    rest = value - high.astype(jnp.float32)
    middle = rest.astype(jnp.bfloat16)
    low = (rest - middle.astype(jnp.float32)).astype(jnp.bfloat16)
    return high, middle, low


def regroup_kernel(src_ref, dst_ref):
    planes, tiles, _ = src_ref.shape
    lane = lax.broadcasted_iota(jnp.int32, (SUB, LANES), 1)
    source = (lane & 96) + ((lane & 15) << 1) + ((lane >> 4) & 1)
    for plane in range(planes):
        for base in range(0, tiles, SUB):
            parts = [
                lane_gather(src_ref[plane, pl.ds(base, SUB), pl.ds(c * LANES, LANES)], source)
                for c in range(CHUNKS)
            ]
            for step in (1, 2, 4):
                keep = ((lane >> 4) & step) == 0
                for c in range(CHUNKS):
                    if c & step:
                        continue
                    one, two = parts[c], parts[c + step]
                    parts[c] = jnp.where(keep, one, pltpu.roll(two, step * 16, 1))
                    parts[c + step] = jnp.where(keep, pltpu.roll(one, LANES - step * 16, 1), two)
            for c in range(CHUNKS):
                rows = pl.ds((plane * tiles + base) * CHUNKS + c, SUB, stride=CHUNKS)
                dst_ref[rows, :] = parts[c]


def pack_kernel(n_sky, each, per_owner, me_ref, dest_ref, ids_ref, rays_ref, *out_refs):
    me = me_ref[0]
    bundles = dest_ref.shape[1]
    planes = ids_ref.shape[0]
    slots = n_sky * each
    size = 4 * each + SUB
    dest_row = jnp.broadcast_to(dest_ref[...], (bundles, bundles))
    dest_col = jnp.transpose(dest_row)
    row = lax.broadcasted_iota(jnp.int32, (bundles, bundles), 0)
    col = lax.broadcasted_iota(jnp.int32, (bundles, bundles), 1)
    hits = jnp.where((dest_row == dest_col) & (row < col), 1.0, 0.0)
    rank = jnp.sum(hits, axis=0, keepdims=True).astype(jnp.int32)
    slot = (dest_ref[...] ^ me) * each + rank
    place = lax.broadcasted_iota(jnp.int32, (slots, bundles), 0) == slot
    place = jnp.where(place, 1.0, 0.0)
    found = jnp.dot(
        place.astype(jnp.bfloat16),
        jnp.ones((bundles, LANES), jnp.bfloat16),
        preferred_element_type=jnp.float32,
    )
    place3 = jnp.concatenate([place] * 3, axis=1).astype(jnp.bfloat16)
    for part in range(4):
        rays = rays_ref[pl.ds(part, bundles, stride=4), :]
        terms = jnp.concatenate(split3(rays), axis=0)
        sent = jnp.dot(place3, terms, preferred_element_type=jnp.float32)
        if part % 2 == 0:
            sent = jnp.where(found > 0.5, sent, EMPTY)
        for s in range(n_sky):
            rows = pl.ds(s // NEAR * size + part, each, stride=4)
            out_refs[s % NEAR][rows, :] = sent[s * each:(s + 1) * each]
    ids = ids_ref[...]
    plane = lax.broadcasted_iota(jnp.int32, ids.shape, 0)
    owner = (ids // per_owner) ^ dest_ref[...]
    spot = (owner * planes + plane) * per_owner + ids % per_owner
    pad = jnp.zeros((SUB - planes, bundles), jnp.float32)
    fine = jnp.concatenate([(spot & 15).astype(jnp.float32), pad], axis=0)
    coarse = jnp.concatenate([(spot >> 4).astype(jnp.float32), pad], axis=0)
    place = place.astype(jnp.bfloat16)
    contract = (((1,), (1,)), ((), ()))
    fine = lax.dot_general(fine.astype(jnp.bfloat16), place, contract, preferred_element_type=jnp.float32)
    coarse = lax.dot_general(coarse.astype(jnp.bfloat16), place, contract, preferred_element_type=jnp.float32)
    numbers = coarse * 16.0 + fine
    for s in range(n_sky):
        first = s * each
        block = numbers[:, first // LANES * LANES:first // LANES * LANES + LANES]
        turn = (LANES - first % LANES) % LANES
        if turn:
            block = pltpu.roll(block, turn, 1)
        out_refs[s % NEAR][pl.ds(s // NEAR * size + 4 * each, SUB), :] = block


def prepare_kernel(n_sky, each, me_ref, dest_ref, ids_ref, rays_ref, src_ref, dst_ref, *out_refs):
    regroup_kernel(src_ref, dst_ref)
    pack_kernel(n_sky, each, src_ref.shape[1], me_ref, dest_ref, ids_ref, rays_ref, *out_refs)


def prepare(n_sky, each, me, dest, ids, rays, potential):
    planes, tiles, pixels = potential.shape
    part = jax.ShapeDtypeStruct((n_sky // NEAR * (4 * each + SUB), LANES), jnp.float32)
    own = jax.ShapeDtypeStruct((planes * tiles * pixels // LANES, LANES), jnp.float32)
    own, *sent = pl.pallas_call(
        functools.partial(prepare_kernel, n_sky, each),
        out_shape=[own] + [part] * NEAR,
        in_specs=[pl.BlockSpec(memory_space=pltpu.SMEM)] + [pl.BlockSpec(memory_space=pltpu.VMEM)] * 4,
        out_specs=[pl.BlockSpec(memory_space=pltpu.VMEM)] * (1 + NEAR),
        compiler_params=pltpu.CompilerParams(vmem_limit_bytes=16 * 1024 * 1024),
        name="prepare",
    )(me, dest, ids, rays, potential)
    return own, sent


def turn_kernel(size, *refs):
    far = len(refs) - NEAR
    for f in range(far):
        for c in range(NEAR):
            refs[NEAR + f][pl.ds(c * size, size), :] = refs[c][pl.ds(f * size, size), :]


def turn(size, parts):
    far = parts[0].shape[0] // size
    block = jax.ShapeDtypeStruct((NEAR * size, LANES), jnp.float32)
    return pl.pallas_call(
        functools.partial(turn_kernel, size),
        out_shape=[block] * far,
        in_specs=[pl.BlockSpec(memory_space=pltpu.VMEM)] * NEAR,
        out_specs=[pl.BlockSpec(memory_space=pltpu.VMEM)] * far,
        compiler_params=pltpu.CompilerParams(vmem_limit_bytes=4 * 1024 * 1024),
        name="turn",
    )(*parts)


def bilinear(f00, f01, f10, f11, u, v):
    one = f00 + u * (f01 - f00)
    two = f10 + u * (f11 - f10)
    return one + v * (two - one)


def lerp(one, two, t):
    return one + t * (two - one)


def window(tables, pos_x, pos_y):
    ix = (pos_x + float(SIDE)).astype(jnp.int32)
    iy = (pos_y + float(SIDE)).astype(jnp.int32)
    u = pos_x - (ix.astype(jnp.float32) - float(SIDE))
    v = pos_y - (iy.astype(jnp.float32) - float(SIDE))
    odd = (ix - 1) >> 1
    even = ix >> 1
    columns = (((even & 15), ((even + 1) & 15)), ((odd & 15), ((odd + 1) & 15)))
    odd_first = (ix & 1) == 0
    by_two = ((iy - 1) & 2) != 0
    by_one = (iy & 1) == 0
    sorted_columns = []
    for a in range(4):
        line = ((iy + (2 - a)) & 28) << 2
        e0, e1 = [lane_gather(tables[2 * a], line + c) for c in columns[0]]
        o0, o1 = [lane_gather(tables[2 * a + 1], line + c) for c in columns[1]]
        sorted_columns.append((
            jnp.where(odd_first, o0, e0),
            jnp.where(odd_first, e0, o0),
            jnp.where(odd_first, o1, e1),
            jnp.where(odd_first, e1, o1),
        ))
    w = [[None] * 4 for _ in range(4)]
    for k in range(4):
        half = [jnp.where(by_two, sorted_columns[(r + 2) & 3][k], sorted_columns[r][k]) for r in range(4)]
        for r in range(4):
            w[r][k] = jnp.where(by_one, half[(r + 1) & 3], half[r])
    return w, u, v


def trace_step(tables, strength, pos_x, pos_y, matrix):
    w, u, v = window(tables, pos_x, pos_y)
    gx = [lerp(w[1][k + 1] - w[1][k], w[2][k + 1] - w[2][k], v) for k in range(3)]
    gy = [lerp(w[r + 1][1] - w[r][1], w[r + 1][2] - w[r][2], u) for r in range(3)]
    fx2 = lerp(gx[0] + gx[1], gx[1] + gx[2], u)
    fxx = lerp(gx[1] - gx[0], gx[2] - gx[1], u)
    fy2 = lerp(gy[0] + gy[1], gy[1] + gy[2], v)
    fyy = lerp(gy[1] - gy[0], gy[2] - gy[1], v)
    wide = [[w[r][k + 2] - w[r][k] for k in range(2)] for r in range(4)]
    fxy4 = bilinear(
        wide[2][0] - wide[0][0], wide[2][1] - wide[0][1],
        wide[3][0] - wide[1][0], wide[3][1] - wide[1][1], u, v)
    half = 0.5 * strength
    hxx, hxy, hyy = strength * fxx, (0.25 * strength) * fxy4, strength * fyy
    m11, m12, m21, m22 = matrix
    matrix = (
        m11 - (hxx * m11 + hxy * m21),
        m12 - (hxx * m12 + hxy * m22),
        m21 - (hxy * m11 + hyy * m21),
        m22 - (hxy * m12 + hyy * m22),
    )
    return pos_x - half * fx2, pos_y - half * fy2, matrix


def trace_kernel(n_sky, each, planes, together, me_ref, lens_ref, *refs):
    far = n_sky // NEAR
    size = 4 * each + SUB
    tile_refs, got_refs = refs[:n_sky], refs[n_sky:n_sky + far]
    shift_ref, matrix_ref, tiles, chosen, rays, places, sems = refs[n_sky + far:]
    me = me_ref[0]
    slots = n_sky * each
    rows = tile_refs[0].shape[0]
    numbers = []
    for s in range(n_sky):
        source = me ^ s
        got_ref, first = got_refs[s // NEAR], s % NEAR * size
        copy = pltpu.make_async_copy(
            got_ref.at[pl.ds(first + 4 * each, SUB), :],
            places.at[pl.ds(source * SUB, SUB), :],
            sems.at[s])
        copy.start()
        numbers.append(copy)
    for s in range(n_sky):
        source = me ^ s
        got_ref, first = got_refs[s // NEAR], s % NEAR * size
        block = pl.ds(pl.multiple_of(source * (4 * each), SUB), 4 * each)
        rays[block, :] = got_ref[pl.ds(first, 4 * each), :]
        tiles[pl.ds(s * rows, rows), :] = tile_refs[s][...]
    for copy in numbers:
        copy.wait()

    def body(step, carry):
        chains = []
        first = pl.multiple_of(step * (together * SUB), together * SUB)
        for plane in range(planes):
            for part in range(together):
                for k in range(SUB):
                    slot = first + (part * SUB + k)
                    spot = places[slot // each * SUB + plane, slot % each].astype(jnp.int32)
                    tile = tiles[pl.ds(pl.multiple_of(spot * CHUNKS, CHUNKS), CHUNKS), :]
                    chosen[pl.ds((plane * together + part) * CHUNKS * SUB + k, CHUNKS, stride=SUB), :] = tile
        for part in range(together):
            base = first + part * SUB
            for h in range(2):
                x0 = rays[pl.ds(base * 4 + 2 * h, SUB, stride=4), :]
                y0 = rays[pl.ds(base * 4 + 2 * h + 1, SUB, stride=4), :]
                one = jnp.ones_like(x0)
                zero = jnp.zeros_like(x0)
                chains.append((part, h, x0, y0, (x0, y0, (one, zero, zero, one))))
        for plane in range(planes):
            strength = lens_ref[plane]
            later = []
            for part, h, x0, y0, state in chains:
                tables = [
                    chosen[pl.ds(((plane * together + part) * CHUNKS + c) * SUB, SUB), :]
                    for c in range(CHUNKS)
                ]
                later.append((part, h, x0, y0, trace_step(tables, strength, *state)))
            chains = later
        for part, h, x0, y0, (x, y, matrix) in chains:
            base = first + part * SUB
            used = x0 > EMPTY * 0.5
            shift_ref[pl.ds(base * 4 + 2 * h, SUB, stride=4), :] = jnp.where(used, x - x0, 0.0)
            shift_ref[pl.ds(base * 4 + 2 * h + 1, SUB, stride=4), :] = jnp.where(used, y - y0, 0.0)
            for e in range(4):
                matrix_ref[pl.ds(base * 8 + 4 * h + e, SUB, stride=8), :] = jnp.where(used, matrix[e], 0.0)
        return carry

    lax.fori_loop(0, slots // (SUB * together), body, 0)


def trace(each, planes, me, lens_weight, tiles, got):
    n_sky = len(tiles)
    slots = n_sky * each
    rows = tiles[0].shape[0]
    together = 4
    return pl.pallas_call(
        functools.partial(trace_kernel, n_sky, each, planes, together),
        out_shape=(
            jax.ShapeDtypeStruct((slots * 4, LANES), jnp.float32),
            jax.ShapeDtypeStruct((slots * 8, LANES), jnp.float32),
        ),
        in_specs=[pl.BlockSpec(memory_space=pltpu.SMEM)] * 2 + [pl.BlockSpec(memory_space=pltpu.VMEM)] * (n_sky + len(got)),
        out_specs=(
            pl.BlockSpec(memory_space=pltpu.VMEM),
            pl.BlockSpec(memory_space=pltpu.VMEM),
        ),
        scratch_shapes=[
            pltpu.VMEM((n_sky * rows, LANES), jnp.float32),
            pltpu.VMEM((planes * together * CHUNKS * SUB, LANES), jnp.float32),
            pltpu.VMEM((slots * 4, LANES), jnp.float32),
            pltpu.SMEM((n_sky * SUB, LANES), jnp.float32),
            pltpu.SemaphoreType.DMA((n_sky,)),
        ],
        compiler_params=pltpu.CompilerParams(vmem_limit_bytes=20 * 1024 * 1024),
        name="trace",
    )(me, lens_weight, *tiles, *got)


def flipped(value, n_sky, bits):
    return lax.ppermute(value, "sky", [(i, i ^ bits) for i in range(n_sky)])


def spread(held, n_sky, bits):
    for bit in bits:
        for s in [s for s in held if s & (2 * bit - 1) == 0]:
            if s ^ bit not in held:
                held[s ^ bit] = flipped(held[s], n_sky, bit)


def shards(potential, lens_weight, ray_start, patch_index, destination):
    n_sky = lax.axis_size("sky")
    me = lax.axis_index("sky").reshape(1)
    planes = potential.shape[0]
    bundles, _, rays = ray_start.shape
    each = max(2, 2 * bundles // n_sky)
    slots = n_sky * each
    halves = rays // LANES
    bits = [1 << k for k in reversed(range((n_sky - 1).bit_length()))]
    flat = ray_start.reshape(bundles, 2, halves, LANES).transpose(0, 2, 1, 3).reshape(bundles * 2 * halves, LANES)
    own, sent = prepare(n_sky, each, me, destination.reshape(1, bundles), patch_index, flat, potential)
    sent = [sent[0]] + [flipped(sent[s], n_sky, s) for s in range(1, NEAR)]
    held = {0: own}
    for bit in bits[:2]:
        held[bit] = flipped(own, n_sky, bit)
    held[bits[0] ^ bits[1]] = flipped(held[bits[0]], n_sky, bits[1])
    got = turn(4 * each + SUB, sent)
    early = [0, bits[0], bits[1]]
    *got, a, b, c = lax.optimization_barrier((*got, *[held[s] for s in early]))
    held.update(zip(early, (a, b, c)))
    got = [got[0]] + [flipped(got[f], n_sky, f * NEAR) for f in range(1, len(got))]
    spread(held, n_sky, bits[:-1])
    half = len(got) // 2
    for mid, low in ((half, 0), (half + 1, n_sky // 2)):
        some = range(low, low + n_sky // 2, 2)
        got[mid], *evens = lax.optimization_barrier((got[mid], *[held[s] for s in some]))
        held.update(zip(some, evens))
    spread(held, n_sky, bits)
    shift, matrix = trace(each, planes, me, lens_weight, [held[s] for s in range(n_sky)], got)
    shift = shift.reshape(slots, halves, 2, LANES).transpose(0, 2, 1, 3).reshape(slots, 2, rays)
    matrix = matrix.reshape(slots, halves, 4, LANES).transpose(0, 2, 1, 3).reshape(slots, 4, rays)
    return shift, matrix


def solution(mesh):
    in_specs = (
        P("groups", "sky", None),
        P(),
        P(("groups", "sky"), None, None),
        P("groups", "sky"),
        P(("groups", "sky"), None),
    )
    out_specs = (P(("groups", "sky"), None, None), P(("groups", "sky"), None, None))
    return jax.shard_map(shards, mesh=mesh, in_specs=in_specs, out_specs=out_specs, check_vma=False)
```

```python
import functools

import jax
import jax.numpy as jnp
from jax import lax
from jax.experimental import pallas as pl
from jax.experimental.pallas import tpu as pltpu
from jax.sharding import PartitionSpec as P

LANES = 128
SUB = 8
SIDE = 32
CHUNKS = 8
EMPTY = -1024.0
NEAR = 4


def lane_gather(table, idx):
    dims = lax.GatherDimensionNumbers(
        offset_dims=(),
        collapsed_slice_dims=(1,),
        start_index_map=(1,),
        operand_batching_dims=(0,),
        start_indices_batching_dims=(0,),
    )
    return lax.gather(
        table,
        idx[..., None],
        dims,
        slice_sizes=(1, 1),
        mode=lax.GatherScatterMode.PROMISE_IN_BOUNDS,
    )


def split3(value):
    high = value.astype(jnp.bfloat16)
    rest = value - high.astype(jnp.float32)
    middle = rest.astype(jnp.bfloat16)
    low = (rest - middle.astype(jnp.float32)).astype(jnp.bfloat16)
    return high, middle, low


def regroup_kernel(src_ref, dst_ref):
    planes, tiles, _ = src_ref.shape
    lane = lax.broadcasted_iota(jnp.int32, (SUB, LANES), 1)
    source = (lane & 96) + ((lane & 15) << 1) + ((lane >> 4) & 1)
    for plane in range(planes):
        for base in range(0, tiles, SUB):
            parts = [
                lane_gather(src_ref[plane, pl.ds(base, SUB), pl.ds(c * LANES, LANES)], source)
                for c in range(CHUNKS)
            ]
            for step in (1, 2, 4):
                keep = ((lane >> 4) & step) == 0
                for c in range(CHUNKS):
                    if c & step:
                        continue
                    one, two = parts[c], parts[c + step]
                    parts[c] = jnp.where(keep, one, pltpu.roll(two, step * 16, 1))
                    parts[c + step] = jnp.where(keep, pltpu.roll(one, LANES - step * 16, 1), two)
            for c in range(CHUNKS):
                rows = pl.ds((plane * tiles + base) * CHUNKS + c, SUB, stride=CHUNKS)
                dst_ref[rows, :] = parts[c]


def pack_kernel(n_sky, each, per_owner, me_ref, dest_ref, ids_ref, rays_ref, *out_refs):
    me = me_ref[0]
    bundles = dest_ref.shape[1]
    planes = ids_ref.shape[0]
    slots = n_sky * each
    size = 4 * each + SUB
    dest_row = jnp.broadcast_to(dest_ref[...], (bundles, bundles))
    dest_col = jnp.transpose(dest_row)
    row = lax.broadcasted_iota(jnp.int32, (bundles, bundles), 0)
    col = lax.broadcasted_iota(jnp.int32, (bundles, bundles), 1)
    hits = jnp.where((dest_row == dest_col) & (row < col), 1.0, 0.0)
    rank = jnp.sum(hits, axis=0, keepdims=True).astype(jnp.int32)
    slot = (dest_ref[...] ^ me) * each + rank
    place = lax.broadcasted_iota(jnp.int32, (slots, bundles), 0) == slot
    place = jnp.where(place, 1.0, 0.0)
    found = jnp.dot(
        place.astype(jnp.bfloat16),
        jnp.ones((bundles, LANES), jnp.bfloat16),
        preferred_element_type=jnp.float32,
    )
    place3 = jnp.concatenate([place] * 3, axis=1).astype(jnp.bfloat16)
    for part in range(4):
        rays = rays_ref[pl.ds(part, bundles, stride=4), :]
        terms = jnp.concatenate(split3(rays), axis=0)
        sent = jnp.dot(place3, terms, preferred_element_type=jnp.float32)
        if part % 2 == 0:
            sent = jnp.where(found > 0.5, sent, EMPTY)
        for s in range(n_sky):
            rows = pl.ds(s // NEAR * size + part, each, stride=4)
            out_refs[s % NEAR][rows, :] = sent[s * each:(s + 1) * each]
    ids = ids_ref[...]
    plane = lax.broadcasted_iota(jnp.int32, ids.shape, 0)
    owner = (ids // per_owner) ^ dest_ref[...]
    spot = (owner * planes + plane) * per_owner + ids % per_owner
    pad = jnp.zeros((SUB - planes, bundles), jnp.float32)
    fine = jnp.concatenate([(spot & 15).astype(jnp.float32), pad], axis=0)
    coarse = jnp.concatenate([(spot >> 4).astype(jnp.float32), pad], axis=0)
    place = place.astype(jnp.bfloat16)
    contract = (((1,), (1,)), ((), ()))
    fine = lax.dot_general(fine.astype(jnp.bfloat16), place, contract, preferred_element_type=jnp.float32)
    coarse = lax.dot_general(coarse.astype(jnp.bfloat16), place, contract, preferred_element_type=jnp.float32)
    numbers = coarse * 16.0 + fine
    for s in range(n_sky):
        first = s * each
        block = numbers[:, first // LANES * LANES:first // LANES * LANES + LANES]
        turn = (LANES - first % LANES) % LANES
        if turn:
            block = pltpu.roll(block, turn, 1)
        out_refs[s % NEAR][pl.ds(s // NEAR * size + 4 * each, SUB), :] = block


def prepare_kernel(n_sky, each, me_ref, dest_ref, ids_ref, rays_ref, src_ref, dst_ref, *out_refs):
    regroup_kernel(src_ref, dst_ref)
    pack_kernel(n_sky, each, src_ref.shape[1], me_ref, dest_ref, ids_ref, rays_ref, *out_refs)


def prepare(n_sky, each, me, dest, ids, rays, potential):
    planes, tiles, pixels = potential.shape
    part = jax.ShapeDtypeStruct((n_sky // NEAR * (4 * each + SUB), LANES), jnp.float32)
    own = jax.ShapeDtypeStruct((planes * tiles * pixels // LANES, LANES), jnp.float32)
    own, *sent = pl.pallas_call(
        functools.partial(prepare_kernel, n_sky, each),
        out_shape=[own] + [part] * NEAR,
        in_specs=[pl.BlockSpec(memory_space=pltpu.SMEM)] + [pl.BlockSpec(memory_space=pltpu.VMEM)] * 4,
        out_specs=[pl.BlockSpec(memory_space=pltpu.VMEM)] * (1 + NEAR),
        compiler_params=pltpu.CompilerParams(vmem_limit_bytes=16 * 1024 * 1024),
        name="prepare",
    )(me, dest, ids, rays, potential)
    return own, sent


def turn_kernel(size, *refs):
    far = len(refs) - NEAR
    for f in range(far):
        for c in range(NEAR):
            refs[NEAR + f][pl.ds(c * size, size), :] = refs[c][pl.ds(f * size, size), :]


def turn(size, parts):
    far = parts[0].shape[0] // size
    block = jax.ShapeDtypeStruct((NEAR * size, LANES), jnp.float32)
    return pl.pallas_call(
        functools.partial(turn_kernel, size),
        out_shape=[block] * far,
        in_specs=[pl.BlockSpec(memory_space=pltpu.VMEM)] * NEAR,
        out_specs=[pl.BlockSpec(memory_space=pltpu.VMEM)] * far,
        compiler_params=pltpu.CompilerParams(vmem_limit_bytes=4 * 1024 * 1024),
        name="turn",
    )(*parts)


def bilinear(f00, f01, f10, f11, u, v):
    one = f00 + u * (f01 - f00)
    two = f10 + u * (f11 - f10)
    return one + v * (two - one)


def lerp(one, two, t):
    return one + t * (two - one)


def window(tables, pos_x, pos_y):
    ix = (pos_x + float(SIDE)).astype(jnp.int32)
    iy = (pos_y + float(SIDE)).astype(jnp.int32)
    u = pos_x - (ix.astype(jnp.float32) - float(SIDE))
    v = pos_y - (iy.astype(jnp.float32) - float(SIDE))
    odd = (ix - 1) >> 1
    even = ix >> 1
    columns = (((even & 15), ((even + 1) & 15)), ((odd & 15), ((odd + 1) & 15)))
    odd_first = (ix & 1) == 0
    by_two = ((iy - 1) & 2) != 0
    by_one = (iy & 1) == 0
    sorted_columns = []
    for a in range(4):
        line = ((iy + (2 - a)) & 28) << 2
        e0, e1 = [lane_gather(tables[2 * a], line + c) for c in columns[0]]
        o0, o1 = [lane_gather(tables[2 * a + 1], line + c) for c in columns[1]]
        sorted_columns.append((
            jnp.where(odd_first, o0, e0),
            jnp.where(odd_first, e0, o0),
            jnp.where(odd_first, o1, e1),
            jnp.where(odd_first, e1, o1),
        ))
    w = [[None] * 4 for _ in range(4)]
    for k in range(4):
        half = [jnp.where(by_two, sorted_columns[(r + 2) & 3][k], sorted_columns[r][k]) for r in range(4)]
        for r in range(4):
            w[r][k] = jnp.where(by_one, half[(r + 1) & 3], half[r])
    return w, u, v


def trace_step(tables, strength, pos_x, pos_y, matrix):
    w, u, v = window(tables, pos_x, pos_y)
    gx = [lerp(w[1][k + 1] - w[1][k], w[2][k + 1] - w[2][k], v) for k in range(3)]
    gy = [lerp(w[r + 1][1] - w[r][1], w[r + 1][2] - w[r][2], u) for r in range(3)]
    fx2 = lerp(gx[0] + gx[1], gx[1] + gx[2], u)
    fxx = lerp(gx[1] - gx[0], gx[2] - gx[1], u)
    fy2 = lerp(gy[0] + gy[1], gy[1] + gy[2], v)
    fyy = lerp(gy[1] - gy[0], gy[2] - gy[1], v)
    wide = [[w[r][k + 2] - w[r][k] for k in range(2)] for r in range(4)]
    fxy4 = bilinear(
        wide[2][0] - wide[0][0], wide[2][1] - wide[0][1],
        wide[3][0] - wide[1][0], wide[3][1] - wide[1][1], u, v)
    half = 0.5 * strength
    hxx, hxy, hyy = strength * fxx, (0.25 * strength) * fxy4, strength * fyy
    m11, m12, m21, m22 = matrix
    matrix = (
        m11 - (hxx * m11 + hxy * m21),
        m12 - (hxx * m12 + hxy * m22),
        m21 - (hxy * m11 + hyy * m21),
        m22 - (hxy * m12 + hyy * m22),
    )
    return pos_x - half * fx2, pos_y - half * fy2, matrix


def trace_kernel(n_sky, each, planes, together, me_ref, lens_ref, *refs):
    far = n_sky // NEAR
    size = 4 * each + SUB
    tile_refs, got_refs = refs[:n_sky], refs[n_sky:n_sky + far]
    shift_out, matrix_out, tiles, chosen, rays, places, shift_ref, matrix_ref, sems, out_sems = refs[n_sky + far:]
    me = me_ref[0]
    slots = n_sky * each
    rows = tile_refs[0].shape[0]
    numbers = []
    for s in range(n_sky):
        source = me ^ s
        got_ref, first = got_refs[s // NEAR], s % NEAR * size
        copy = pltpu.make_async_copy(
            got_ref.at[pl.ds(first + 4 * each, SUB), :],
            places.at[pl.ds(source * SUB, SUB), :],
            sems.at[s])
        copy.start()
        numbers.append(copy)
    for s in range(n_sky):
        source = me ^ s
        got_ref, first = got_refs[s // NEAR], s % NEAR * size
        block = pl.ds(pl.multiple_of(source * (4 * each), SUB), 4 * each)
        rays[block, :] = got_ref[pl.ds(first, 4 * each), :]
        tiles[pl.ds(s * rows, rows), :] = tile_refs[s][...]
    for copy in numbers:
        copy.wait()

    def body(step, carry):
        chains = []
        first = pl.multiple_of(step * (together * SUB), together * SUB)
        for plane in range(planes):
            for part in range(together):
                for k in range(SUB):
                    slot = first + (part * SUB + k)
                    spot = places[slot // each * SUB + plane, slot % each].astype(jnp.int32)
                    tile = tiles[pl.ds(pl.multiple_of(spot * CHUNKS, CHUNKS), CHUNKS), :]
                    chosen[pl.ds((plane * together + part) * CHUNKS * SUB + k, CHUNKS, stride=SUB), :] = tile
        for part in range(together):
            base = first + part * SUB
            for h in range(2):
                x0 = rays[pl.ds(base * 4 + 2 * h, SUB, stride=4), :]
                y0 = rays[pl.ds(base * 4 + 2 * h + 1, SUB, stride=4), :]
                one = jnp.ones_like(x0)
                zero = jnp.zeros_like(x0)
                chains.append((part, h, x0, y0, (x0, y0, (one, zero, zero, one))))
        for plane in range(planes):
            strength = lens_ref[plane]
            later = []
            for part, h, x0, y0, state in chains:
                tables = [
                    chosen[pl.ds(((plane * together + part) * CHUNKS + c) * SUB, SUB), :]
                    for c in range(CHUNKS)
                ]
                later.append((part, h, x0, y0, trace_step(tables, strength, *state)))
            chains = later
        for part, h, x0, y0, (x, y, matrix) in chains:
            base = first + part * SUB
            used = x0 > EMPTY * 0.5
            shift_ref[pl.ds(base * 4 + 2 * h, SUB, stride=4), :] = jnp.where(used, x - x0, 0.0)
            shift_ref[pl.ds(base * 4 + 2 * h + 1, SUB, stride=4), :] = jnp.where(used, y - y0, 0.0)
            for e in range(4):
                matrix_ref[pl.ds(base * 8 + 4 * h + e, SUB, stride=8), :] = jnp.where(used, matrix[e], 0.0)
        for copy in results(step):
            copy.start()
        return carry

    def results(step):
        count = together * SUB
        return [
            pltpu.make_async_copy(
                block.at[pl.ds(step * (count * rows_each), count * rows_each), :],
                out.at[pl.ds(step * (count * rows_each), count * rows_each), :],
                out_sems.at[kind, step])
            for kind, (block, out, rows_each) in enumerate(((shift_ref, shift_out, 4), (matrix_ref, matrix_out, 8)))
        ]

    def finish(step, carry):
        for copy in results(step):
            copy.wait()
        return carry

    lax.fori_loop(0, slots // (SUB * together), body, 0)
    lax.fori_loop(0, slots // (SUB * together), finish, 0)


def trace(each, planes, me, lens_weight, tiles, got):
    n_sky = len(tiles)
    slots = n_sky * each
    rows = tiles[0].shape[0]
    together = 4
    return pl.pallas_call(
        functools.partial(trace_kernel, n_sky, each, planes, together),
        out_shape=(
            jax.ShapeDtypeStruct((slots * 4, LANES), jnp.float32),
            jax.ShapeDtypeStruct((slots * 8, LANES), jnp.float32),
        ),
        in_specs=[pl.BlockSpec(memory_space=pltpu.SMEM)] * 2 + [pl.BlockSpec(memory_space=pltpu.VMEM)] * (n_sky + len(got)),
        out_specs=(
            pl.BlockSpec(memory_space=pl.ANY),
            pl.BlockSpec(memory_space=pl.ANY),
        ),
        scratch_shapes=[
            pltpu.VMEM((n_sky * rows, LANES), jnp.float32),
            pltpu.VMEM((planes * together * CHUNKS * SUB, LANES), jnp.float32),
            pltpu.VMEM((slots * 4, LANES), jnp.float32),
            pltpu.SMEM((n_sky * SUB, LANES), jnp.float32),
            pltpu.VMEM((slots * 4, LANES), jnp.float32),
            pltpu.VMEM((slots * 8, LANES), jnp.float32),
            pltpu.SemaphoreType.DMA((n_sky,)),
            pltpu.SemaphoreType.DMA((2, slots // (SUB * 4))),
        ],
        compiler_params=pltpu.CompilerParams(vmem_limit_bytes=20 * 1024 * 1024),
        name="trace",
    )(me, lens_weight, *tiles, *got)


def flipped(value, n_sky, bits):
    return lax.ppermute(value, "sky", [(i, i ^ bits) for i in range(n_sky)])


def spread(held, n_sky, bits):
    for bit in bits:
        for s in [s for s in held if s & (2 * bit - 1) == 0]:
            if s ^ bit not in held:
                held[s ^ bit] = flipped(held[s], n_sky, bit)


def shards(potential, lens_weight, ray_start, patch_index, destination):
    n_sky = lax.axis_size("sky")
    me = lax.axis_index("sky").reshape(1)
    planes = potential.shape[0]
    bundles, _, rays = ray_start.shape
    each = max(2, 2 * bundles // n_sky)
    slots = n_sky * each
    halves = rays // LANES
    bits = [1 << k for k in reversed(range((n_sky - 1).bit_length()))]
    flat = ray_start.reshape(bundles, 2, halves, LANES).transpose(0, 2, 1, 3).reshape(bundles * 2 * halves, LANES)
    own, sent = prepare(n_sky, each, me, destination.reshape(1, bundles), patch_index, flat, potential)
    sent = [sent[0]] + [flipped(sent[s], n_sky, s) for s in range(1, NEAR)]
    held = {0: own}
    for bit in bits[:2]:
        held[bit] = flipped(own, n_sky, bit)
    held[bits[0] ^ bits[1]] = flipped(held[bits[0]], n_sky, bits[1])
    got = turn(4 * each + SUB, sent)
    early = [0, bits[0], bits[1]]
    *got, a, b, c = lax.optimization_barrier((*got, *[held[s] for s in early]))
    held.update(zip(early, (a, b, c)))
    got = [got[0]] + [flipped(got[f], n_sky, f * NEAR) for f in range(1, len(got))]
    spread(held, n_sky, bits[:-1])
    half = len(got) // 2
    for mid, low in ((half, 0), (half + 1, n_sky // 2)):
        some = range(low, low + n_sky // 2, 2)
        got[mid], *evens = lax.optimization_barrier((got[mid], *[held[s] for s in some]))
        held.update(zip(some, evens))
    spread(held, n_sky, bits)
    shift, matrix = trace(each, planes, me, lens_weight, [held[s] for s in range(n_sky)], got)
    shift = shift.reshape(slots, halves, 2, LANES).transpose(0, 2, 1, 3).reshape(slots, 2, rays)
    matrix = matrix.reshape(slots, halves, 4, LANES).transpose(0, 2, 1, 3).reshape(slots, 4, rays)
    return shift, matrix


def solution(mesh):
    in_specs = (
        P("groups", "sky", None),
        P(),
        P(("groups", "sky"), None, None),
        P("groups", "sky"),
        P(("groups", "sky"), None),
    )
    out_specs = (P(("groups", "sky"), None, None), P(("groups", "sky"), None, None))
    return jax.shard_map(shards, mesh=mesh, in_specs=in_specs, out_specs=out_specs, check_vma=False)
```

```python
import functools

import jax
import jax.numpy as jnp
from jax import lax
from jax.experimental import pallas as pl
from jax.experimental.pallas import tpu as pltpu
from jax.sharding import PartitionSpec as P

LANES = 128
SUB = 8
SIDE = 32
CHUNKS = 8
EMPTY = -1024.0
NEAR = 4


def lane_gather(table, idx):
    dims = lax.GatherDimensionNumbers(
        offset_dims=(),
        collapsed_slice_dims=(1,),
        start_index_map=(1,),
        operand_batching_dims=(0,),
        start_indices_batching_dims=(0,),
    )
    return lax.gather(
        table,
        idx[..., None],
        dims,
        slice_sizes=(1, 1),
        mode=lax.GatherScatterMode.PROMISE_IN_BOUNDS,
    )


def split3(value):
    high = value.astype(jnp.bfloat16)
    rest = value - high.astype(jnp.float32)
    middle = rest.astype(jnp.bfloat16)
    low = (rest - middle.astype(jnp.float32)).astype(jnp.bfloat16)
    return high, middle, low


def regroup_kernel(src_ref, dst_ref):
    planes, tiles, _ = src_ref.shape
    lane = lax.broadcasted_iota(jnp.int32, (SUB, LANES), 1)
    source = (lane & 96) + ((lane & 15) << 1) + ((lane >> 4) & 1)
    for plane in range(planes):
        for base in range(0, tiles, SUB):
            parts = [
                lane_gather(src_ref[plane, pl.ds(base, SUB), pl.ds(c * LANES, LANES)], source)
                for c in range(CHUNKS)
            ]
            for step in (1, 2, 4):
                keep = ((lane >> 4) & step) == 0
                for c in range(CHUNKS):
                    if c & step:
                        continue
                    one, two = parts[c], parts[c + step]
                    parts[c] = jnp.where(keep, one, pltpu.roll(two, step * 16, 1))
                    parts[c + step] = jnp.where(keep, pltpu.roll(one, LANES - step * 16, 1), two)
            for c in range(CHUNKS):
                rows = pl.ds((plane * tiles + base) * CHUNKS + c, SUB, stride=CHUNKS)
                dst_ref[rows, :] = parts[c]


def pack_kernel(n_sky, each, per_owner, me_ref, dest_ref, ids_ref, rays_ref, *out_refs):
    me = me_ref[0]
    bundles = dest_ref.shape[1]
    planes = ids_ref.shape[0]
    slots = n_sky * each
    size = 4 * each + SUB
    dest_row = jnp.broadcast_to(dest_ref[...], (bundles, bundles))
    dest_col = jnp.transpose(dest_row)
    row = lax.broadcasted_iota(jnp.int32, (bundles, bundles), 0)
    col = lax.broadcasted_iota(jnp.int32, (bundles, bundles), 1)
    hits = jnp.where((dest_row == dest_col) & (row < col), 1.0, 0.0)
    rank = jnp.sum(hits, axis=0, keepdims=True).astype(jnp.int32)
    slot = (dest_ref[...] ^ me) * each + rank
    place = lax.broadcasted_iota(jnp.int32, (slots, bundles), 0) == slot
    place = jnp.where(place, 1.0, 0.0)
    found = jnp.dot(
        place.astype(jnp.bfloat16),
        jnp.ones((bundles, LANES), jnp.bfloat16),
        preferred_element_type=jnp.float32,
    )
    place3 = jnp.concatenate([place] * 3, axis=1).astype(jnp.bfloat16)
    for part in range(4):
        rays = rays_ref[pl.ds(part, bundles, stride=4), :]
        terms = jnp.concatenate(split3(rays), axis=0)
        sent = jnp.dot(place3, terms, preferred_element_type=jnp.float32)
        if part % 2 == 0:
            sent = jnp.where(found > 0.5, sent, EMPTY)
        for s in range(n_sky):
            rows = pl.ds(s // NEAR * size + part, each, stride=4)
            out_refs[s % NEAR][rows, :] = sent[s * each:(s + 1) * each]
    ids = ids_ref[...]
    plane = lax.broadcasted_iota(jnp.int32, ids.shape, 0)
    owner = (ids // per_owner) ^ dest_ref[...]
    spot = (owner * planes + plane) * per_owner + ids % per_owner
    pad = jnp.zeros((SUB - planes, bundles), jnp.float32)
    fine = jnp.concatenate([(spot & 15).astype(jnp.float32), pad], axis=0)
    coarse = jnp.concatenate([(spot >> 4).astype(jnp.float32), pad], axis=0)
    place = place.astype(jnp.bfloat16)
    contract = (((1,), (1,)), ((), ()))
    fine = lax.dot_general(fine.astype(jnp.bfloat16), place, contract, preferred_element_type=jnp.float32)
    coarse = lax.dot_general(coarse.astype(jnp.bfloat16), place, contract, preferred_element_type=jnp.float32)
    numbers = coarse * 16.0 + fine
    for s in range(n_sky):
        first = s * each
        block = numbers[:, first // LANES * LANES:first // LANES * LANES + LANES]
        turn = (LANES - first % LANES) % LANES
        if turn:
            block = pltpu.roll(block, turn, 1)
        out_refs[s % NEAR][pl.ds(s // NEAR * size + 4 * each, SUB), :] = block


def prepare_kernel(n_sky, each, me_ref, dest_ref, ids_ref, rays_ref, src_ref, dst_ref, *out_refs):
    regroup_kernel(src_ref, dst_ref)
    pack_kernel(n_sky, each, src_ref.shape[1], me_ref, dest_ref, ids_ref, rays_ref, *out_refs)


def prepare(n_sky, each, me, dest, ids, rays, potential):
    planes, tiles, pixels = potential.shape
    part = jax.ShapeDtypeStruct((n_sky // NEAR * (4 * each + SUB), LANES), jnp.float32)
    own = jax.ShapeDtypeStruct((planes * tiles * pixels // LANES, LANES), jnp.float32)
    own, *sent = pl.pallas_call(
        functools.partial(prepare_kernel, n_sky, each),
        out_shape=[own] + [part] * NEAR,
        in_specs=[pl.BlockSpec(memory_space=pltpu.SMEM)] + [pl.BlockSpec(memory_space=pltpu.VMEM)] * 4,
        out_specs=[pl.BlockSpec(memory_space=pltpu.VMEM)] * (1 + NEAR),
        compiler_params=pltpu.CompilerParams(vmem_limit_bytes=16 * 1024 * 1024),
        name="prepare",
    )(me, dest, ids, rays, potential)
    return own, sent


def turn_kernel(size, *refs):
    far = len(refs) - NEAR
    for f in range(far):
        for c in range(NEAR):
            refs[NEAR + f][pl.ds(c * size, size), :] = refs[c][pl.ds(f * size, size), :]


def turn(size, parts):
    far = parts[0].shape[0] // size
    block = jax.ShapeDtypeStruct((NEAR * size, LANES), jnp.float32)
    return pl.pallas_call(
        functools.partial(turn_kernel, size),
        out_shape=[block] * far,
        in_specs=[pl.BlockSpec(memory_space=pltpu.VMEM)] * NEAR,
        out_specs=[pl.BlockSpec(memory_space=pltpu.VMEM)] * far,
        compiler_params=pltpu.CompilerParams(vmem_limit_bytes=4 * 1024 * 1024),
        name="turn",
    )(*parts)


def bilinear(f00, f01, f10, f11, u, v):
    one = f00 + u * (f01 - f00)
    two = f10 + u * (f11 - f10)
    return one + v * (two - one)


def lerp(one, two, t):
    return one + t * (two - one)


def window(tables, pos_x, pos_y):
    ix = (pos_x + float(SIDE)).astype(jnp.int32)
    iy = (pos_y + float(SIDE)).astype(jnp.int32)
    u = pos_x - (ix.astype(jnp.float32) - float(SIDE))
    v = pos_y - (iy.astype(jnp.float32) - float(SIDE))
    odd = (ix - 1) >> 1
    even = ix >> 1
    columns = (((even & 15), ((even + 1) & 15)), ((odd & 15), ((odd + 1) & 15)))
    odd_first = (ix & 1) == 0
    by_two = ((iy - 1) & 2) != 0
    by_one = (iy & 1) == 0
    sorted_columns = []
    for a in range(4):
        line = ((iy + (2 - a)) & 28) << 2
        e0, e1 = [lane_gather(tables[2 * a], line + c) for c in columns[0]]
        o0, o1 = [lane_gather(tables[2 * a + 1], line + c) for c in columns[1]]
        sorted_columns.append((
            jnp.where(odd_first, o0, e0),
            jnp.where(odd_first, e0, o0),
            jnp.where(odd_first, o1, e1),
            jnp.where(odd_first, e1, o1),
        ))
    w = [[None] * 4 for _ in range(4)]
    for k in range(4):
        half = [jnp.where(by_two, sorted_columns[(r + 2) & 3][k], sorted_columns[r][k]) for r in range(4)]
        for r in range(4):
            w[r][k] = jnp.where(by_one, half[(r + 1) & 3], half[r])
    return w, u, v


def trace_step(tables, strength, pos_x, pos_y, matrix):
    w, u, v = window(tables, pos_x, pos_y)
    gx = [lerp(w[1][k + 1] - w[1][k], w[2][k + 1] - w[2][k], v) for k in range(3)]
    gy = [lerp(w[r + 1][1] - w[r][1], w[r + 1][2] - w[r][2], u) for r in range(3)]
    fx2 = lerp(gx[0] + gx[1], gx[1] + gx[2], u)
    fxx = lerp(gx[1] - gx[0], gx[2] - gx[1], u)
    fy2 = lerp(gy[0] + gy[1], gy[1] + gy[2], v)
    fyy = lerp(gy[1] - gy[0], gy[2] - gy[1], v)
    wide = [[w[r][k + 2] - w[r][k] for k in range(2)] for r in range(4)]
    fxy4 = bilinear(
        wide[2][0] - wide[0][0], wide[2][1] - wide[0][1],
        wide[3][0] - wide[1][0], wide[3][1] - wide[1][1], u, v)
    half = 0.5 * strength
    hxx, hxy, hyy = strength * fxx, (0.25 * strength) * fxy4, strength * fyy
    m11, m12, m21, m22 = matrix
    matrix = (
        m11 - (hxx * m11 + hxy * m21),
        m12 - (hxx * m12 + hxy * m22),
        m21 - (hxy * m11 + hyy * m21),
        m22 - (hxy * m12 + hyy * m22),
    )
    return pos_x - half * fx2, pos_y - half * fy2, matrix


def trace_kernel(n_sky, each, planes, together, me_ref, lens_ref, *refs):
    far = n_sky // NEAR
    size = 4 * each + SUB
    tile_refs, got_refs = refs[:n_sky], refs[n_sky:n_sky + far]
    shift_out, matrix_out, tiles, chosen, rays, places, shift_ref, matrix_ref, sems, out_sems = refs[n_sky + far:]
    me = me_ref[0]
    slots = n_sky * each
    rows = tile_refs[0].shape[0]
    numbers = []
    for s in range(n_sky):
        source = me ^ s
        got_ref, first = got_refs[s // NEAR], s % NEAR * size
        copy = pltpu.make_async_copy(
            got_ref.at[pl.ds(first + 4 * each, SUB), :],
            places.at[pl.ds(source * SUB, SUB), :],
            sems.at[s])
        copy.start()
        numbers.append(copy)
    for s in range(n_sky):
        source = me ^ s
        got_ref, first = got_refs[s // NEAR], s % NEAR * size
        block = pl.ds(pl.multiple_of(source * (4 * each), SUB), 4 * each)
        rays[block, :] = got_ref[pl.ds(first, 4 * each), :]
        tiles[pl.ds(s * rows, rows), :] = tile_refs[s][...]
    for copy in numbers:
        copy.wait()

    def body(step, carry):
        chains = []
        first = pl.multiple_of(step * (together * SUB), together * SUB)
        for plane in range(planes):
            for part in range(together):
                for k in range(SUB):
                    slot = first + (part * SUB + k)
                    spot = places[slot // each * SUB + plane, slot % each].astype(jnp.int32)
                    tile = tiles[pl.ds(pl.multiple_of(spot * CHUNKS, CHUNKS), CHUNKS), :]
                    chosen[pl.ds((plane * together + part) * CHUNKS * SUB + k, CHUNKS, stride=SUB), :] = tile
        for part in range(together):
            base = first + part * SUB
            for h in range(2):
                x0 = rays[pl.ds(base * 4 + 2 * h, SUB, stride=4), :]
                y0 = rays[pl.ds(base * 4 + 2 * h + 1, SUB, stride=4), :]
                one = jnp.ones_like(x0)
                zero = jnp.zeros_like(x0)
                chains.append((part, h, x0, y0, (x0, y0, (one, zero, zero, one))))
        for plane in range(planes):
            strength = lens_ref[plane]
            later = []
            for part, h, x0, y0, state in chains:
                tables = [
                    chosen[pl.ds(((plane * together + part) * CHUNKS + c) * SUB, SUB), :]
                    for c in range(CHUNKS)
                ]
                later.append((part, h, x0, y0, trace_step(tables, strength, *state)))
            chains = later
        for part, h, x0, y0, (x, y, matrix) in chains:
            base = first + part * SUB
            used = x0 > EMPTY * 0.5
            shift_ref[pl.ds(base * 4 + 2 * h, SUB, stride=4), :] = jnp.where(used, x - x0, 0.0)
            shift_ref[pl.ds(base * 4 + 2 * h + 1, SUB, stride=4), :] = jnp.where(used, y - y0, 0.0)
            for e in range(4):
                matrix_ref[pl.ds(base * 8 + 4 * h + e, SUB, stride=8), :] = jnp.where(used, matrix[e], 0.0)
        for copy in results(step):
            copy.start()
        return carry

    def results(step):
        count = together * SUB
        return [
            pltpu.make_async_copy(
                block.at[pl.ds(step * (count * rows_each), count * rows_each), :],
                out.at[pl.ds(step * (count * rows_each), count * rows_each), :],
                out_sems.at[kind, step])
            for kind, (block, out, rows_each) in enumerate(((shift_ref, shift_out, 4), (matrix_ref, matrix_out, 8)))
        ]

    def finish(step, carry):
        for copy in results(step):
            copy.wait()
        return carry

    lax.fori_loop(0, slots // (SUB * together), body, 0)
    lax.fori_loop(0, slots // (SUB * together), finish, 0)


def trace(each, planes, me, lens_weight, tiles, got):
    n_sky = len(tiles)
    slots = n_sky * each
    rows = tiles[0].shape[0]
    together = 4
    return pl.pallas_call(
        functools.partial(trace_kernel, n_sky, each, planes, together),
        out_shape=(
            jax.ShapeDtypeStruct((slots * 4, LANES), jnp.float32),
            jax.ShapeDtypeStruct((slots * 8, LANES), jnp.float32),
        ),
        in_specs=[pl.BlockSpec(memory_space=pltpu.SMEM)] * 2 + [pl.BlockSpec(memory_space=pltpu.VMEM)] * (n_sky + len(got)),
        out_specs=(
            pl.BlockSpec(memory_space=pl.ANY),
            pl.BlockSpec(memory_space=pl.ANY),
        ),
        scratch_shapes=[
            pltpu.VMEM((n_sky * rows, LANES), jnp.float32),
            pltpu.VMEM((planes * together * CHUNKS * SUB, LANES), jnp.float32),
            pltpu.VMEM((slots * 4, LANES), jnp.float32),
            pltpu.SMEM((n_sky * SUB, LANES), jnp.float32),
            pltpu.VMEM((slots * 4, LANES), jnp.float32),
            pltpu.VMEM((slots * 8, LANES), jnp.float32),
            pltpu.SemaphoreType.DMA((n_sky,)),
            pltpu.SemaphoreType.DMA((2, slots // (SUB * 4))),
        ],
        compiler_params=pltpu.CompilerParams(vmem_limit_bytes=20 * 1024 * 1024),
        name="trace",
    )(me, lens_weight, *tiles, *got)


def flipped(value, n_sky, bits):
    return lax.ppermute(value, "sky", [(i, i ^ bits) for i in range(n_sky)])


def spread(held, n_sky, bits):
    for bit in bits:
        for s in [s for s in held if s & (2 * bit - 1) == 0]:
            if s ^ bit not in held:
                held[s ^ bit] = flipped(held[s], n_sky, bit)


def shards(potential, lens_weight, ray_start, patch_index, destination):
    n_sky = lax.axis_size("sky")
    me = lax.axis_index("sky").reshape(1)
    planes = potential.shape[0]
    bundles, _, rays = ray_start.shape
    each = max(2, 2 * bundles // n_sky)
    slots = n_sky * each
    halves = rays // LANES
    bits = [1 << k for k in reversed(range((n_sky - 1).bit_length()))]
    flat = ray_start.reshape(bundles, 2, halves, LANES).transpose(0, 2, 1, 3).reshape(bundles * 2 * halves, LANES)
    own, sent = prepare(n_sky, each, me, destination.reshape(1, bundles), patch_index, flat, potential)
    sent = [sent[0]] + [flipped(sent[s], n_sky, s) for s in range(1, NEAR)]
    held = {0: own}
    for bit in bits[:2]:
        held[bit] = flipped(own, n_sky, bit)
    held[bits[0] ^ bits[1]] = flipped(held[bits[0]], n_sky, bits[1])
    got = turn(4 * each + SUB, sent)
    early = [0, bits[0]]
    *got, a, b = lax.optimization_barrier((*got, *[held[s] for s in early]))
    held.update(zip(early, (a, b)))
    got = [got[0]] + [flipped(got[f], n_sky, f * NEAR) for f in range(1, len(got))]
    spread(held, n_sky, bits[:-1])
    half = len(got) // 2
    for mid, low in ((half, 0), (half + 1, n_sky // 2)):
        some = range(low, low + n_sky // 2, 2)
        got[mid], *evens = lax.optimization_barrier((got[mid], *[held[s] for s in some]))
        held.update(zip(some, evens))
    spread(held, n_sky, bits)
    shift, matrix = trace(each, planes, me, lens_weight, [held[s] for s in range(n_sky)], got)
    shift = shift.reshape(slots, halves, 2, LANES).transpose(0, 2, 1, 3).reshape(slots, 2, rays)
    matrix = matrix.reshape(slots, halves, 4, LANES).transpose(0, 2, 1, 3).reshape(slots, 4, rays)
    return shift, matrix


def solution(mesh):
    in_specs = (
        P("groups", "sky", None),
        P(),
        P(("groups", "sky"), None, None),
        P("groups", "sky"),
        P(("groups", "sky"), None),
    )
    out_specs = (P(("groups", "sky"), None, None), P(("groups", "sky"), None, None))
    return jax.shard_map(shards, mesh=mesh, in_specs=in_specs, out_specs=out_specs, check_vma=False)
```

```python
import functools

import jax
import jax.numpy as jnp
from jax import lax
from jax.experimental import pallas as pl
from jax.experimental.pallas import tpu as pltpu
from jax.sharding import PartitionSpec as P

LANES = 128
SUB = 8
SIDE = 32
CHUNKS = 8
EMPTY = -1024.0
NEAR = 4


def lane_gather(table, idx):
    dims = lax.GatherDimensionNumbers(
        offset_dims=(),
        collapsed_slice_dims=(1,),
        start_index_map=(1,),
        operand_batching_dims=(0,),
        start_indices_batching_dims=(0,),
    )
    return lax.gather(
        table,
        idx[..., None],
        dims,
        slice_sizes=(1, 1),
        mode=lax.GatherScatterMode.PROMISE_IN_BOUNDS,
    )


def split3(value):
    high = value.astype(jnp.bfloat16)
    rest = value - high.astype(jnp.float32)
    middle = rest.astype(jnp.bfloat16)
    low = (rest - middle.astype(jnp.float32)).astype(jnp.bfloat16)
    return high, middle, low


def regroup_kernel(src_ref, dst_ref):
    planes, tiles, _ = src_ref.shape
    lane = lax.broadcasted_iota(jnp.int32, (SUB, LANES), 1)
    source = (lane & 96) + ((lane & 15) << 1) + ((lane >> 4) & 1)
    for plane in range(planes):
        for base in range(0, tiles, SUB):
            parts = [
                lane_gather(src_ref[plane, pl.ds(base, SUB), pl.ds(c * LANES, LANES)], source)
                for c in range(CHUNKS)
            ]
            for step in (1, 2, 4):
                keep = ((lane >> 4) & step) == 0
                for c in range(CHUNKS):
                    if c & step:
                        continue
                    one, two = parts[c], parts[c + step]
                    parts[c] = jnp.where(keep, one, pltpu.roll(two, step * 16, 1))
                    parts[c + step] = jnp.where(keep, pltpu.roll(one, LANES - step * 16, 1), two)
            for c in range(CHUNKS):
                rows = pl.ds((plane * tiles + base) * CHUNKS + c, SUB, stride=CHUNKS)
                dst_ref[rows, :] = parts[c]


def pack_kernel(n_sky, each, per_owner, me_ref, dest_ref, ids_ref, rays_ref, *out_refs):
    me = me_ref[0]
    bundles = dest_ref.shape[1]
    planes = ids_ref.shape[0]
    slots = n_sky * each
    size = 4 * each + SUB
    dest_row = jnp.broadcast_to(dest_ref[...], (bundles, bundles))
    dest_col = jnp.transpose(dest_row)
    row = lax.broadcasted_iota(jnp.int32, (bundles, bundles), 0)
    col = lax.broadcasted_iota(jnp.int32, (bundles, bundles), 1)
    hits = jnp.where((dest_row == dest_col) & (row < col), 1.0, 0.0)
    rank = jnp.sum(hits, axis=0, keepdims=True).astype(jnp.int32)
    slot = (dest_ref[...] ^ me) * each + rank
    place = lax.broadcasted_iota(jnp.int32, (slots, bundles), 0) == slot
    place = jnp.where(place, 1.0, 0.0)
    found = jnp.dot(
        place.astype(jnp.bfloat16),
        jnp.ones((bundles, LANES), jnp.bfloat16),
        preferred_element_type=jnp.float32,
    )
    place3 = jnp.concatenate([place] * 3, axis=1).astype(jnp.bfloat16)
    for part in range(4):
        rays = rays_ref[pl.ds(part, bundles, stride=4), :]
        terms = jnp.concatenate(split3(rays), axis=0)
        sent = jnp.dot(place3, terms, preferred_element_type=jnp.float32)
        if part % 2 == 0:
            sent = jnp.where(found > 0.5, sent, EMPTY)
        for s in range(n_sky):
            rows = pl.ds(s // NEAR * size + part, each, stride=4)
            out_refs[s % NEAR][rows, :] = sent[s * each:(s + 1) * each]
    ids = ids_ref[...]
    plane = lax.broadcasted_iota(jnp.int32, ids.shape, 0)
    owner = (ids // per_owner) ^ dest_ref[...]
    spot = (owner * planes + plane) * per_owner + ids % per_owner
    pad = jnp.zeros((SUB - planes, bundles), jnp.float32)
    fine = jnp.concatenate([(spot & 15).astype(jnp.float32), pad], axis=0)
    coarse = jnp.concatenate([(spot >> 4).astype(jnp.float32), pad], axis=0)
    place = place.astype(jnp.bfloat16)
    contract = (((1,), (1,)), ((), ()))
    fine = lax.dot_general(fine.astype(jnp.bfloat16), place, contract, preferred_element_type=jnp.float32)
    coarse = lax.dot_general(coarse.astype(jnp.bfloat16), place, contract, preferred_element_type=jnp.float32)
    numbers = coarse * 16.0 + fine
    for s in range(n_sky):
        first = s * each
        block = numbers[:, first // LANES * LANES:first // LANES * LANES + LANES]
        turn = (LANES - first % LANES) % LANES
        if turn:
            block = pltpu.roll(block, turn, 1)
        out_refs[s % NEAR][pl.ds(s // NEAR * size + 4 * each, SUB), :] = block


def prepare_kernel(n_sky, each, me_ref, dest_ref, ids_ref, rays_ref, src_ref, dst_ref, *out_refs):
    regroup_kernel(src_ref, dst_ref)
    pack_kernel(n_sky, each, src_ref.shape[1], me_ref, dest_ref, ids_ref, rays_ref, *out_refs)


def prepare(n_sky, each, me, dest, ids, rays, potential):
    planes, tiles, pixels = potential.shape
    part = jax.ShapeDtypeStruct((n_sky // NEAR * (4 * each + SUB), LANES), jnp.float32)
    own = jax.ShapeDtypeStruct((planes * tiles * pixels // LANES, LANES), jnp.float32)
    own, *sent = pl.pallas_call(
        functools.partial(prepare_kernel, n_sky, each),
        out_shape=[own] + [part] * NEAR,
        in_specs=[pl.BlockSpec(memory_space=pltpu.SMEM)] + [pl.BlockSpec(memory_space=pltpu.VMEM)] * 4,
        out_specs=[pl.BlockSpec(memory_space=pltpu.VMEM)] * (1 + NEAR),
        compiler_params=pltpu.CompilerParams(vmem_limit_bytes=16 * 1024 * 1024),
        name="prepare",
    )(me, dest, ids, rays, potential)
    return own, sent


def turn_kernel(size, *refs):
    far = len(refs) - NEAR
    for f in range(far):
        for c in range(NEAR):
            refs[NEAR + f][pl.ds(c * size, size), :] = refs[c][pl.ds(f * size, size), :]


def turn(size, parts):
    far = parts[0].shape[0] // size
    block = jax.ShapeDtypeStruct((NEAR * size, LANES), jnp.float32)
    return pl.pallas_call(
        functools.partial(turn_kernel, size),
        out_shape=[block] * far,
        in_specs=[pl.BlockSpec(memory_space=pltpu.VMEM)] * NEAR,
        out_specs=[pl.BlockSpec(memory_space=pltpu.VMEM)] * far,
        compiler_params=pltpu.CompilerParams(vmem_limit_bytes=4 * 1024 * 1024),
        name="turn",
    )(*parts)


def bilinear(f00, f01, f10, f11, u, v):
    one = f00 + u * (f01 - f00)
    two = f10 + u * (f11 - f10)
    return one + v * (two - one)


def lerp(one, two, t):
    return one + t * (two - one)


def window(tables, pos_x, pos_y):
    ix = (pos_x + float(SIDE)).astype(jnp.int32)
    iy = (pos_y + float(SIDE)).astype(jnp.int32)
    u = pos_x - (ix.astype(jnp.float32) - float(SIDE))
    v = pos_y - (iy.astype(jnp.float32) - float(SIDE))
    odd = (ix - 1) >> 1
    even = ix >> 1
    columns = (((even & 15), ((even + 1) & 15)), ((odd & 15), ((odd + 1) & 15)))
    odd_first = (ix & 1) == 0
    by_two = ((iy - 1) & 2) != 0
    by_one = (iy & 1) == 0
    sorted_columns = []
    for a in range(4):
        line = ((iy + (2 - a)) & 28) << 2
        e0, e1 = [lane_gather(tables[2 * a], line + c) for c in columns[0]]
        o0, o1 = [lane_gather(tables[2 * a + 1], line + c) for c in columns[1]]
        sorted_columns.append((
            jnp.where(odd_first, o0, e0),
            jnp.where(odd_first, e0, o0),
            jnp.where(odd_first, o1, e1),
            jnp.where(odd_first, e1, o1),
        ))
    w = [[None] * 4 for _ in range(4)]
    for k in range(4):
        half = [jnp.where(by_two, sorted_columns[(r + 2) & 3][k], sorted_columns[r][k]) for r in range(4)]
        for r in range(4):
            w[r][k] = jnp.where(by_one, half[(r + 1) & 3], half[r])
    return w, u, v


def trace_step(tables, strength, pos_x, pos_y, matrix):
    w, u, v = window(tables, pos_x, pos_y)
    gx = [lerp(w[1][k + 1] - w[1][k], w[2][k + 1] - w[2][k], v) for k in range(3)]
    gy = [lerp(w[r + 1][1] - w[r][1], w[r + 1][2] - w[r][2], u) for r in range(3)]
    fx2 = lerp(gx[0] + gx[1], gx[1] + gx[2], u)
    fxx = lerp(gx[1] - gx[0], gx[2] - gx[1], u)
    fy2 = lerp(gy[0] + gy[1], gy[1] + gy[2], v)
    fyy = lerp(gy[1] - gy[0], gy[2] - gy[1], v)
    wide = [[w[r][k + 2] - w[r][k] for k in range(2)] for r in range(4)]
    fxy4 = bilinear(
        wide[2][0] - wide[0][0], wide[2][1] - wide[0][1],
        wide[3][0] - wide[1][0], wide[3][1] - wide[1][1], u, v)
    half = 0.5 * strength
    hxx, hxy, hyy = strength * fxx, (0.25 * strength) * fxy4, strength * fyy
    m11, m12, m21, m22 = matrix
    matrix = (
        m11 - (hxx * m11 + hxy * m21),
        m12 - (hxx * m12 + hxy * m22),
        m21 - (hxy * m11 + hyy * m21),
        m22 - (hxy * m12 + hyy * m22),
    )
    return pos_x - half * fx2, pos_y - half * fy2, matrix


def trace_kernel(n_sky, each, planes, together, me_ref, lens_ref, *refs):
    far = n_sky // NEAR
    size = 4 * each + SUB
    tile_refs, got_refs = refs[:n_sky], refs[n_sky:n_sky + far]
    shift_out, matrix_out, tiles, chosen, rays, places, shift_ref, matrix_ref, sems, out_sems = refs[n_sky + far:]
    me = me_ref[0]
    slots = n_sky * each
    rows = tile_refs[0].shape[0]
    numbers = []
    for s in range(n_sky):
        source = me ^ s
        got_ref, first = got_refs[s // NEAR], s % NEAR * size
        copy = pltpu.make_async_copy(
            got_ref.at[pl.ds(first + 4 * each, SUB), :],
            places.at[pl.ds(source * SUB, SUB), :],
            sems.at[s])
        copy.start()
        numbers.append(copy)
    for s in range(n_sky):
        source = me ^ s
        got_ref, first = got_refs[s // NEAR], s % NEAR * size
        block = pl.ds(pl.multiple_of(source * (4 * each), SUB), 4 * each)
        rays[block, :] = got_ref[pl.ds(first, 4 * each), :]
        tiles[pl.ds(s * rows, rows), :] = tile_refs[s][...]
    for copy in numbers:
        copy.wait()

    def body(step, carry):
        chains = []
        first = pl.multiple_of(step * (together * SUB), together * SUB)
        for plane in range(planes):
            for part in range(together):
                for k in range(SUB):
                    slot = first + (part * SUB + k)
                    spot = places[slot // each * SUB + plane, slot % each].astype(jnp.int32)
                    tile = tiles[pl.ds(pl.multiple_of(spot * CHUNKS, CHUNKS), CHUNKS), :]
                    chosen[pl.ds((plane * together + part) * CHUNKS * SUB + k, CHUNKS, stride=SUB), :] = tile
        for part in range(together):
            base = first + part * SUB
            for h in range(2):
                x0 = rays[pl.ds(base * 4 + 2 * h, SUB, stride=4), :]
                y0 = rays[pl.ds(base * 4 + 2 * h + 1, SUB, stride=4), :]
                one = jnp.ones_like(x0)
                zero = jnp.zeros_like(x0)
                chains.append((part, h, x0, y0, (x0, y0, (one, zero, zero, one))))
        for plane in range(planes):
            strength = lens_ref[plane]
            later = []
            for part, h, x0, y0, state in chains:
                tables = [
                    chosen[pl.ds(((plane * together + part) * CHUNKS + c) * SUB, SUB), :]
                    for c in range(CHUNKS)
                ]
                later.append((part, h, x0, y0, trace_step(tables, strength, *state)))
            chains = later
        for part, h, x0, y0, (x, y, matrix) in chains:
            base = first + part * SUB
            used = x0 > EMPTY * 0.5
            shift_ref[pl.ds(base * 4 + 2 * h, SUB, stride=4), :] = jnp.where(used, x - x0, 0.0)
            shift_ref[pl.ds(base * 4 + 2 * h + 1, SUB, stride=4), :] = jnp.where(used, y - y0, 0.0)
            for e in range(4):
                matrix_ref[pl.ds(base * 8 + 4 * h + e, SUB, stride=8), :] = jnp.where(used, matrix[e], 0.0)
        for copy in results(step):
            copy.start()
        return carry

    def results(step):
        count = together * SUB
        return [
            pltpu.make_async_copy(
                block.at[pl.ds(step * (count * rows_each), count * rows_each), :],
                out.at[pl.ds(step * (count * rows_each), count * rows_each), :],
                out_sems.at[kind, step])
            for kind, (block, out, rows_each) in enumerate(((shift_ref, shift_out, 4), (matrix_ref, matrix_out, 8)))
        ]

    def finish(step, carry):
        for copy in results(step):
            copy.wait()
        return carry

    lax.fori_loop(0, slots // (SUB * together), body, 0)
    lax.fori_loop(0, slots // (SUB * together), finish, 0)


def trace(each, planes, me, lens_weight, tiles, got):
    n_sky = len(tiles)
    slots = n_sky * each
    rows = tiles[0].shape[0]
    together = 4
    return pl.pallas_call(
        functools.partial(trace_kernel, n_sky, each, planes, together),
        out_shape=(
            jax.ShapeDtypeStruct((slots * 4, LANES), jnp.float32),
            jax.ShapeDtypeStruct((slots * 8, LANES), jnp.float32),
        ),
        in_specs=[pl.BlockSpec(memory_space=pltpu.SMEM)] * 2 + [pl.BlockSpec(memory_space=pltpu.VMEM)] * (n_sky + len(got)),
        out_specs=(
            pl.BlockSpec(memory_space=pl.ANY),
            pl.BlockSpec(memory_space=pl.ANY),
        ),
        scratch_shapes=[
            pltpu.VMEM((n_sky * rows, LANES), jnp.float32),
            pltpu.VMEM((planes * together * CHUNKS * SUB, LANES), jnp.float32),
            pltpu.VMEM((slots * 4, LANES), jnp.float32),
            pltpu.SMEM((n_sky * SUB, LANES), jnp.float32),
            pltpu.VMEM((slots * 4, LANES), jnp.float32),
            pltpu.VMEM((slots * 8, LANES), jnp.float32),
            pltpu.SemaphoreType.DMA((n_sky,)),
            pltpu.SemaphoreType.DMA((2, slots // (SUB * 4))),
        ],
        compiler_params=pltpu.CompilerParams(vmem_limit_bytes=20 * 1024 * 1024),
        name="trace",
    )(me, lens_weight, *tiles, *got)


def flipped(value, n_sky, bits):
    return lax.ppermute(value, "sky", [(i, i ^ bits) for i in range(n_sky)])


def spread(held, n_sky, bits):
    for bit in bits:
        for s in [s for s in held if s & (2 * bit - 1) == 0]:
            if s ^ bit not in held:
                held[s ^ bit] = flipped(held[s], n_sky, bit)


def shards(potential, lens_weight, ray_start, patch_index, destination):
    n_sky = lax.axis_size("sky")
    me = lax.axis_index("sky").reshape(1)
    planes = potential.shape[0]
    bundles, _, rays = ray_start.shape
    each = max(2, 2 * bundles // n_sky)
    slots = n_sky * each
    halves = rays // LANES
    bits = [1 << k for k in reversed(range((n_sky - 1).bit_length()))]
    flat = ray_start.reshape(bundles, 2, halves, LANES).transpose(0, 2, 1, 3).reshape(bundles * 2 * halves, LANES)
    own, sent = prepare(n_sky, each, me, destination.reshape(1, bundles), patch_index, flat, potential)
    sent = [sent[0]] + [flipped(sent[s], n_sky, s) for s in range(1, NEAR)]
    held = {0: own}
    for bit in bits[:2]:
        held[bit] = flipped(own, n_sky, bit)
    held[bits[0] ^ bits[1]] = flipped(held[bits[0]], n_sky, bits[1])
    got = turn(4 * each + SUB, sent)
    early = [0]
    *got, a = lax.optimization_barrier((*got, *[held[s] for s in early]))
    held.update(zip(early, (a,)))
    got = [got[0]] + [flipped(got[f], n_sky, f * NEAR) for f in range(1, len(got))]
    spread(held, n_sky, bits[:-1])
    half = len(got) // 2
    for mid, low in ((half, 0), (half + 1, n_sky // 2)):
        some = range(low, low + n_sky // 2, 2)
        got[mid], *evens = lax.optimization_barrier((got[mid], *[held[s] for s in some]))
        held.update(zip(some, evens))
    spread(held, n_sky, bits)
    shift, matrix = trace(each, planes, me, lens_weight, [held[s] for s in range(n_sky)], got)
    shift = shift.reshape(slots, halves, 2, LANES).transpose(0, 2, 1, 3).reshape(slots, 2, rays)
    matrix = matrix.reshape(slots, halves, 4, LANES).transpose(0, 2, 1, 3).reshape(slots, 4, rays)
    return shift, matrix


def solution(mesh):
    in_specs = (
        P("groups", "sky", None),
        P(),
        P(("groups", "sky"), None, None),
        P("groups", "sky"),
        P(("groups", "sky"), None),
    )
    out_specs = (P(("groups", "sky"), None, None), P(("groups", "sky"), None, None))
    return jax.shard_map(shards, mesh=mesh, in_specs=in_specs, out_specs=out_specs, check_vma=False)
```
